32 devices in a mesh: grp: 8 (over z, y), dp: 4 (over x, core).
Axes of the slice: x: 2, y: 2, z: 4, core: 2. Of those that a mesh axis runs over, the one named last changes fastest.
Arguments:
- tokens: bfloat16 [32, 256, 768], P(('grp', 'dp')), may hold values from -6 to 6
- condition: bfloat16 [32, 768], P(('grp', 'dp')), may hold values from -6 to 6
- bucket: int32 [32], P(('grp', 'dp')), may hold values from 0 to 63, as said below
- live_mask: int32 [32], P(('grp', 'dp')), may hold values from 0 to 1, as said below
- routes: int32 [32, 256, 2], P(('grp', 'dp')), may hold values from 0 to 3, all different within a row; in each aligned block of 256 rows (0 to 255, 256 to 511, ..., all dimensions but the last counted through in order) at most 256 rows name the same one
- bucket_table: bfloat16 [64, 768], replicated, may hold values from -6 to 6
- ada_weight: bfloat16 [768, 4608], replicated, may hold values from -0.21875 to 0.21875
- ada_bias: bfloat16 [4608], replicated, may hold values from -3 to 3
- qkv_weight: bfloat16 [768, 2304], replicated, may hold values from -0.21875 to 0.21875
- proj_weight: bfloat16 [768, 768], replicated, may hold values from -0.875 to 0.875
- shared_up: bfloat16 [768, 3072], replicated, may hold values from -0.21875 to 0.21875
- shared_down: bfloat16 [3072, 768], replicated, may hold values from -0.109375 to 0.109375
- router_weight: bfloat16 [768, 4], replicated, may hold values from -0.21875 to 0.21875
- expert_up: bfloat16 [4, 768, 3072], P('dp'), may hold values from -0.21875 to 0.21875
- expert_down: bfloat16 [4, 3072, 768], P('dp'), may hold values from -0.109375 to 0.109375
- cotangent: bfloat16 [32, 256, 768], P(('grp', 'dp')), may hold values from -6 to 6
Outputs:
- mixed_out: bfloat16 [32, 256, 768], P(('grp', 'dp'))
- grad_tokens: float32 [32, 256, 768], P(('grp', 'dp'))
- grad_condition: float32 [32, 768], P(('grp', 'dp'))
- grad_table: float32 [64, 768], P('grp')
- grad_ada_weight: float32 [768, 4608], P('grp')
- grad_ada_bias: float32 [4608], P('grp')
- grad_qkv: float32 [768, 2304], P('grp')
- grad_proj: float32 [768, 768], P('grp')
- grad_shared_up: float32 [768, 3072], P('grp')
- grad_shared_down: float32 [3072, 768], P('grp')
- grad_router: float32 [768, 4], P('grp')
- grad_expert_up: float32 [4, 768, 3072], P('dp', 'grp')
- grad_expert_down: float32 [4, 3072, 768], P('dp', 'grp')
The draws below stay inside these ranges and needn't reach their ends.
Inputs may be any that keep to these rules, and one draw needn't show every extreme that they name: `routes`: in the rows of one device (256 patches in order) each patch names 2 different experts, no expert is named by more than 256 of them. An image of group g (slots g * 4 to g * 4 + 3) has a bucket from g * 8 to g * 8 + 7; lower buckets of a group are more common. `live_mask`: in each group of 4 slots the live images come first; every group holds one or more, the first group is full, and no group holds more than the one before it.
All inputs are finite; a program needn't handle non-finite values.
Results may differ from the reference program's by a relative error of at most 0.024.
Values may be sent and summed in bfloat16 or wider, within the bound.
No kernel may reach another device: no remote copies, remote signals or barrier semaphores. Data moves between devices by JAX's collectives and lax.ppermute only.
A program may use at most 192 MiB of HBM per device.

```python
import math
import jax
import jax.numpy as jnp
import numpy as np
from jax import lax

D = 768
HEADS = 12
FF = 3072
PATCHES = 256
TOP = 2
EXPERTS = 4
BUCK_GRP = 8
TOK_DEV = 256
SLOTS = 4
IMAGES = 32
BUCKETS = 64
CAP = 256
DEVICES = 32


def draw_live_mask(key, part):
    key = jax.random.fold_in(key, 11)
    group_total = IMAGES // SLOTS
    counts = jax.random.randint(key, (group_total,), 1, SLOTS + 1).astype(jnp.int32)
    counts = -jnp.sort(-counts.at[0].set(SLOTS))
    slot_number = jnp.arange(IMAGES, dtype=jnp.int32) % SLOTS
    group_number = jnp.arange(IMAGES, dtype=jnp.int32) // SLOTS
    return (slot_number < counts[group_number]).astype(jnp.int32)


def draw_bucket(key, part):
    key = jax.random.fold_in(key, 23)
    first_key = jax.random.fold_in(key, 1)
    second_key = jax.random.fold_in(key, 2)
    group_number = jnp.arange(IMAGES, dtype=jnp.int32) // SLOTS
    first_pick = jax.random.randint(first_key, (IMAGES,), 0, BUCK_GRP).astype(jnp.int32)
    second_pick = jax.random.randint(second_key, (IMAGES,), 0, BUCK_GRP).astype(jnp.int32)
    offsets = jnp.minimum(first_pick, second_pick).astype(jnp.int32)
    buckets = group_number * BUCK_GRP + offsets
    return buckets.at[0].set(0).at[IMAGES - 1].set(BUCKETS - 1).astype(jnp.int32)


def level_of(stream_key, dims, cuts, smallest, high):
    def one(position, parts):
        draws = jax.random.uniform(jax.random.fold_in(jax.random.fold_in(stream_key, 6), position), (parts,), jnp.float32, smallest / len(cuts), high / len(cuts))
        return jnp.repeat(jnp.exp(draws), dims[position] // parts).reshape((-1,) + (1,) * (len(dims) - position - 1))

    loudness = one(*cuts[0])
    for cut in cuts[1:]:
        loudness = loudness * one(*cut)
    return loudness


def deal_out(stream_key, own, number, rows, count, top, bound, slope):
    sequence = jax.random.permutation(stream_key, count)
    heavy_load, common = portions_of(count, rows * top, bound, slope, True), portions_of(count, rows * top, bound, slope, False)
    places = jnp.arange(count)

    def named(lengths, turn):
        used = int((lengths > 0).sum())
        fixed = max(1, used // 4)
        passed = fixed + (places - fixed + turn * (used - fixed)) % max(1, count - fixed)
        return jnp.zeros((count,), jnp.int32).at[sequence[jnp.where(places < fixed, places, passed)]].set(jnp.asarray(lengths, jnp.int32))

    lengths = jnp.where(number % 4 == 0, named(heavy_load, number // 4), named(common, number - number // 4 - 1))
    mixed = jax.random.permutation(jax.random.fold_in(own, 3), count)
    giver, sink = mixed[0:count // 2 * 2:2], mixed[1:count // 2 * 2:2]
    slack = jnp.minimum(lengths[giver] - 1, bound - lengths[sink]) // 2
    slack = jnp.where((giver == sequence[0]) | (sink == sequence[0]) | (lengths[sink] == 0), 0, jnp.maximum(slack, 0))
    passed = jax.random.randint(jax.random.fold_in(own, 4), (count // 2,), 0, 1 << 20) % (slack + 1)
    lengths = lengths.at[giver].add(-passed).at[sink].add(passed)
    labels = jnp.searchsorted(jnp.cumsum(lengths), jnp.arange(rows * top), side="right").astype(jnp.int32)
    listing = labels.reshape(top, rows).T
    listing = listing[jax.random.permutation(jax.random.fold_in(own, 1), rows)]
    turn = jax.random.randint(jax.random.fold_in(own, 2), (rows, 1), 0, top)
    return jnp.take_along_axis(listing, (jnp.arange(top)[None, :] + turn) % top, axis=1)


def portions_of(amount, total, most, slope, full):
    weights = [(1 << 20) // math.isqrt(rank ** slope) + 1 for rank in range(1, amount + 1)]
    largest = most if full else min(most, max(-(-total // amount), total * weights[0] // sum(weights)))
    least = 1 if total - largest >= amount - 1 else 0
    given, surplus = [largest] + [least] * (amount - 1), total - largest - least * (amount - 1)
    while surplus > 0:
        movable = [i for i in range(1, amount) if given[i] < largest] or [i for i in range(1, amount) if given[i] < most]
        mass, remaining = sum([weights[i] for i in movable]), surplus
        for i in movable:
            extra = min(most - given[i], max(1, remaining * weights[i] // mass), surplus)
            given[i] = given[i] + extra
            surplus = surplus - extra
    return np.array(given)


def bell_draw(rng, shape, spread, bound, cuts=(), kind=jnp.bfloat16):
    entries = spread * jax.random.normal(rng, shape, jnp.float32)
    if cuts:
        entries = entries * level_of(rng, shape, cuts, -0.22, 0.18)
    return jnp.clip(entries, -bound, bound).astype(kind)


def setup_inputs(seed: int = 0) -> dict:
    splits = jax.random.split(jax.random.key(seed), 17)
    tokens = bell_draw(splits[0], (IMAGES, PATCHES, D), 1.0, 6.0, ((0, 32),))
    condition = bell_draw(splits[1], (IMAGES, D), 1.0, 6.0, ((0, 32),))
    bucket = draw_bucket(jax.random.fold_in(splits[16], 71), 0)
    live_mask = draw_live_mask(jax.random.fold_in(splits[16], 71), 0)
    routes_keys = jax.random.split(jax.random.fold_in(splits[4], 1), IMAGES * PATCHES // TOK_DEV)
    routes_turns = jax.random.permutation(jax.random.fold_in(splits[4], 3), IMAGES * PATCHES // TOK_DEV)
    routes = jax.vmap(lambda own, number: deal_out(jax.random.fold_in(splits[4], 2), own, number, TOK_DEV, EXPERTS, TOP, CAP, 1))(routes_keys, routes_turns).reshape((IMAGES, PATCHES, TOP))
    bucket_table = bell_draw(splits[5], (BUCKETS, D), 1.0, 6.0)
    ada_weight = bell_draw(splits[6], (D, 6 * D), D ** -0.5, 0.21875)
    ada_bias = bell_draw(splits[7], (6 * D,), 0.5, 3.0)
    qkv_weight = bell_draw(splits[8], (D, 3 * D), D ** -0.5, 0.21875)
    proj_weight = bell_draw(splits[9], (D, D), (D // 16) ** -0.5, 0.875)
    shared_up = bell_draw(splits[10], (D, FF), D ** -0.5, 0.21875)
    shared_down = bell_draw(splits[11], (FF, D), FF ** -0.5, 0.109375)
    router_weight = bell_draw(splits[12], (D, EXPERTS), D ** -0.5, 0.21875)
    expert_up = bell_draw(splits[13], (EXPERTS, D, FF), D ** -0.5, 0.21875, ((0, 4),))
    expert_down = bell_draw(splits[14], (EXPERTS, FF, D), FF ** -0.5, 0.109375, ((0, 4),))
    cotangent = bell_draw(splits[15], (IMAGES, PATCHES, D), 1.0, 6.0, ((0, 32),))
    return dict(tokens=tokens, condition=condition, bucket=bucket, live_mask=live_mask, routes=routes, bucket_table=bucket_table, ada_weight=ada_weight, ada_bias=ada_bias, qkv_weight=qkv_weight, proj_weight=proj_weight, shared_up=shared_up, shared_down=shared_down, router_weight=router_weight, expert_up=expert_up, expert_down=expert_down, cotangent=cotangent)


HIGHEST_PRECISION = lax.Precision.HIGHEST

@jax.custom_vjp
def low(v):
    return lax.optimization_barrier(v.astype(jnp.bfloat16)).astype(jnp.float32)

@jax.custom_vjp
def low_back(v):
    return v

def low_keep(v):
    return (low(v), None)

def low_pass(kept, grad):
    return (grad,)

def back_keep(v):
    return (v, None)

def back_low(kept, grad):
    return (low(grad),)
low.defvjp(low_keep, low_pass)
low_back.defvjp(back_keep, back_low)

def dot_high(left_mat, right_mat):
    return jnp.dot(left_mat, right_mat, precision=HIGHEST_PRECISION)

def normalize(tensor):
    average = lax.optimization_barrier(jnp.mean(tensor, axis=-1, keepdims=True))
    centered = tensor - average
    return centered * lax.rsqrt(lax.optimization_barrier(jnp.mean(centered * centered, axis=-1, keepdims=True)) + 1e-06)

def fill_slots(slot_row, owners):
    return jnp.full((EXPERTS * CAP,), TOK_DEV, jnp.int32).at[slot_row].set(owners)

def reference(tokens, condition, bucket, live_mask, routes, bucket_table, ada_weight, ada_bias, qkv_weight, proj_weight, shared_up, shared_down, router_weight, expert_up, expert_down, cotangent):
    head_size = D // HEADS
    scaling = float(head_size) ** (-0.5)
    block_images = math.gcd(IMAGES, max(1, 4096 // PATCHES))
    block_count = IMAGES // block_images
    flat_routes = routes.reshape(DEVICES, TOK_DEV * TOP).astype(jnp.int32)
    route_hot = (flat_routes[:, :, None] == jnp.arange(EXPERTS, dtype=jnp.int32)[None, None, :]).astype(jnp.int32)
    places = lax.optimization_barrier(jnp.sum(route_hot * (jnp.cumsum(route_hot, axis=1).astype(jnp.int32) - 1), axis=2)).astype(jnp.int32)
    slot_index = (flat_routes * CAP + places).astype(jnp.int32)
    owners = (jnp.arange(TOK_DEV * TOP, dtype=jnp.int32) // TOP).astype(jnp.int32)
    slot_owner = jax.vmap(fill_slots, in_axes=(0, None))(slot_index, owners)
    device_ids = jnp.arange(DEVICES, dtype=jnp.int32)[:, None]
    selector = (bucket[:, None] == jnp.arange(BUCKETS, dtype=jnp.int32)[None, :]).astype(jnp.float32)
    chosen_hot = (routes.reshape(IMAGES * PATCHES, TOP)[:, :, None] == jnp.arange(EXPERTS, dtype=jnp.int32)[None, None, :]).astype(jnp.float32)
    alive_rows = live_mask.astype(jnp.float32)[:, None, None]

    def forward(inputs, cond_vals, table_vals, ada_mat, ada_vec, qkv_mat, proj_mat, up_mat, down_mat, router_mat, expert_ups, expert_downs):
        conditioned = cond_vals + dot_high(selector, table_vals)
        activated = low(jax.nn.silu(conditioned))
        modulation = low_back(dot_high(activated, ada_mat)) + ada_vec
        shift_attn, scale_attn, gate_attn, shift_mix, scale_mix, gate_mix = jnp.split(modulation, 6, axis=1)

        def attend(block):
            block_in, shift_blk, scale_blk, gate_blk = block
            attn_in = low(normalize(block_in) * (1.0 + scale_blk[:, None, :]) + shift_blk[:, None, :])
            projected = low(low_back(jnp.einsum('bpd,de->bpe', attn_in, qkv_mat, precision=HIGHEST_PRECISION)))
            projected = projected.reshape(block_images, PATCHES, 3, HEADS, head_size)
            query_rows = projected[:, :, 0]
            key_rows = projected[:, :, 1]
            value_rows = projected[:, :, 2]
            scores = low_back(jnp.einsum('bqhd,bkhd->bhqk', query_rows, key_rows, precision=HIGHEST_PRECISION) * scaling)
            probs_low = low(jax.nn.softmax(scores, axis=-1))
            attended = jnp.einsum('bhqk,bkhd->bqhd', probs_low, value_rows, precision=HIGHEST_PRECISION)
            attended = low(low_back(attended.reshape(block_images, PATCHES, D)))
            attn_out = low_back(jnp.einsum('bpd,de->bpe', attended, proj_mat, precision=HIGHEST_PRECISION))
            return block_in + gate_blk[:, None, :] * attn_out
        blocks = (inputs.reshape(block_count, block_images, PATCHES, D), shift_attn.reshape(block_count, block_images, D), scale_attn.reshape(block_count, block_images, D), gate_attn.reshape(block_count, block_images, D))
        middle = lax.map(jax.checkpoint(attend), blocks).reshape(IMAGES, PATCHES, D)
        mix_in = low(normalize(middle) * (1.0 + scale_mix[:, None, :]) + shift_mix[:, None, :]).reshape(IMAGES * PATCHES, D)
        shared_act = low(jax.nn.gelu(low_back(dot_high(mix_in, up_mat))))
        shared_out = low_back(dot_high(shared_act, down_mat))
        logits = low_back(dot_high(mix_in, router_mat))
        chosen = lax.optimization_barrier(jnp.sum(logits[:, None, :] * chosen_hot, axis=-1))
        gate_vals = jax.nn.softmax(chosen, axis=-1)
        padded = jnp.concatenate([mix_in.reshape(DEVICES, TOK_DEV, D), jnp.zeros((DEVICES, 1, D), mix_in.dtype)], axis=1)
        outgoing = padded[device_ids, slot_owner]
        outgoing = outgoing.reshape(DEVICES, EXPERTS, CAP, D).transpose(1, 0, 2, 3).reshape(EXPERTS, DEVICES * CAP, D)

        def expert(item):
            rows_in, up_one, down_one = item
            hidden = low(jax.nn.gelu(low_back(dot_high(rows_in, up_one))))
            return low(low_back(dot_high(hidden, down_one)))
        results = lax.map(jax.checkpoint(expert), (outgoing, expert_ups, expert_downs))
        results = results.reshape(EXPERTS, DEVICES, CAP, D).transpose(1, 0, 2, 3).reshape(DEVICES, EXPERTS * CAP, D)
        routed = results[device_ids, slot_index].reshape(IMAGES * PATCHES, TOP, D)
        mixture = shared_out + lax.optimization_barrier(jnp.sum(gate_vals[:, :, None] * routed, axis=1))
        result = middle + gate_mix[:, None, :] * mixture.reshape(IMAGES, PATCHES, D)
        return result * alive_rows
    result, pullback = jax.vjp(forward, tokens.astype(jnp.float32), condition.astype(jnp.float32), bucket_table.astype(jnp.float32), ada_weight.astype(jnp.float32), ada_bias.astype(jnp.float32), qkv_weight.astype(jnp.float32), proj_weight.astype(jnp.float32), shared_up.astype(jnp.float32), shared_down.astype(jnp.float32), router_weight.astype(jnp.float32), expert_up.astype(jnp.float32), expert_down.astype(jnp.float32))
    grads = pullback(cotangent.astype(jnp.float32))
    return (result.astype(jnp.bfloat16), grads[0], grads[1], grads[2], grads[3], grads[4], grads[5], grads[6], grads[7], grads[8], grads[9], grads[10], grads[11])
```

```python
import jax
import jax.numpy as jnp
from jax import lax
from jax.sharding import PartitionSpec as P

HEADS = 12
TOP = 2


EPSILON = 1e-06


def product(left_mat, right_mat):
    return jnp.dot(left_mat, right_mat, preferred_element_type=jnp.float32)


def product_tn(left_mat, right_mat):
    return lax.dot_general(
        left_mat, right_mat, (((0,), (0,)), ((), ())), preferred_element_type=jnp.float32
    )


def product_nt(left_mat, right_mat):
    return lax.dot_general(
        left_mat, right_mat, (((1,), (1,)), ((), ())), preferred_element_type=jnp.float32
    )


def to_low(tensor):
    return tensor.astype(jnp.bfloat16)


def wide(tensor):
    return tensor.astype(jnp.float32)


def normalize(tensor):
    average = jnp.mean(tensor, axis=-1, keepdims=True)
    centered = tensor - average
    inverse = lax.rsqrt(jnp.mean(centered * centered, axis=-1, keepdims=True) + EPSILON)
    return (centered * inverse, inverse)


def normalize_back(gradient, normed, inverse):
    first_term = jnp.mean(gradient, axis=-1, keepdims=True)
    second_term = jnp.mean(gradient * normed, axis=-1, keepdims=True)
    return inverse * (gradient - first_term - normed * second_term)


def local_back(function, tensor, gradient):
    return jax.vjp(function, tensor)[1](gradient)[0]


def swap(tensor, axis, bit):
    pairs = [(i, i ^ (1 << bit)) for i in range(lax.axis_size(axis))]
    return lax.ppermute(tensor, axis, pairs)


def bits_of(axis):
    return lax.axis_size(axis).bit_length() - 1


def halve(tensor, place, axis, bit):
    mine = (lax.axis_index(axis) >> bit) & 1
    send = lax.dynamic_index_in_dim(tensor, 1 - mine, place, keepdims=False)
    keep = lax.dynamic_index_in_dim(tensor, mine, place, keepdims=False)
    return to_low(wide(keep) + wide(swap(send, axis, bit)))


def scatter_sum(tensor, axis, order):
    count = bits_of(axis)
    tensor = tensor.reshape((2,) * count + tensor.shape[1:])
    left = list(range(count - 1, -1, -1))
    for bit in order:
        place = left.index(bit)
        left.remove(bit)
        tensor = halve(tensor, place, axis, bit)
    return tensor


def gather_near(tensor, axis):
    blocks = {0: tensor}
    for bit in range(bits_of(axis) - 1, -1, -1):
        for far in list(blocks):
            blocks[far ^ (1 << bit)] = swap(blocks[far], axis, bit)
    return [blocks[i] for i in range(len(blocks))]


def gather_order(tensor, axis):
    me = lax.axis_index(axis)
    blocks = jnp.stack(gather_near(tensor, axis))
    return jnp.stack(
        [lax.dynamic_index_in_dim(blocks, i ^ me, 0, keepdims=False) for i in range(blocks.shape[0])]
    )


def return_near(blocks, axis):
    blocks = dict(enumerate(blocks))
    for bit in range(bits_of(axis)):
        for far in [r for r in blocks if r >> bit & 1]:
            got = swap(to_low(blocks.pop(far)), axis, bit)
            blocks[far ^ (1 << bit)] = wide(blocks[far ^ (1 << bit)]) + wide(got)
    return blocks[0]


def per_device(
    tokens,
    condition,
    bucket,
    live_mask,
    routes,
    bucket_table,
    ada_weight,
    ada_bias,
    qkv_weight,
    proj_weight,
    shared_up,
    shared_down,
    router_weight,
    expert_up,
    expert_down,
    cotangent,
):
    image_count, patch_count, width = tokens.shape
    rows = image_count * patch_count
    head = width // HEADS
    scaling = float(head) ** (-0.5)
    members, groups = lax.axis_size("dp"), lax.axis_size("grp")
    me, group = lax.axis_index("dp"), lax.axis_index("grp")
    experts = expert_up.shape[0] * members
    hidden = shared_up.shape[1]
    table_rows = bucket_table.shape[0]
    own_up, own_down = expert_up[0], expert_down[0]

    inputs = wide(tokens[0])
    selector = wide(bucket[:, None] == jnp.arange(table_rows, dtype=jnp.int32)[None, :])
    conditioned = wide(condition) + jnp.dot(
        selector, wide(bucket_table), precision=lax.Precision.HIGHEST
    )
    activated = to_low(jax.nn.silu(conditioned))
    modulation = product(activated, ada_weight) + wide(ada_bias)
    shift_attn, scale_attn, gate_attn, shift_mix, scale_mix, gate_mix = jnp.split(
        modulation, 6, axis=1
    )
    alive = wide(live_mask)[0]
    grad_result = wide(cotangent[0]) * alive
    grad_mixture = to_low(gate_mix * grad_result)
    expert_ids = jnp.arange(experts, dtype=jnp.int32)
    chosen = jnp.any(routes[0][:, :, None] == expert_ids[None, None, :], axis=1)
    grads_in = jnp.concatenate(
        [grad_mixture, jnp.pad(to_low(chosen), ((0, 0), (0, 128 - experts)))], axis=1
    )
    grads_in = jnp.concatenate(gather_near(grads_in, "dp"), axis=0)

    normed_one, inverse_one = normalize(inputs)
    attn_in = to_low(normed_one * (1.0 + scale_attn) + shift_attn)
    projected = to_low(product(attn_in, qkv_weight)).reshape(rows, 3, HEADS, head)
    query, key, value = [projected[:, i] for i in range(3)]
    scores = jnp.einsum("qhd,khd->hqk", query, key, preferred_element_type=jnp.float32) * scaling
    top_score = jnp.max(scores, axis=-1, keepdims=True)
    weights_exp = jnp.exp(scores - top_score)
    totals = jnp.sum(weights_exp, axis=-1, keepdims=True)
    log_total = top_score + jnp.log(totals)
    probs_first = to_low(weights_exp / totals)
    attended = jnp.einsum("hqk,khd->qhd", probs_first, value, preferred_element_type=jnp.float32)
    attended = to_low(attended.reshape(rows, width))
    attn_out = product(attended, proj_weight)
    middle = inputs + gate_attn * attn_out
    normed_two, inverse_two = normalize(middle)
    mix_in = to_low(normed_two * (1.0 + scale_mix) + shift_mix)

    seen = jnp.concatenate(gather_near(mix_in, "dp"), axis=0)
    grad_seen, seen_hot = grads_in[:, :width], wide(grads_in[:, width : width + experts])
    logits = product(seen, router_weight)
    top_logit = jnp.max(jnp.where(seen_hot > 0, logits, -jnp.inf), axis=1, keepdims=True)
    gates = jnp.where(seen_hot > 0, jnp.exp(logits - top_logit), 0.0)
    gates = gates / jnp.sum(gates, axis=1, keepdims=True)
    mine_hot = wide(expert_ids == me)[None, :]
    gate = jnp.sum(gates * mine_hot, axis=1, keepdims=True)

    part = hidden // (groups * members)
    part_up = lax.dynamic_index_in_dim(
        shared_up.reshape(width, groups, members, part), me, 2, keepdims=False
    ).reshape(width, groups * part)
    part_down = lax.dynamic_index_in_dim(
        shared_down.reshape(groups, members, part, width), me, 1, keepdims=False
    ).reshape(groups * part, width)

    def feed(up, down, grads):
        pre = product(seen, up)
        act = to_low(jax.nn.gelu(pre))
        out = product(act, down)
        grad_down = to_low(product_tn(act, grads))
        grad_pre = to_low(local_back(jax.nn.gelu, pre, product_nt(grads, down)))
        grad_up = to_low(product_tn(seen, grad_pre))
        return out, product_nt(grad_pre, up), grad_up, grad_down

    shared_out, shared_back, grad_part_up, grad_part_down = feed(part_up, part_down, grad_seen)
    grad_routed = to_low(gate * wide(grad_seen))
    routed, routed_back, grad_own_up, grad_own_down = feed(own_up, own_down, grad_routed)
    routed = wide(to_low(routed))
    weighed = jnp.sum(wide(grad_routed) * routed, axis=1, keepdims=True) * mine_hot
    weighed_high = to_low(weighed)
    weighed_low = to_low(weighed - wide(weighed_high))
    back = jnp.concatenate(
        [
            to_low(shared_back + routed_back),
            weighed_high,
            weighed_low,
            jnp.zeros((members * rows, 128 - 2 * experts), jnp.bfloat16),
        ],
        axis=1,
    )
    mixed = to_low(shared_out + gate * routed)
    back = return_near(jnp.split(back, members), "dp")
    mixture = return_near(jnp.split(mixed, members), "dp")

    result = (middle + gate_mix * mixture) * alive
    mixed_out = to_low(result)
    grad_gate_mix = jnp.sum(grad_result * mixture, axis=0, keepdims=True)
    weighed = back[:, width : width + experts] + back[:, width + experts : width + 2 * experts]
    own_gates = gates[:rows]
    grad_logits = to_low(weighed - own_gates * jnp.sum(weighed, axis=1, keepdims=True))
    grad_router = product_tn(mix_in, grad_logits)
    grad_mix_in = back[:, :width] + product_nt(grad_logits, router_weight)
    grad_shift_mix = jnp.sum(grad_mix_in, axis=0, keepdims=True)
    grad_scale_mix = jnp.sum(grad_mix_in * normed_two, axis=0, keepdims=True)
    grad_middle = grad_result + normalize_back(
        grad_mix_in * (1.0 + scale_mix), normed_two, inverse_two
    )
    grad_gate_attn = jnp.sum(grad_middle * attn_out, axis=0, keepdims=True)
    grad_attn_out = to_low(gate_attn * grad_middle)
    grad_proj = product_tn(attended, grad_attn_out)
    grad_attended = to_low(product_nt(grad_attn_out, proj_weight)).reshape(rows, HEADS, head)
    scores_again = (
        jnp.einsum("qhd,khd->hqk", query, key, preferred_element_type=jnp.float32) * scaling
    )
    probs_again = jnp.exp(scores_again - log_total)
    grad_probs = jnp.einsum(
        "qhd,khd->hqk", grad_attended, value, preferred_element_type=jnp.float32
    )
    grad_value = jnp.einsum(
        "hqk,qhd->khd", to_low(probs_again), grad_attended, preferred_element_type=jnp.float32
    )
    grad_scores = to_low(
        probs_again * (grad_probs - jnp.sum(probs_again * grad_probs, axis=-1, keepdims=True))
    )
    grad_query = (
        jnp.einsum("hqk,khd->qhd", grad_scores, key, preferred_element_type=jnp.float32) * scaling
    )
    grad_key = (
        jnp.einsum("hqk,qhd->khd", grad_scores, query, preferred_element_type=jnp.float32) * scaling
    )
    grad_projected = to_low(
        jnp.stack([grad_query, grad_key, grad_value], axis=1).reshape(rows, 3 * width)
    )
    grad_qkv = product_tn(attn_in, grad_projected)
    grad_attn_in = product_nt(grad_projected, qkv_weight)
    grad_shift_attn = jnp.sum(grad_attn_in, axis=0, keepdims=True)
    grad_scale_attn = jnp.sum(grad_attn_in * normed_one, axis=0, keepdims=True)
    grad_tokens = grad_middle + normalize_back(
        grad_attn_in * (1.0 + scale_attn), normed_one, inverse_one
    )
    grad_modulation = jnp.concatenate(
        [
            grad_shift_attn,
            grad_scale_attn,
            grad_gate_attn,
            grad_shift_mix,
            grad_scale_mix,
            grad_gate_mix,
        ],
        axis=1,
    )
    grad_mod_low = to_low(grad_modulation)
    grad_condition = local_back(jax.nn.silu, conditioned, product_nt(grad_mod_low, ada_weight))

    share = table_rows // groups
    near = wide(bucket[:, None] == group * share + jnp.arange(share, dtype=jnp.int32)[None, :])
    table_part = near.T * grad_condition
    for bit in range(bits_of("dp")):
        table_part = table_part + swap(table_part, "dp", bit)

    factors = jnp.concatenate([activated, grad_mod_low], axis=1)
    for axis in ("dp", "grp"):
        for bit in range(bits_of(axis)):
            factors = jnp.concatenate([factors, swap(factors, axis, bit)], axis=0)
    shard = width // groups
    left = lax.dynamic_slice_in_dim(factors[:, :width], group * shard, shard, axis=1)
    right = factors[:, width:]
    ada_w_part = product_tn(left, right)
    ada_share = 6 * width // groups
    ada_b_part = jnp.sum(
        wide(lax.dynamic_slice_in_dim(right, group * ada_share, ada_share, axis=1)), axis=0
    )

    y_first = tuple(range(bits_of("grp")))
    z_first = y_first[1:] + y_first[:1]

    def over_groups(tensor, order):
        return scatter_sum(
            tensor.reshape((groups, tensor.shape[0] // groups) + tensor.shape[1:]), "grp", order
        )

    up_part = over_groups(grad_part_up, z_first)
    down_part = over_groups(grad_part_down, y_first)
    expert_up_part = over_groups(grad_own_up, y_first)
    expert_down_part = over_groups(grad_own_down, y_first)
    up_part = wide(gather_order(up_part, "dp")).reshape(members, shard, groups, part)
    up_part = up_part.transpose(1, 2, 0, 3).reshape(shard, hidden)
    down_part = wide(gather_order(down_part, "dp")).reshape(hidden // groups, width)

    def over_all(tensor):
        tensor = to_low(tensor)
        columns = tensor.shape[1]
        tensor = tensor.reshape(groups, members, -1, columns).swapaxes(0, 1)
        tensor = scatter_sum(tensor, "dp", range(bits_of("dp")))
        tensor = scatter_sum(tensor, "grp", y_first)
        return wide(gather_order(tensor, "dp")).reshape(-1, columns)

    proj_part = over_all(
        jnp.concatenate(
            [grad_proj, grad_router, jnp.zeros((width, 128 - experts), jnp.float32)], axis=1
        )
    )
    qkv_part = over_all(grad_qkv)
    return (
        mixed_out[None],
        grad_tokens[None],
        grad_condition,
        table_part,
        ada_w_part,
        ada_b_part,
        qkv_part,
        proj_part[:, :width],
        up_part,
        down_part,
        proj_part[:, width : width + experts],
        wide(expert_up_part)[None],
        wide(expert_down_part)[None],
    )


def solution(mesh):
    in_specs = (
        P(("grp", "dp"), None, None),
        P(("grp", "dp"), None),
        P(("grp", "dp")),
        P(("grp", "dp")),
        P(("grp", "dp"), None, None),
        P(),
        P(),
        P(),
        P(),
        P(),
        P(),
        P(),
        P(),
        P("dp", None, None),
        P("dp", None, None),
        P(("grp", "dp"), None, None),
    )
    out_specs = (
        P(("grp", "dp"), None, None),
        P(("grp", "dp"), None, None),
        P(("grp", "dp"), None),
        P("grp", None),
        P("grp", None),
        P("grp"),
        P("grp", None),
        P("grp", None),
        P("grp", None),
        P("grp", None),
        P("grp", None),
        P("dp", "grp", None),
        P("dp", "grp", None),
    )
    return jax.shard_map(
        per_device, mesh=mesh, in_specs=in_specs, out_specs=out_specs, check_vma=False
    )
```

```python
import functools
import math

import jax
import jax.numpy as jnp
from jax import lax
from jax.experimental import pallas as pl
from jax.experimental.pallas import tpu as pltpu
from jax.sharding import PartitionSpec as P

HEADS = 12
LANES = 128
CHUNKS = 3
PEAK = 1.15e9
MOST = 58


EPSILON = 1e-06
CURVE = math.sqrt(2.0 / math.pi)
CUBIC = 0.044715

low, full = jnp.bfloat16, jnp.float32
VMEM = pl.BlockSpec(memory_space=pltpu.VMEM)
SMEM = pl.BlockSpec(memory_space=pltpu.SMEM)
HBM = pl.BlockSpec(memory_space=pltpu.MemorySpace.HBM)


def product(left_mat, right_mat, left_dim=1, right_dim=0):
    return lax.dot_general(
        left_mat,
        right_mat,
        (((left_dim,), (right_dim,)), ((), ())),
        preferred_element_type=jnp.float32,
    )


def product_nt(left_mat, right_mat):
    return product(left_mat, right_mat, 1, 1)


def product_tn(left_mat, right_mat):
    return product(left_mat, right_mat, 0, 0)


def to_low(tensor):
    return tensor.astype(low)


def wide(tensor):
    return tensor.astype(full)


def like(shape, kind):
    return jax.ShapeDtypeStruct(shape, kind)


def kernel_call(
    body, outs, in_specs, args, scratch=(), megabytes=24, microseconds=1, out_specs=None
):
    return pl.pallas_call(
        body,
        out_shape=outs,
        in_specs=in_specs,
        out_specs=out_specs or [VMEM] * len(outs),
        scratch_shapes=list(scratch),
        compiler_params=pltpu.CompilerParams(vmem_limit_bytes=megabytes << 20),
        cost_estimate=pl.CostEstimate(
            flops=int(microseconds * PEAK), bytes_accessed=0, transcendentals=0
        ),
    )(*args)


def normalize(tensor):
    average = jnp.mean(tensor, axis=-1, keepdims=True)
    centered = tensor - average
    inverse = lax.rsqrt(jnp.mean(centered * centered, axis=-1, keepdims=True) + EPSILON)
    return (centered * inverse, inverse)


def normalize_back(gradient, normed, inverse):
    first_term = jnp.mean(gradient, axis=-1, keepdims=True)
    second_term = jnp.mean(gradient * normed, axis=-1, keepdims=True)
    return inverse * (gradient - first_term - normed * second_term)


def column_sum(tensor):
    return jnp.sum(tensor, axis=0, keepdims=True)


def gelu_pair(pre):
    square = pre * pre
    bend = jnp.tanh(CURVE * (pre + CUBIC * pre * square))
    half = 0.5 + 0.5 * bend
    slope = half + (0.5 * CURVE) * pre * (1.0 - bend * bend) * (1.0 + 3.0 * CUBIC * square)
    return pre * half, slope


def halves(width):
    lane = lax.broadcasted_iota(jnp.int32, (1, LANES), 1)
    return [lane // width == i for i in range(LANES // width)]


def attend_body(
    tokens,
    condition,
    bucket,
    live,
    routes,
    table,
    ada_bias,
    router,
    ada_hbm,
    qkv_hbm,
    proj_hbm,
    packed,
    gates_out,
    modulation_out,
    conditioned_out,
    activated_out,
    attn_in_hbm,
    projected_hbm,
    log_hbm,
    attended_hbm,
    attn_out_hbm,
    middle_hbm,
    attn_in_out,
    projected_out,
    log_out,
    attended_out,
    attn_out_out,
    middle_out,
    ada,
    qkv,
    proj,
    sems,
):
    rows, width = tokens.shape
    experts = router.shape[0]
    leaving = []

    def leave(source, target):
        copy = pltpu.make_async_copy(source, target, sems.at[4 + len(leaving)])
        copy.start()
        leaving.append(copy)

    head = width // HEADS
    scaling = float(head) ** (-0.5)
    early = 2 * width
    copies = [
        pltpu.make_async_copy(ada_hbm.at[:, :early], ada.at[:, :early], sems.at[0]),
        pltpu.make_async_copy(qkv_hbm, qkv, sems.at[1]),
        pltpu.make_async_copy(ada_hbm.at[:, early:], ada.at[:, early:], sems.at[2]),
        pltpu.make_async_copy(proj_hbm, proj, sems.at[3]),
    ]
    for copy in copies:
        copy.start()

    named = lax.broadcasted_iota(jnp.int32, (table.shape[0], 1), 0) == bucket[0]
    conditioned = wide(condition[...]) + column_sum(jnp.where(named, wide(table[...]), 0.0))
    activated = to_low(conditioned * (1.0 / (1.0 + jnp.exp(-conditioned))))
    conditioned_out[...] = conditioned
    activated_out[...] = activated
    activated = jnp.broadcast_to(activated, (16, width))

    bias = wide(ada_bias[...])
    bias = jnp.concatenate([bias[i : i + 1] for i in range(bias.shape[0])], axis=1)
    inputs = wide(tokens[...])
    normed, _ = normalize(inputs)
    copies[0].wait()
    modulation_out[:, :early] = product(activated, ada[:, :early])[:1] + bias[:, :early]
    shift_attn = modulation_out[:, :width]
    scale_attn = modulation_out[:, width:early]
    attn_in = to_low(normed * (1.0 + scale_attn) + shift_attn)
    attn_in_out[...] = attn_in
    leave(attn_in_out, attn_in_hbm)
    copies[1].wait()
    projected_out[...] = to_low(product(attn_in, qkv[...]))
    leave(projected_out, projected_hbm)
    copies[2].wait()
    modulation_out[:, early:] = product(activated, ada[:, early:])[:1] + bias[:, early:]

    masks = halves(head)
    column = lax.broadcasted_iota(jnp.int32, (1, LANES), 1)
    logs = jnp.zeros((rows, LANES), full)
    for block in range(width // LANES):
        at = pl.ds(block * LANES, LANES)
        query = projected_out[:, at]
        key = projected_out[:, pl.ds(width + block * LANES, LANES)]
        value = projected_out[:, pl.ds(2 * width + block * LANES, LANES)]
        total = jnp.zeros((rows, LANES), full)
        for i, mask in enumerate(masks):
            scores = product_nt(jnp.where(mask, query, jnp.zeros_like(query)), key) * scaling
            top = jnp.max(scores, axis=-1, keepdims=True)
            raised = jnp.exp(scores - top)
            whole = jnp.sum(raised, axis=-1, keepdims=True)
            probs = to_low(raised / whole)
            logs = jnp.where(column == block * len(masks) + i, top + jnp.log(whole), logs)
            total = jnp.where(mask, product(probs, value), total)
        attended_out[:, at] = to_low(total)
    log_out[...] = logs
    leave(log_out, log_hbm)
    leave(attended_out, attended_hbm)

    copies[3].wait()
    attn_out = product(attended_out[...], proj[...])
    attn_out_out[...] = attn_out
    leave(attn_out_out, attn_out_hbm)
    piece = lambda i: modulation_out[:, pl.ds(i * width, width)]
    middle = inputs + piece(2) * attn_out
    middle_out[...] = middle
    leave(middle_out, middle_hbm)
    normed, _ = normalize(middle)
    mix_in = to_low(normed * (1.0 + piece(4)) + piece(3))
    packed[:rows, :] = mix_in

    logits = product_nt(router[...], mix_in)
    ids = lax.broadcasted_iota(jnp.int32, (experts, rows), 0)
    hot = (routes[:1] == ids) | (routes[1:2] == ids)
    top = jnp.max(jnp.where(hot, logits, -jnp.inf), axis=0, keepdims=True)
    turned = jnp.where(hot, jnp.exp(jnp.where(hot, logits, top) - top), 0.0)
    turned = turned / jnp.sum(turned, axis=0, keepdims=True)
    gates_out[...] = jnp.transpose(
        jnp.concatenate([turned, jnp.zeros((LANES - experts, rows), full)], axis=0)
    )
    gate_mix = piece(5) * wide(live[0])
    extra = packed.shape[0] - rows
    high, turned_high = to_low(gate_mix), to_low(turned)
    wall = jnp.zeros((experts, width - rows), full)
    packed[rows:, :] = to_low(
        jnp.concatenate(
            [
                jnp.concatenate([wide(turned_high), wall], axis=1),
                jnp.concatenate([turned - wide(turned_high), wall], axis=1),
                wide(high),
                gate_mix - wide(high),
                jnp.zeros((extra - 2 * experts - 2, width), full),
            ],
            axis=0,
        )
    )
    for copy in leaving:
        copy.wait()


class Mover:
    def __init__(self, sems):
        self.sems, self.count, self.open = sems, 0, []

    def start(self, source, target, keep=True):
        copy = pltpu.make_async_copy(source, target, self.sems.at[self.count])
        copy.start()
        self.count += 1
        if keep:
            self.open.append(copy)
        return copy

    def finish(self):
        for copy in self.open:
            copy.wait()


def wait(copies):
    while copies:
        copies.pop().wait()


def pick_body(members, shared_up, part_up):
    groups = lax.axis_size("grp")
    span = shared_up.shape[1] // groups
    part = span // members
    pick = spread_units(span, part, lax.axis_index("dp"), 0)
    for i in range(0, groups, 4):
        part_up[:, pl.ds(i * part, 4 * part)] = to_low(
            product(shared_up[:, pl.ds(i * span, 4 * span)], pick)
        )


def spread_units(span, part, member, dim):
    shape = (4 * span, 4 * part) if dim == 0 else (4 * part, 4 * span)
    whole = lax.broadcasted_iota(jnp.int32, shape, dim)
    own = lax.broadcasted_iota(jnp.int32, shape, 1 - dim)
    place = own + (own // part) * (span - part) + member * part
    return to_low(jnp.where(whole == place, 1.0, 0.0))


def parted(groups, bit, mine, i):
    return ((i >> bit) << (bit + 1)) + (mine << bit) + (i & ((1 << bit) - 1))


def bring_part_down(mover, members, shared_down, part_down):
    groups = lax.axis_size("grp")
    span = shared_down.shape[0] // groups
    part = span // members
    copies = []
    for i in range(groups):
        start = pl.multiple_of(i * span + lax.axis_index("dp") * part, 16)
        copies.append(
            mover.start(
                shared_down.at[pl.ds(start, part)], part_down.at[pl.ds(i * part, part)], False
            )
        )
    return copies


def bring_cut(mover, chunk, half, expert, own, lanes):
    groups = lax.axis_size("grp")
    span = expert.shape[2 if lanes else 1] // groups
    cut = span // CHUNKS
    side = lax.axis_index("grp") & 1
    copies = []
    for place in range(groups // 2):
        group = 2 * place + (side if half else 1 - side)
        start = pl.multiple_of(group * span + chunk * cut, LANES)
        to = pl.ds((half * groups // 2 + place) * cut, cut)
        if lanes:
            copies.append(mover.start(expert.at[0, :, pl.ds(start, cut)], own.at[:, to], False))
        else:
            copies.append(mover.start(expert.at[0, pl.ds(start, cut)], own.at[to], False))
    return copies


def feed_rows(mover, bit, rows, seen, grads, up, down, act, grad_pre, up_keep, up_send, held, outs, waits, ordered):
    act_out, pre_out, up_keep_out, up_send_out, put_down = outs
    wait_up, wait_down, wait_seen, wait_grads = waits
    groups = lax.axis_size("grp")
    mine = (lax.axis_index("grp") >> bit) & 1
    side = lax.axis_index("grp") & 1
    share = seen.shape[1] // groups
    step = held.shape[1]
    for number, start in enumerate(range(0, up.shape[1], step)):
        at = pl.ds(start, step)
        wait(wait_up[number])
        slopes = []
        for i in range(0, seen.shape[0], rows):
            wait(wait_seen[i // rows])
            raised, slope = gelu_pair(product(seen[pl.ds(i, rows), :], up[:, at]))
            act[pl.ds(i, rows), at] = to_low(raised)
            slopes.append(slope)
            if i == 0:
                wait(wait_down[number])
            wait(wait_grads[i // rows])
            slope = slopes.pop()
            grad_pre[pl.ds(i, rows), at] = to_low(
                slope * product_nt(grads[pl.ds(i, rows), :], down[at, :])
            )
        if act_out is not None:
            mover.start(act.at[:, at], act_out.at[:, at])
            mover.start(grad_pre.at[:, at], pre_out.at[:, at])
        held[...] = product_tn(seen[...], grad_pre[:, at])
        if ordered:
            at_up = pl.ds(pl.multiple_of((1 - side if number == 0 else side) * step, LANES), step)
        else:
            at_up = at
        for target, out, value in ((up_send, up_send_out, 1 - mine), (up_keep, up_keep_out, mine)):
            for i in range(groups // 2):
                first = pl.multiple_of(parted(groups, bit, value, i) * share, 8)
                target[i, :, at] = to_low(held[pl.ds(first, share)])
            mover.start(target.at[:, :, at], out.at[:, :, at_up])
        put_down(number, at, to_low(product_tn(act[:, at], grads[...])))


def shared_body(bit, members, rows, experts, tiled, *refs):
    packs_hbm, cotangents_hbm = refs[:members], refs[members : 2 * members]
    (
        up_hbm,
        down_hbm,
        seen_out,
        routed_out,
        gate_out,
        up_keep_out,
        up_send_out,
        down_out,
        act_out,
        pre_out,
        packs,
        cotangents,
        up,
        down,
        seen,
        routed_grads,
        grads,
        gate_held,
        act,
        grad_pre,
        up_keep,
        up_send,
        grad_down,
        held,
        sems,
    ) = refs[2 * members :]
    mover = Mover(sems)
    width = seen.shape[1]
    me = lax.axis_index("dp")
    named = lax.broadcasted_iota(jnp.int32, (experts, 1), 0) == me
    pack_copies = [mover.start(p, packs.at[i], False) for i, p in enumerate(packs_hbm)]
    up_copy = mover.start(up_hbm, up, False)
    cotangent_copies = [mover.start(c, cotangents.at[i], False) for i, c in enumerate(cotangents_hbm)]
    if tiled:
        down_copies = bring_part_down(mover, members, down_hbm, down)
    else:
        down_copies = [mover.start(down_hbm, down, False)]
    for i in range(members):
        at = pl.ds(i * rows, rows)
        pack_copies[i].wait()
        seen[at, :] = packs[i, :rows, :]
        extra = wide(packs[i, rows:, :])
        gates = extra[:experts, :rows] + extra[experts : 2 * experts, :rows]
        gate = column_sum(jnp.where(named, gates, 0.0))
        gate = jnp.transpose(jnp.broadcast_to(gate, (LANES, rows)))
        gate_held[at, :] = gate
        gate_mix = extra[2 * experts : 2 * experts + 1] + extra[2 * experts + 1 : 2 * experts + 2]
        cotangent_copies[i].wait()
        mixture_grads = to_low(gate_mix * wide(cotangents[i]))
        grads[at, :] = mixture_grads
        routed_grads[at, :] = to_low(gate[:, :1] * wide(mixture_grads))
    mover.start(seen, seen_out)
    mover.start(routed_grads, routed_out)
    mover.start(gate_held, gate_out)

    def put_down(number, at, value):
        grad_down[at, :] = value
        mover.start(grad_down.at[at], down_out.at[at])

    blocks = range(seen.shape[0] // rows)
    waits = ([[up_copy], []], [down_copies, []], [[] for _ in blocks], [[] for _ in blocks])
    outs = (act_out, pre_out, up_keep_out, up_send_out, put_down)
    feed_rows(
        mover, bit, rows, seen, grads, up, down, act, grad_pre, up_keep, up_send, held, outs, waits, False
    )
    mover.finish()


def bring_rows(mover, rows, source, target):
    return [
        [mover.start(source.at[pl.ds(i, rows)], target.at[pl.ds(i, rows)], False)]
        for i in range(0, source.shape[0], rows)
    ]


def bring_cut_all(mover, chunk, tiled, up_hbm, down_hbm, up, down, seen, grads, rows):
    if tiled:
        wait_up = [bring_cut(mover, chunk, 0, up_hbm, up, True)]
        wait_seen = bring_rows(mover, rows, *seen)
        wait_down = [bring_cut(mover, chunk, 0, down_hbm, down, False)]
        wait_grads = bring_rows(mover, rows, *grads)
        wait_up.append(bring_cut(mover, chunk, 1, up_hbm, up, True))
        wait_down.append(bring_cut(mover, chunk, 1, down_hbm, down, False))
    else:
        wait_up = [[mover.start(up_hbm, up, False)], []]
        wait_seen = bring_rows(mover, rows, *seen)
        wait_down = [[mover.start(down_hbm, down, False)], []]
        wait_grads = bring_rows(mover, rows, *grads)
    return wait_up, wait_down, wait_seen, wait_grads


def routed_body(
    bit,
    chunk,
    rows,
    tiled,
    seen_hbm,
    grads_hbm,
    up_hbm,
    down_hbm,
    up_keep_out,
    up_send_out,
    down_keep_out,
    down_send_out,
    act_out,
    pre_out,
    seen,
    grads,
    up,
    down,
    act,
    grad_pre,
    up_keep,
    up_send,
    down_keep,
    down_send,
    held,
    sems,
):
    mover = Mover(sems)
    waits = bring_cut_all(
        mover, chunk, tiled, up_hbm, down_hbm, up, down, (seen_hbm, seen), (grads_hbm, grads), rows
    )

    def put_down(number, at, value):
        target, out = ((down_send, down_send_out), (down_keep, down_keep_out))[number]
        target[...] = value.reshape(target.shape)
        mover.start(target, out)

    outs = (act_out, pre_out, up_keep_out, up_send_out, put_down)
    feed_rows(
        mover, bit, rows, seen, grads, up, down, act, grad_pre, up_keep, up_send, held, outs, waits, True
    )
    mover.finish()


def result_body(bit, members, rows, block, experts, tiled, *refs):
    parts = 1 + CHUNKS
    acts_hbm, pres_hbm = refs[:CHUNKS], refs[CHUNKS : 2 * CHUNKS]
    given = 4 if tiled else 2 * parts
    weights_hbm = refs[2 * CHUNKS : 2 * CHUNKS + given]
    rest = refs[2 * CHUNKS + given :]
    seen_hbm, grads_hbm, gate_hbm = rest[:3]
    up_keep_out, up_send_out, down_keep_out, down_send_out = rest[3:7]
    back_keep_out, back_send_out, mixed_keep_out, mixed_send_out = rest[7:11]
    scratch, sems = rest[11:-1], rest[-1]
    acts, pres, ups, downs = [scratch[i * parts : (i + 1) * parts] for i in range(4)]
    seen, grads, gate, back, up_keep, up_send, down_keep, down_send, held = scratch[4 * parts :]
    mover = Mover(sems)
    width = grads.shape[1]
    me = lax.axis_index("dp")
    column = lax.broadcasted_iota(jnp.int32, (1, LANES), 1)
    last = CHUNKS - 1
    if tiled:
        up_hbm, down_hbm = weights_hbm[2:]
    else:
        up_hbm, down_hbm = weights_hbm[parts - 1], weights_hbm[2 * parts - 1]
    waits = bring_cut_all(
        mover,
        last,
        tiled,
        up_hbm,
        down_hbm,
        ups[-1],
        downs[-1],
        (seen_hbm, seen),
        (grads_hbm, grads),
        block,
    )

    def bring_weights(kind, targets):
        if not tiled:
            sources = weights_hbm[kind * parts : (kind + 1) * parts]
            return [[mover.start(a, b, False)] for a, b in zip(sources[:-1], targets)]
        part, expert = weights_hbm[kind], weights_hbm[2 + kind]
        if kind:
            found = [bring_part_down(mover, members, part, targets[0])]
        else:
            found = [[mover.start(part, targets[0], False)]]
        for c in range(last):
            found.append(
                bring_cut(mover, c, 0, expert, targets[1 + c], kind == 0)
                + bring_cut(mover, c, 1, expert, targets[1 + c], kind == 0)
            )
        return found

    more = [mover.start(a, b, False) for a, b in zip(acts_hbm, acts)]
    for found in bring_weights(1, downs):
        more += found
    more.append(mover.start(gate_hbm, gate, False))
    more += [mover.start(a, b, False) for a, b in zip(pres_hbm, pres)]
    for found in bring_weights(0, ups):
        more += found

    def put_down(number, at, value):
        target, out = ((down_send, down_send_out), (down_keep, down_keep_out))[number]
        target[...] = value.reshape(target.shape)
        mover.start(target, out)

    outs = (None, None, up_keep_out, up_send_out, put_down)
    feed_rows(
        mover,
        bit,
        block,
        seen,
        grads,
        ups[-1],
        downs[-1],
        acts[-1],
        pres[-1],
        up_keep,
        up_send,
        held,
        outs,
        waits,
        True,
    )
    wait(more)
    mixed = seen
    for i in [*range(1, members, 2), *range(0, members, 2)]:
        at = pl.ds(i * rows, rows)
        to = pl.ds((i // 2) * rows, rows)
        routed = sum(product(a[at, :], d[...]) for a, d in zip(acts[1:], downs[1:]))
        routed = wide(to_low(routed))
        mixed[at, :] = to_low(product(acts[0][at, :], downs[0][...]) + gate[at, :1] * routed)
        mover.start(mixed.at[at], (mixed_send_out if i % 2 else mixed_keep_out).at[to])
        weighed = jnp.sum(wide(grads[at, :]) * routed, axis=1, keepdims=True)
        high = wide(to_low(weighed))
        back[at, width:] = to_low(
            jnp.where(column == me, high, 0.0)
            + jnp.where(column == experts + me, weighed - high, 0.0)
        )
        back[at, :width] = to_low(sum(product_nt(p[at, :], u[...]) for p, u in zip(pres, ups)))
        mover.start(back.at[at], (back_send_out if i % 2 else back_keep_out).at[to])
    mover.finish()


def middle_back_body(
    kept,
    got,
    packed,
    middle,
    modulation,
    gates,
    cotangent,
    live,
    attn_out,
    attended,
    proj,
    router,
    proj_keep,
    proj_send,
    grad_attended,
    grad_middle_out,
    grad_pieces,
    held,
):
    rows, width = cotangent.shape
    experts = router.shape[0]
    piece = lambda i: modulation[:, pl.ds(i * width, width)]
    back = wide(kept[:, width:]) + wide(got[:, width:])
    weighed = back[:, :experts] + back[:, experts : 2 * experts]
    mine = gates[:, :experts]
    grad_logits = to_low(weighed - mine * jnp.sum(weighed, axis=1, keepdims=True))
    mix_in = packed[:rows, :]
    grad_mix_in = wide(kept[:, :width]) + wide(got[:, :width])
    grad_mix_in = grad_mix_in + product(grad_logits, router[...])
    normed, inverse = normalize(middle[...])
    grad_result = wide(cotangent[...]) * wide(live[0])
    grad_middle = grad_result + normalize_back(grad_mix_in * (1.0 + piece(4)), normed, inverse)
    grad_middle_out[...] = grad_middle
    grad_attn_out = to_low(piece(2) * grad_middle)
    held[:, width:] = jnp.zeros((width, LANES), full)
    held[:, width : width + experts] = product_tn(mix_in, grad_logits)
    held[:, :width] = product_tn(attended[...], grad_attn_out)
    part_rows(held, proj_keep, proj_send, slice(None))
    grad_attended[...] = to_low(product_nt(grad_attn_out, proj[...]))
    grad_pieces[0:1] = column_sum(grad_middle * attn_out[...])
    grad_pieces[1:2] = column_sum(grad_mix_in)
    grad_pieces[2:3] = column_sum(grad_mix_in * normed)


def part_rows(held, keep, send, at):
    groups, members = lax.axis_size("grp"), lax.axis_size("dp")
    share = held.shape[0] // (groups * members)
    if len(keep.shape) == 2:
        keep[:, at] = to_low(held[...])
        return
    mine = lax.axis_index("dp") & 1
    for target, value in ((send, 1 - mine), (keep, mine)):
        for i in range(members // 2):
            for g in range(groups):
                first = pl.multiple_of((g * members + 2 * i + value) * share, 8)
                target[i * groups + g, :, at] = to_low(held[pl.ds(first, share)])


def attend_back_body(
    grad_attended,
    projected,
    logs,
    attn_in,
    tokens,
    grad_middle,
    modulation,
    qkv,
    grad_tokens,
    qkv_keep,
    qkv_send,
    grad_pieces,
    grad_projected,
    held,
):
    rows, width = tokens.shape
    head = width // HEADS
    scaling = float(head) ** (-0.5)
    masks = halves(head)
    column = lax.broadcasted_iota(jnp.int32, (1, LANES), 1)
    for block in range(width // LANES):
        parts = [pl.ds(i * width + block * LANES, LANES) for i in range(3)]
        query, key, value = [projected[:, at] for at in parts]
        grads = grad_attended[:, parts[0]]
        grad_query, grad_key, grad_value = [jnp.zeros((rows, LANES), full)] * 3
        for i, mask in enumerate(masks):
            zero = jnp.zeros_like(query)
            scores = product_nt(jnp.where(mask, query, zero), key) * scaling
            log = jnp.sum(
                jnp.where(column == block * len(masks) + i, logs[...], 0.0), axis=1, keepdims=True
            )
            probs = jnp.exp(scores - log)
            grad_probs = product_nt(jnp.where(mask, grads, zero), value)
            grad_value = jnp.where(mask, product_tn(to_low(probs), grads), grad_value)
            drift = jnp.sum(probs * grad_probs, axis=-1, keepdims=True)
            grad_scores = to_low(probs * (grad_probs - drift))
            grad_query = jnp.where(mask, product(grad_scores, key), grad_query)
            grad_key = jnp.where(mask, product_tn(grad_scores, query), grad_key)
        for at, grad in zip(parts, (grad_query * scaling, grad_key * scaling, grad_value)):
            grad_projected[:, at] = to_low(grad)
    for i in range(3):
        at = pl.ds(i * width, width)
        held[...] = product_tn(attn_in[...], grad_projected[:, at])
        part_rows(held, qkv_keep, qkv_send, at)
    grad_attn_in = product_nt(grad_projected[...], qkv[...])
    normed, inverse = normalize(wide(tokens[...]))
    scale_attn = modulation[:, pl.ds(width, width)]
    grad_pieces[0:1] = column_sum(grad_attn_in)
    grad_pieces[1:2] = column_sum(grad_attn_in * normed)
    grad_tokens[...] = grad_middle[...] + normalize_back(
        grad_attn_in * (1.0 + scale_attn), normed, inverse
    )


def condition_body(
    kept,
    got,
    middle,
    modulation,
    cotangent,
    live,
    attn_pieces,
    mix_pieces,
    conditioned,
    activated,
    bucket,
    ada_hbm,
    mixed_out,
    factors,
    grad_condition,
    table_part,
    ada,
    sem,
):
    rows, width = cotangent.shape
    copy = pltpu.make_async_copy(ada_hbm, ada, sem)
    copy.start()
    alive = wide(live[0])
    gate_mix = modulation[:, pl.ds(5 * width, width)]
    mixture = wide(kept[...]) + wide(got[...])
    mixed_out[...] = to_low((middle[...] + gate_mix * mixture) * alive)
    grad_gate_mix = column_sum(wide(cotangent[...]) * alive * mixture)
    grads = [
        attn_pieces[0:1],
        attn_pieces[1:2],
        mix_pieces[0:1],
        mix_pieces[1:2],
        mix_pieces[2:3],
        grad_gate_mix,
    ]
    factors[...] = to_low(
        jnp.concatenate(grads + [wide(activated[...]), jnp.zeros((1, width), full)], axis=0)
    )
    copy.wait()
    pulled = jnp.zeros((1, width), full)
    for i, grad in enumerate(grads):
        spread = jnp.broadcast_to(to_low(grad), (16, width))
        pulled = pulled + product_nt(spread, ada[:, pl.ds(i * width, width)])[:1]
    drive = conditioned[...]
    gate = 1.0 / (1.0 + jnp.exp(-drive))
    grad = pulled * gate * (1.0 + drive * (1.0 - gate))
    grad_condition[...] = grad
    share = table_part.shape[0]
    row = lax.broadcasted_iota(jnp.int32, (share, 1), 0) + lax.axis_index("grp") * share
    table_part[...] = jnp.where(row == bucket[0], grad, 0.0)


def split_body(mine, keep_a, got_a, keep_b, got_b, keep_out, send_out):
    keep_out[...] = to_low(wide(keep_a[...]) + wide(got_a[...]))
    send_out[...] = to_low(wide(keep_b[...]) + wide(got_b[...]))


def split_sum(axis, bit, place, keep, got):
    mine = ((lax.axis_index(axis) >> bit) & 1).reshape(1)
    count, *block = keep.shape
    spec = lambda other: pl.BlockSpec(
        (1, *block), lambda i, mine: (parted(count, place, mine[0] ^ other, i), 0, 0)
    )
    out = pl.BlockSpec((1, *block), lambda i, mine: (i, 0, 0))
    return pl.pallas_call(
        split_body,
        grid_spec=pltpu.PrefetchScalarGridSpec(
            num_scalar_prefetch=1,
            grid=(count // 2,),
            in_specs=[spec(0), spec(0), spec(1), spec(1)],
            out_specs=[out, out],
        ),
        out_shape=[like((count // 2, *block), low)] * 2,
        compiler_params=pltpu.CompilerParams(vmem_limit_bytes=16 << 20),
        cost_estimate=pl.CostEstimate(flops=int(1.5 * PEAK), bytes_accessed=0, transcendentals=0),
    )(mine, keep, got, keep, got)


def sum_body(keep, got, total):
    total[...] = to_low(wide(keep[...]) + wide(got[...]))


def own_up_body(*refs):
    *pairs, out = refs
    rows, columns = pairs[0].shape
    groups = lax.axis_size("grp")
    cut = columns // groups
    for c in range(CHUNKS):
        total = wide(pairs[2 * c][...]) + wide(pairs[2 * c + 1][...])
        for i in range(groups):
            side, place = i & 1, i >> 1
            start = side * (columns // 2) + place * cut
            out[:, pl.ds(i * cut * CHUNKS + c * cut, cut)] = total[:, start : start + cut]


def own_down_body(*refs):
    *pairs, out = refs
    cut = pairs[0].shape[0]
    for c in range(CHUNKS):
        out[pl.ds(c * cut, cut)] = wide(pairs[2 * c][...]) + wide(pairs[2 * c + 1][...])


def shared_end_body(members, *refs):
    ups, downs, up_out, down_out = refs[:members], refs[members : 2 * members], refs[-2], refs[-1]
    me = lax.axis_index("dp")
    groups = lax.axis_size("grp")
    span = up_out.shape[1] // groups
    part = span // members
    for i in range(0, groups, 4):
        total = 0.0
        for far in range(members):
            pick = spread_units(span, part, me ^ far, 1)
            total = total + product(ups[far][:, pl.ds(i * part, 4 * part)], pick)
        up_out[:, pl.ds(i * span, 4 * span)] = total
    for far in range(members):
        start = pl.multiple_of((me ^ far) * part, 8)
        down_out[pl.ds(start, part)] = wide(downs[far][...])


def rows_end_body(members, *refs):
    blocks, outs = refs[:members], refs[members:]
    me = lax.axis_index("dp")
    share = blocks[0].shape[0]
    for far in range(members):
        start = pl.multiple_of((me ^ far) * share, 8)
        column = 0
        for out in outs:
            out[pl.ds(start, share), :] = wide(blocks[far][:, column : column + out.shape[1]])
            column += out.shape[1]


def bits_of(axis):
    return lax.axis_size(axis).bit_length() - 1


def tie(tensor, *before):
    return lax.optimization_barrier((tensor, *before))[0]


TURNS = """
sd su d0 p u0 t u1 p d1 f t p u2 p q d2 q f u2 q d2 q f
"""


DEPTH_X, DEPTH_Y, DEPTH_Z = 1, 2, 2


class Links:
    depth = {"y": DEPTH_Y, "z": DEPTH_Z, "x": DEPTH_X}

    def __init__(self):
        self.past = {}

    def swap(self, tensor, axis, bit):
        pairs = [(i, i ^ (1 << bit)) for i in range(lax.axis_size(axis))]
        if axis == "dp":
            name = "x" if bit else None
        else:
            name = "y" if bit < bits_of("grp") // 2 else "z"
        past = self.past.setdefault(name, [])
        depth = self.depth.get(name, 0)
        if 0 < depth <= len(past):
            tensor = tie(tensor, past[-depth])
        past.append(lax.ppermute(tensor, axis, pairs))
        return past[-1]


def over_call(body, outs, args):
    return kernel_call(body, outs, [VMEM] * len(args), args, (), 16, 1.5)


class Sum:
    def __init__(self, links, tiled, keep, send, order, left):
        self.links, self.tiled, self.keep, self.send = links, tiled, keep, send
        self.order = list(order)
        self.left = [bit for bit in left if bit != order[0]]

    def move(self, *before):
        send = tie(self.send, *before) if before else self.send
        self.got = self.links.swap(send, *self.order.pop(0))

    def fold(self):
        bit = self.order[0]
        place = len(self.left) - 1 - self.left.index(bit)
        self.left.remove(bit)
        if self.tiled:
            self.keep, self.send = split_sum(*bit, place, self.keep, self.got)
        else:
            total = to_low(wide(self.keep) + wide(self.got))
            self.keep, self.send = split(total, *bit, place)
        return self.send

    def steps(self):
        while self.order:
            self.fold()
            self.move()
            yield

    def terms(self):
        return self.keep[0], self.got[0]


def split(tensor, axis, bit, place):
    mine = (lax.axis_index(axis) >> bit) & 1
    parts = tensor.reshape((-1, 2, 1 << place) + tensor.shape[1:])
    halves_of = [
        lax.dynamic_index_in_dim(parts, i, 1, keepdims=False).reshape((-1,) + tensor.shape[1:])
        for i in (mine, 1 - mine)
    ]
    return halves_of


def gather_near(links, tensor, axis, before=()):
    blocks = {0: tensor}
    for bit in range(bits_of(axis) - 1, -1, -1):
        for far in list(blocks):
            block = tie(blocks[far], *before) if far and not bit and before else blocks[far]
            blocks[far ^ (1 << bit)] = links.swap(block, axis, bit)
    return [blocks[i] for i in range(len(blocks))]


def in_order(blocks, axis):
    me = lax.axis_index(axis)
    blocks = jnp.stack(blocks)
    return jnp.stack(
        [lax.dynamic_index_in_dim(blocks, i ^ me, 0, keepdims=False) for i in range(blocks.shape[0])]
    )


def return_near(links, keep, send, rows):
    total = to_low(wide(keep) + wide(links.swap(send, "dp", 0)))
    for bit in range(1, bits_of("dp")):
        columns = total.shape[-1]
        parts = total.reshape(-1, 2, rows, columns)
        kept, sent = parts[:, 0].reshape(-1, columns), parts[:, 1].reshape(-1, columns)
        got = links.swap(sent, "dp", bit)
        if bit == bits_of("dp") - 1:
            return kept, got
        total = to_low(wide(kept) + wide(got))


def per_device(
    tokens,
    condition,
    bucket,
    live_mask,
    routes,
    bucket_table,
    ada_weight,
    ada_bias,
    qkv_weight,
    proj_weight,
    shared_up,
    shared_down,
    router_weight,
    expert_up,
    expert_down,
    cotangent,
):
    tokens, routes, cotangent = tokens[0], routes[0], cotangent[0]
    rows, width = tokens.shape
    members, groups = lax.axis_size("dp"), lax.axis_size("grp")
    me, group = lax.axis_index("dp"), lax.axis_index("grp")
    experts = expert_up.shape[0] * members
    hidden = shared_up.shape[1]
    table_rows = bucket_table.shape[0]
    seen_rows = members * rows
    y_first = tuple(range(bits_of("grp")))
    z_first = y_first[1:] + y_first[:1]
    y_first, z_first = [tuple(("grp", bit) for bit in bits) for bits in (y_first, z_first)]
    all_left = tuple(("dp", bit) for bit in range(bits_of("dp") - 1, 0, -1)) + y_first[::-1]
    all_order = tuple(("dp", bit) for bit in range(bits_of("dp"))) + y_first

    links = Links()
    cotangents = gather_near(links, cotangent, "dp")

    extra = -(-(2 * experts + 2) // 16) * 16
    saved = [
        like((rows, width), low),
        like((rows, 3 * width), low),
        like((rows, LANES), full),
        like((rows, width), low),
        like((rows, width), full),
        like((rows, width), full),
    ]
    (
        packed,
        gates,
        modulation,
        conditioned,
        activated,
        attn_in,
        projected,
        logs,
        attended,
        attn_out,
        middle,
    ) = kernel_call(
        attend_body,
        [
            like((rows + extra, width), low),
            like((rows, LANES), full),
            like((1, 6 * width), full),
            like((1, width), full),
            like((1, width), low),
        ]
        + saved,
        [VMEM, VMEM, SMEM, SMEM] + [VMEM] * 4 + [HBM] * 3,
        (
            tokens,
            condition,
            bucket,
            live_mask,
            routes.T,
            bucket_table,
            ada_bias.reshape(-1, LANES),
            router_weight.T,
            ada_weight,
            qkv_weight,
            proj_weight,
        ),
        [pltpu.VMEM(out.shape, out.dtype) for out in saved]
        + [
            pltpu.VMEM(ada_weight.shape, low),
            pltpu.VMEM(qkv_weight.shape, low),
            pltpu.VMEM(proj_weight.shape, low),
            pltpu.SemaphoreType.DMA((4 + len(saved),)),
        ],
        MOST,
        10,
        [VMEM] * 5 + [HBM] * len(saved),
    )


    part = hidden // (groups * members)
    cut = hidden // (groups * CHUNKS)
    tiled = cut % LANES == 0
    if tiled:
        [part_up] = kernel_call(
            functools.partial(pick_body, members),
            [like((width, groups * part), low)],
            [VMEM],
            (shared_up,),
            (),
            20,
            4,
        )
        part_down = shared_down
    else:
        part_up = lax.dynamic_index_in_dim(
            shared_up.reshape(width, groups, members, part), me, 2, keepdims=False
        ).reshape(width, groups * part)
        part_down = lax.dynamic_index_in_dim(
            shared_down.reshape(groups, members, part, width), me, 1, keepdims=False
        ).reshape(groups * part, width)
        sides = lambda tensor, place: jnp.concatenate(
            [
                lax.dynamic_index_in_dim(tensor, side, place + 1, keepdims=False)
                for side in (1 - group % 2, group % 2)
            ],
            axis=place,
        )
        own_ups = sides(expert_up[0].reshape(width, groups // 2, 2, CHUNKS, cut), 1)
        own_downs = sides(expert_down[0].reshape(groups // 2, 2, CHUNKS, cut, width), 0)
        ups = [own_ups[:, :, i].reshape(width, groups * cut) for i in range(CHUNKS)]
        downs = [own_downs[:, i].reshape(groups * cut, width) for i in range(CHUNKS)]
    share = width // groups
    packs = gather_near(links, packed, "dp", (part_up,))
    before = {}

    def sum_of(keep, send, order):
        return Sum(links, tiled, keep, send, order, y_first[::-1])

    def room(columns, step):
        return [
            pltpu.VMEM((seen_rows, columns), low),
            pltpu.VMEM((seen_rows, columns), low),
            pltpu.VMEM((groups // 2, share, columns), low),
            pltpu.VMEM((groups // 2, share, columns), low),
        ]

    ups_first = [z_first, z_first, y_first, y_first]
    columns = groups * part
    halved = [like((groups // 2, share, columns), low)] * 2
    patches = pltpu.VMEM((seen_rows, width), low)
    seen, routed_grads, gate, up_keep, up_send, grad_part_down, *kept = kernel_call(
        functools.partial(shared_body, ups_first[0][0][1], members, rows, experts, tiled),
        [
            like((seen_rows, width), low),
            like((seen_rows, width), low),
            like((seen_rows, LANES), full),
        ]
        + halved
        + [like((columns, width), low)]
        + [like((seen_rows, columns), low)] * 2,
        [HBM] * (2 * members + 2),
        (*packs, *cotangents, part_up, part_down),
        [
            pltpu.VMEM((members, rows + extra, width), low),
            pltpu.VMEM((members, rows, width), low),
            pltpu.VMEM((width, columns), low),
            pltpu.VMEM((columns, width), low),
            patches,
            patches,
            patches,
            pltpu.VMEM((seen_rows, LANES), full),
        ]
        + room(columns, 384)
        + [
            pltpu.VMEM((columns, width), low),
            pltpu.VMEM((width, 384), full),
            pltpu.SemaphoreType.DMA((64,)),
        ],
        MOST,
        9,
        [HBM] * 8,
    )
    acts, pres = [kept[0]], [kept[1]]
    sums = {"su": sum_of(up_keep, up_send, ups_first[0])}
    sums["su"].move()
    grad_part_down = grad_part_down.reshape(groups, part, width)
    sums["sd"] = sum_of(*split(grad_part_down, "grp", 0, 0), y_first)
    sums["sd"].move()
    columns = groups * cut
    halved = [like((groups // 2, share, columns), low)] * 2
    halved += [like((groups // 2, cut, width), low)] * 2
    block = seen_rows if members == 4 else rows
    for i in range(CHUNKS - 1):
        if i == 1:
            routed_grads = tie(routed_grads, sums["su"].fold(), sums["sd"].fold())
            for name in ("su", "sd", "d0", "u0"):
                sums[name].move()
        up_keep, up_send, down_keep, down_send, act, grad_pre = kernel_call(
            functools.partial(routed_body, ups_first[1 + i][0][1], i, block, tiled),
            halved + [like((seen_rows, columns), low)] * 2,
            [HBM] * 4,
            (
                seen,
                routed_grads,
                *((expert_up, expert_down) if tiled else (ups[i], downs[i])),
            ),
            [
                patches,
                patches,
                pltpu.VMEM((width, columns), low),
                pltpu.VMEM((columns, width), low),
            ]
            + room(columns, columns // 2)
            + [
                pltpu.VMEM((groups // 2, cut, width), low),
                pltpu.VMEM((groups // 2, cut, width), low),
                pltpu.VMEM((width, columns // 2), full),
                pltpu.SemaphoreType.DMA((64,)),
            ],
            MOST,
            10,
            [HBM] * 6,
        )
        sums["u%d" % i] = sum_of(up_keep, up_send, ups_first[1 + i])
        sums["d%d" % i] = sum_of(down_keep, down_send, y_first)
        acts.append(act)
        pres.append(grad_pre)
    routed_grads = tie(routed_grads, sums["su"].got, sums["sd"].got)
    sums["u1"].move()
    sums["d1"].move()
    (
        up_keep,
        up_send,
        down_keep,
        down_send,
        back_keep,
        back_send,
        mixed_keep,
        mixed_send,
    ) = kernel_call(
        functools.partial(
            result_body, ups_first[-1][0][1], members, rows, block, experts, tiled
        ),
        halved
        + [like((seen_rows // 2, width + LANES), low)] * 2
        + [like((seen_rows // 2, width), low)] * 2,
        [HBM] * (2 * CHUNKS + (4 if tiled else 2 * (1 + CHUNKS)) + 3),
        (
            *acts,
            *pres,
            *(
                (part_up, part_down, expert_up, expert_down)
                if tiled
                else (part_up, *ups, part_down, *downs)
            ),
            seen,
            routed_grads,
            gate,
        ),
        [pltpu.VMEM(a.shape, low) for a in acts]
        + [pltpu.VMEM((seen_rows, columns), low)]
        + [pltpu.VMEM(a.shape, low) for a in pres]
        + [pltpu.VMEM((seen_rows, columns), low)]
        + [pltpu.VMEM((width, groups * part), low)]
        + [pltpu.VMEM((width, columns), low)] * CHUNKS
        + [pltpu.VMEM((groups * part, width), low)]
        + [pltpu.VMEM((columns, width), low)] * CHUNKS
        + [
            patches,
            patches,
            pltpu.VMEM((seen_rows, LANES), full),
            pltpu.VMEM((seen_rows, width + LANES), low),
        ]
        + room(columns, 0)[2:]
        + [
            pltpu.VMEM((groups // 2, cut, width), low),
            pltpu.VMEM((groups // 2, cut, width), low),
            pltpu.VMEM((width, columns // 2), full),
            pltpu.SemaphoreType.DMA((160,)),
        ],
        MOST if members == 4 else 61,
        24,
        [HBM] * 8,
    )
    sums["u2"] = sum_of(up_keep, up_send, ups_first[-1])
    sums["d2"] = sum_of(down_keep, down_send, y_first)
    back = return_near(links, back_keep, back_send, rows)
    mixed = return_near(links, mixed_keep, mixed_send, rows)
    folded = [sums[name].fold() for name in ("su", "sd", "u0", "d0")]
    for name in ("su", "sd", "u0", "d0", "u2", "d2"):
        sums[name].move()

    def row_parts(columns):
        if tiled:
            return [like((members // 2 * groups, share // members, columns), low)] * 2
        return [like((width, columns), low)] * 2

    proj_keep, proj_send, grad_attended, grad_middle, mix_pieces = kernel_call(
        middle_back_body,
        row_parts(width + LANES)
        + [
            like((rows, width), low),
            like((rows, width), full),
            like((8, width), full),
        ],
        [VMEM] * 7 + [SMEM] + [VMEM] * 4,
        (
            back[0],
            tie(back[1], *folded),
            packed,
            middle,
            modulation,
            gates,
            cotangent,
            live_mask,
            attn_out,
            attended,
            proj_weight,
            router_weight.T,
        ),
        [pltpu.VMEM((width, width + LANES), full)],
        20,
        4,
    )
    def all_sum(keep, send):
        if not tiled:
            columns = keep.shape[1]
            tensor = keep.reshape(groups, members, -1, columns)
            tensor = tensor.swapaxes(0, 1).reshape(members * groups, -1, columns)
            keep, send = split(tensor, "dp", 0, bits_of("grp"))
        found = Sum(links, tiled, keep, send, all_order, all_left)
        found.move()
        return found

    sums["p"] = all_sum(proj_keep, proj_send)
    grad_attended = tie(grad_attended, sums["u1"].fold())
    sums["u1"].move()
    sums["p"].fold()
    sums["p"].move()
    grad_tokens, qkv_keep, qkv_send, attn_pieces = kernel_call(
        attend_back_body,
        [like((rows, width), full)] + row_parts(3 * width) + [like((8, width), full)],
        [VMEM] * 8,
        (grad_attended, projected, logs, attn_in, tokens, grad_middle, modulation, qkv_weight),
        [pltpu.VMEM((rows, 3 * width), low), pltpu.VMEM((width, width), full)],
        24,
        8,
    )
    sums["q"] = all_sum(qkv_keep, qkv_send)
    attn_pieces = tie(attn_pieces, sums["d1"].fold(), sums["q"].fold())
    sums["q"].move()
    sums["d1"].move()
    mixed_out, factors, grad_condition, table_part = kernel_call(
        condition_body,
        [
            like((rows, width), low),
            like((8, width), low),
            like((1, width), full),
            like((table_rows // groups, width), full),
        ],
        [VMEM] * 5 + [SMEM] + [VMEM] * 4 + [SMEM, HBM],
        (
            *mixed,
            middle,
            modulation,
            cotangent,
            live_mask,
            attn_pieces,
            mix_pieces,
            conditioned,
            activated,
            bucket,
            ada_weight,
        ),
        [pltpu.VMEM(ada_weight.shape, low), pltpu.SemaphoreType.DMA],
        24,
        4,
    )

    def added(terms):
        if tiled:
            return over_call(sum_body, [like(terms[0].shape, low)], terms)[0]
        return to_low(wide(terms[0]) + wide(terms[1]))

    def steps(name):
        yield from sums[name].steps()
        terms = sums[name].terms()
        if name[0] in "ud":
            return terms
        return gather_near(links, added(terms), "dp")

    def table_flow(table):
        for bit in range(bits_of("dp")):
            table = table + links.swap(table, "dp", bit)
            yield
        return table

    def factor_flow(factors):
        factors = factors[None]
        for axis in ("dp", "grp"):
            for bit in range(bits_of(axis)):
                factors = jnp.concatenate([factors, links.swap(factors, axis, bit)], axis=0)
                yield
        return factors

    running = {name: steps(name) for name in sums}
    running["t"] = table_flow(table_part)
    running["f"] = factor_flow(factors)
    ends = {}

    def advance(name):
        if name not in ends:
            try:
                next(running[name])
            except StopIteration as stop:
                ends[name] = stop.value

    for name in TURNS.split():
        advance(name)
    while len(ends) < len(running):
        for name in running:
            advance(name)

    if tiled:
        up_part, down_part = over_call(
            functools.partial(shared_end_body, members),
            [like((share, hidden), full), like((hidden // groups, width), full)],
            (*ends["su"], *ends["sd"]),
        )
        [expert_up_part] = over_call(
            own_up_body,
            [like((share, hidden), full)],
            [t for i in range(CHUNKS) for t in ends["u%d" % i]],
        )
        [expert_down_part] = over_call(
            own_down_body,
            [like((hidden // groups, width), full)],
            [t for i in range(CHUNKS) for t in ends["d%d" % i]],
        )
        [qkv_part] = over_call(
            functools.partial(rows_end_body, members),
            [like((share, 3 * width), full)],
            ends["q"],
        )
        proj_part, router_part = over_call(
            functools.partial(rows_end_body, members),
            [like((share, width), full), like((share, LANES), full)],
            ends["p"],
        )
    else:
        total = lambda name: wide(ends[name][0]) + wide(ends[name][1])
        up_part = wide(in_order(ends["su"], "dp")).reshape(members, share, groups, part)
        up_part = up_part.transpose(1, 2, 0, 3).reshape(share, hidden)
        down_part = wide(in_order(ends["sd"], "dp")).reshape(hidden // groups, width)
        own_ups = [total("u%d" % i).reshape(share, 2, groups // 2, cut) for i in range(CHUNKS)]
        expert_up_part = jnp.stack(own_ups, axis=3).transpose(0, 2, 1, 3, 4).reshape(share, hidden)
        expert_down_part = jnp.concatenate([total("d%d" % i) for i in range(CHUNKS)], axis=0)
        qkv_part = wide(in_order(ends["q"], "dp")).reshape(share, 3 * width)
        proj_part = wide(in_order(ends["p"], "dp")).reshape(share, width + LANES)
        proj_part, router_part = jnp.split(proj_part, [width], axis=1)
    factors, table_part = ends["f"], ends["t"]
    left = lax.dynamic_slice_in_dim(factors[:, 6], group * share, share, axis=1)
    right = factors[:, :6].reshape(-1, 6 * width)
    ada_w_part = product_tn(left, right)
    ada_share = 6 * width // groups
    ada_b_part = lax.dynamic_slice_in_dim(jnp.sum(wide(right), axis=0), group * ada_share, ada_share)
    return (
        mixed_out[None],
        grad_tokens[None],
        grad_condition,
        table_part,
        ada_w_part,
        ada_b_part,
        qkv_part,
        proj_part,
        up_part,
        down_part,
        router_part[:, :experts],
        expert_up_part[None],
        expert_down_part[None],
    )


def solution(mesh):
    in_specs = (
        P(("grp", "dp"), None, None),
        P(("grp", "dp"), None),
        P(("grp", "dp")),
        P(("grp", "dp")),
        P(("grp", "dp"), None, None),
        P(),
        P(),
        P(),
        P(),
        P(),
        P(),
        P(),
        P(),
        P("dp", None, None),
        P("dp", None, None),
        P(("grp", "dp"), None, None),
    )
    out_specs = (
        P(("grp", "dp"), None, None),
        P(("grp", "dp"), None, None),
        P(("grp", "dp"), None),
        P("grp", None),
        P("grp", None),
        P("grp"),
        P("grp", None),
        P("grp", None),
        P("grp", None),
        P("grp", None),
        P("grp", None),
        P("dp", "grp", None),
        P("dp", "grp", None),
    )
    return jax.shard_map(
        per_device, mesh=mesh, in_specs=in_specs, out_specs=out_specs, check_vma=False
    )
```

```python
import functools
import math

import jax
import jax.numpy as jnp
from jax import lax
from jax.experimental import pallas as pl
from jax.experimental.pallas import tpu as pltpu
from jax.sharding import PartitionSpec as P

HEADS = 12
LANES = 128
CHUNKS = 3
PEAK = 1.15e9
WEIGH = 0.3
MOST = 58
K3A = 58


EPSILON = 1e-06
CURVE = math.sqrt(2.0 / math.pi)
CUBIC = 0.044715

low, full = jnp.bfloat16, jnp.float32
VMEM = pl.BlockSpec(memory_space=pltpu.VMEM)
SMEM = pl.BlockSpec(memory_space=pltpu.SMEM)
HBM = pl.BlockSpec(memory_space=pltpu.MemorySpace.HBM)


def product(left_mat, right_mat, left_dim=1, right_dim=0):
    return lax.dot_general(
        left_mat,
        right_mat,
        (((left_dim,), (right_dim,)), ((), ())),
        preferred_element_type=jnp.float32,
    )


def product_nt(left_mat, right_mat):
    return product(left_mat, right_mat, 1, 1)


def product_tn(left_mat, right_mat):
    return product(left_mat, right_mat, 0, 0)


def to_low(tensor):
    return tensor.astype(low)


def wide(tensor):
    return tensor.astype(full)


def like(shape, kind):
    return jax.ShapeDtypeStruct(shape, kind)


def kernel_call(
    body, outs, in_specs, args, scratch=(), megabytes=24, microseconds=1, out_specs=None
):
    return pl.pallas_call(
        body,
        out_shape=outs,
        in_specs=in_specs,
        out_specs=out_specs or [VMEM] * len(outs),
        scratch_shapes=list(scratch),
        compiler_params=pltpu.CompilerParams(vmem_limit_bytes=megabytes << 20),
        cost_estimate=pl.CostEstimate(
            flops=int(microseconds * PEAK * WEIGH), bytes_accessed=0, transcendentals=0
        ),
    )(*args)


def normalize(tensor):
    average = jnp.mean(tensor, axis=-1, keepdims=True)
    centered = tensor - average
    inverse = lax.rsqrt(jnp.mean(centered * centered, axis=-1, keepdims=True) + EPSILON)
    return (centered * inverse, inverse)


def normalize_back(gradient, normed, inverse):
    first_term = jnp.mean(gradient, axis=-1, keepdims=True)
    second_term = jnp.mean(gradient * normed, axis=-1, keepdims=True)
    return inverse * (gradient - first_term - normed * second_term)


def column_sum(tensor):
    return jnp.sum(tensor, axis=0, keepdims=True)


def gelu_pair(pre):
    square = pre * pre
    bend = jnp.tanh(CURVE * (pre + CUBIC * pre * square))
    half = 0.5 + 0.5 * bend
    slope = half + (0.5 * CURVE) * pre * (1.0 - bend * bend) * (1.0 + 3.0 * CUBIC * square)
    return pre * half, slope


def halves(width):
    lane = lax.broadcasted_iota(jnp.int32, (1, LANES), 1)
    return [lane // width == i for i in range(LANES // width)]


def attend_body(
    tokens,
    condition,
    bucket,
    live,
    routes,
    table,
    ada_bias,
    router,
    ada_hbm,
    qkv_hbm,
    proj_hbm,
    packed,
    gates_out,
    modulation_out,
    conditioned_out,
    activated_out,
    attn_in_hbm,
    projected_hbm,
    log_hbm,
    attended_hbm,
    attn_out_hbm,
    middle_hbm,
    attn_in_out,
    projected_out,
    log_out,
    attended_out,
    attn_out_out,
    middle_out,
    ada,
    qkv,
    proj,
    sems,
):
    rows, width = tokens.shape
    experts = router.shape[0]
    leaving = []

    def leave(source, target):
        copy = pltpu.make_async_copy(source, target, sems.at[4 + len(leaving)])
        copy.start()
        leaving.append(copy)

    head = width // HEADS
    scaling = float(head) ** (-0.5)
    early = 2 * width
    copies = [
        pltpu.make_async_copy(ada_hbm.at[:, :early], ada.at[:, :early], sems.at[0]),
        pltpu.make_async_copy(qkv_hbm, qkv, sems.at[1]),
        pltpu.make_async_copy(ada_hbm.at[:, early:], ada.at[:, early:], sems.at[2]),
        pltpu.make_async_copy(proj_hbm, proj, sems.at[3]),
    ]
    for copy in copies:
        copy.start()

    named = lax.broadcasted_iota(jnp.int32, (table.shape[0], 1), 0) == bucket[0]
    conditioned = wide(condition[...]) + column_sum(jnp.where(named, wide(table[...]), 0.0))
    activated = to_low(conditioned * (1.0 / (1.0 + jnp.exp(-conditioned))))
    conditioned_out[...] = conditioned
    activated_out[...] = activated
    activated = jnp.broadcast_to(activated, (16, width))

    bias = wide(ada_bias[...])
    bias = jnp.concatenate([bias[i : i + 1] for i in range(bias.shape[0])], axis=1)
    inputs = wide(tokens[...])
    normed, _ = normalize(inputs)
    copies[0].wait()
    modulation_out[:, :early] = product(activated, ada[:, :early])[:1] + bias[:, :early]
    shift_attn = modulation_out[:, :width]
    scale_attn = modulation_out[:, width:early]
    attn_in = to_low(normed * (1.0 + scale_attn) + shift_attn)
    attn_in_out[...] = attn_in
    leave(attn_in_out, attn_in_hbm)
    copies[1].wait()
    projected_out[...] = to_low(product(attn_in, qkv[...]))
    leave(projected_out, projected_hbm)
    copies[2].wait()
    modulation_out[:, early:] = product(activated, ada[:, early:])[:1] + bias[:, early:]

    masks = halves(head)
    column = lax.broadcasted_iota(jnp.int32, (1, LANES), 1)
    logs = jnp.zeros((rows, LANES), full)
    for block in range(width // LANES):
        at = pl.ds(block * LANES, LANES)
        query = projected_out[:, at]
        key = projected_out[:, pl.ds(width + block * LANES, LANES)]
        value = projected_out[:, pl.ds(2 * width + block * LANES, LANES)]
        total = jnp.zeros((rows, LANES), full)
        for i, mask in enumerate(masks):
            scores = product_nt(jnp.where(mask, query, jnp.zeros_like(query)), key) * scaling
            top = jnp.max(scores, axis=-1, keepdims=True)
            raised = jnp.exp(scores - top)
            whole = jnp.sum(raised, axis=-1, keepdims=True)
            probs = to_low(raised / whole)
            logs = jnp.where(column == block * len(masks) + i, top + jnp.log(whole), logs)
            total = jnp.where(mask, product(probs, value), total)
        attended_out[:, at] = to_low(total)
    log_out[...] = logs
    leave(log_out, log_hbm)
    leave(attended_out, attended_hbm)

    copies[3].wait()
    attn_out = product(attended_out[...], proj[...])
    attn_out_out[...] = attn_out
    leave(attn_out_out, attn_out_hbm)
    piece = lambda i: modulation_out[:, pl.ds(i * width, width)]
    middle = inputs + piece(2) * attn_out
    middle_out[...] = middle
    leave(middle_out, middle_hbm)
    normed, _ = normalize(middle)
    mix_in = to_low(normed * (1.0 + piece(4)) + piece(3))
    packed[:rows, :] = mix_in

    logits = product_nt(router[...], mix_in)
    ids = lax.broadcasted_iota(jnp.int32, (experts, rows), 0)
    hot = (routes[:1] == ids) | (routes[1:2] == ids)
    top = jnp.max(jnp.where(hot, logits, -jnp.inf), axis=0, keepdims=True)
    turned = jnp.where(hot, jnp.exp(jnp.where(hot, logits, top) - top), 0.0)
    turned = turned / jnp.sum(turned, axis=0, keepdims=True)
    gates_out[...] = jnp.transpose(
        jnp.concatenate([turned, jnp.zeros((LANES - experts, rows), full)], axis=0)
    )
    gate_mix = piece(5) * wide(live[0])
    extra = packed.shape[0] - rows
    high, turned_high = to_low(gate_mix), to_low(turned)
    wall = jnp.zeros((experts, width - rows), full)
    packed[rows:, :] = to_low(
        jnp.concatenate(
            [
                jnp.concatenate([wide(turned_high), wall], axis=1),
                jnp.concatenate([turned - wide(turned_high), wall], axis=1),
                wide(high),
                gate_mix - wide(high),
                jnp.zeros((extra - 2 * experts - 2, width), full),
            ],
            axis=0,
        )
    )
    for copy in leaving:
        copy.wait()


class Mover:
    def __init__(self, sems):
        self.sems, self.count, self.open = sems, 0, []

    def start(self, source, target, keep=True):
        copy = pltpu.make_async_copy(source, target, self.sems.at[self.count])
        copy.start()
        self.count += 1
        if keep:
            self.open.append(copy)
        return copy

    def finish(self):
        for copy in self.open:
            copy.wait()


def wait(copies):
    while copies:
        copies.pop().wait()


def pick_body(members, shared_up, part_up):
    groups = lax.axis_size("grp")
    span = shared_up.shape[1] // groups
    part = span // members
    pick = spread_units(span, part, lax.axis_index("dp"), 0)
    for i in range(0, groups, 4):
        part_up[:, pl.ds(i * part, 4 * part)] = to_low(
            product(shared_up[:, pl.ds(i * span, 4 * span)], pick)
        )


def spread_units(span, part, member, dim):
    shape = (4 * span, 4 * part) if dim == 0 else (4 * part, 4 * span)
    whole = lax.broadcasted_iota(jnp.int32, shape, dim)
    own = lax.broadcasted_iota(jnp.int32, shape, 1 - dim)
    place = own + (own // part) * (span - part) + member * part
    return to_low(jnp.where(whole == place, 1.0, 0.0))


def parted(groups, bit, mine, i):
    return ((i >> bit) << (bit + 1)) + (mine << bit) + (i & ((1 << bit) - 1))


def bring_part_down(mover, members, shared_down, part_down):
    groups = lax.axis_size("grp")
    span = shared_down.shape[0] // groups
    part = span // members
    copies = []
    for i in range(groups):
        start = pl.multiple_of(i * span + lax.axis_index("dp") * part, 16)
        copies.append(
            mover.start(
                shared_down.at[pl.ds(start, part)], part_down.at[pl.ds(i * part, part)], False
            )
        )
    return copies


def bring_cut(mover, chunk, half, expert, own, lanes):
    groups = lax.axis_size("grp")
    span = expert.shape[2 if lanes else 1] // groups
    cut = span // CHUNKS
    side = lax.axis_index("grp") & 1
    copies = []
    for place in range(groups // 2):
        group = 2 * place + (side if half else 1 - side)
        start = pl.multiple_of(group * span + chunk * cut, LANES)
        to = pl.ds((half * groups // 2 + place) * cut, cut)
        if lanes:
            copies.append(mover.start(expert.at[0, :, pl.ds(start, cut)], own.at[:, to], False))
        else:
            copies.append(mover.start(expert.at[0, pl.ds(start, cut)], own.at[to], False))
    return copies


def feed_rows(mover, bit, rows, seen, grads, up, down, act, grad_pre, held, outs, waits, ordered):
    act_out, pre_out, put_up, put_down = outs
    wait_up, wait_down, wait_seen, wait_grads = waits
    groups = lax.axis_size("grp")
    mine = (lax.axis_index("grp") >> bit) & 1
    side = lax.axis_index("grp") & 1
    share = seen.shape[1] // groups
    step = held.shape[1]
    for number, start in enumerate(range(0, up.shape[1], step)):
        at = pl.ds(start, step)
        wait(wait_up[number])
        slopes = []
        for i in range(0, seen.shape[0], rows):
            wait(wait_seen[i // rows])
            raised, slope = gelu_pair(product(seen[pl.ds(i, rows), :], up[:, at]))
            act[pl.ds(i, rows), at] = to_low(raised)
            slopes.append(slope)
            if i == 0:
                wait(wait_down[number])
            wait(wait_grads[i // rows])
            slope = slopes.pop()
            grad_pre[pl.ds(i, rows), at] = to_low(
                slope * product_nt(grads[pl.ds(i, rows), :], down[at, :])
            )
        if act_out is not None:
            mover.start(act.at[:, at], act_out.at[:, at])
            mover.start(grad_pre.at[:, at], pre_out.at[:, at])
        held[...] = product_tn(seen[...], grad_pre[:, at])
        place = (1 - side if number == 0 else side) if ordered else number
        for kind, value in enumerate((1 - mine, mine)):
            rows_of = []
            for i in range(groups // 2):
                first = pl.multiple_of(parted(groups, bit, value, i) * share, 8)
                rows_of.append(to_low(held[pl.ds(first, share)]))
            put_up(kind, place, rows_of)
        put_down(number, at, to_low(product_tn(act[:, at], grads[...])))


def up_putter(mover, send, keep, send_out, keep_out, step):
    def put_up(kind, place, rows_of):
        target, out = ((send, send_out), (keep, keep_out))[kind]
        at = pl.ds(place * step, step)
        if not isinstance(place, int):
            at = pl.ds(pl.multiple_of(place * step, LANES), step)
        for i, value in enumerate(rows_of):
            target[i, :, at] = value
        mover.start(target.at[:, :, at], out.at[:, :, at])

    return put_up


def slab_putters(mover, slabs, slab_outs, step):
    groups, whole, _ = slabs[0].shape
    count = step // LANES

    def put_up(kind, place, rows_of):
        slab, out = slabs[kind], slab_outs[kind]
        share = rows_of[0].shape[0]
        first = pl.multiple_of(place * count * share, 16)
        for i, value in enumerate(rows_of):
            for j in range(count):
                at = pl.ds(pl.multiple_of(first + j * share, 16), share)
                slab[i, at, :] = value[:, j * LANES : (j + 1) * LANES]
        at = pl.ds(first, count * share)
        mover.start(slab.at[:, at], out.at[:, at])

    def put_down(number, at, value):
        slab, out = slabs[number], slab_outs[number]
        cut = value.shape[0] // groups
        first = whole - value.shape[1] // LANES * cut
        for i in range(groups):
            for j in range(value.shape[1] // LANES):
                slab[i, pl.ds(first + j * cut, cut), :] = value[
                    i * cut : (i + 1) * cut, j * LANES : (j + 1) * LANES
                ]
        at = pl.ds(first, whole - first)
        mover.start(slab.at[:, at], out.at[:, at])

    return put_up, put_down


def shared_body(bit, members, rows, experts, tiled, *refs):
    packs_hbm, cotangents_hbm = refs[:members], refs[members : 2 * members]
    (
        up_hbm,
        down_hbm,
        seen_out,
        routed_out,
        gate_out,
        up_keep_out,
        up_send_out,
        down_out,
        act_out,
        pre_out,
        packs,
        cotangents,
        up,
        down,
        seen,
        routed_grads,
        grads,
        gate_held,
        act,
        grad_pre,
        up_keep,
        up_send,
        grad_down,
        held,
        sems,
    ) = refs[2 * members :]
    mover = Mover(sems)
    width = seen.shape[1]
    me = lax.axis_index("dp")
    named = lax.broadcasted_iota(jnp.int32, (experts, 1), 0) == me
    pack_copies = [mover.start(p, packs.at[i], False) for i, p in enumerate(packs_hbm)]
    up_copy = mover.start(up_hbm, up, False)
    cotangent_copies = [mover.start(c, cotangents.at[i], False) for i, c in enumerate(cotangents_hbm)]
    if tiled:
        down_copies = bring_part_down(mover, members, down_hbm, down)
    else:
        down_copies = [mover.start(down_hbm, down, False)]
    for i in range(members):
        at = pl.ds(i * rows, rows)
        pack_copies[i].wait()
        seen[at, :] = packs[i, :rows, :]
        extra = wide(packs[i, rows:, :])
        gates = extra[:experts, :rows] + extra[experts : 2 * experts, :rows]
        gate = column_sum(jnp.where(named, gates, 0.0))
        gate = jnp.transpose(jnp.broadcast_to(gate, (LANES, rows)))
        gate_held[at, :] = gate
        gate_mix = extra[2 * experts : 2 * experts + 1] + extra[2 * experts + 1 : 2 * experts + 2]
        cotangent_copies[i].wait()
        mixture_grads = to_low(gate_mix * wide(cotangents[i]))
        grads[at, :] = mixture_grads
        routed_grads[at, :] = to_low(gate[:, :1] * wide(mixture_grads))
    mover.start(seen, seen_out)
    mover.start(routed_grads, routed_out)
    mover.start(gate_held, gate_out)

    def put_down(number, at, value):
        grad_down[at, :] = value
        mover.start(grad_down.at[at], down_out.at[at])

    blocks = range(seen.shape[0] // rows)
    waits = ([[up_copy], []], [down_copies, []], [[] for _ in blocks], [[] for _ in blocks])
    put_up = up_putter(mover, up_send, up_keep, up_send_out, up_keep_out, held.shape[1])
    outs = (act_out, pre_out, put_up, put_down)
    feed_rows(mover, bit, rows, seen, grads, up, down, act, grad_pre, held, outs, waits, False)
    mover.finish()


def bring_rows(mover, rows, source, target):
    return [
        [mover.start(source.at[pl.ds(i, rows)], target.at[pl.ds(i, rows)], False)]
        for i in range(0, source.shape[0], rows)
    ]


def bring_cut_all(mover, chunk, tiled, up_hbm, down_hbm, up, down, seen, grads, rows):
    if tiled:
        wait_up = [bring_cut(mover, chunk, 0, up_hbm, up, True)]
        wait_seen = bring_rows(mover, rows, *seen)
        wait_down = [bring_cut(mover, chunk, 0, down_hbm, down, False)]
        wait_grads = bring_rows(mover, rows, *grads)
        wait_up.append(bring_cut(mover, chunk, 1, up_hbm, up, True))
        wait_down.append(bring_cut(mover, chunk, 1, down_hbm, down, False))
    else:
        wait_up = [[mover.start(up_hbm, up, False)], []]
        wait_seen = bring_rows(mover, rows, *seen)
        wait_down = [[mover.start(down_hbm, down, False)], []]
        wait_grads = bring_rows(mover, rows, *grads)
    return wait_up, wait_down, wait_seen, wait_grads


def routed_body(bit, chunk, rows, tiled, one, *refs):
    seen_hbm, grads_hbm, up_hbm, down_hbm = refs[:4]
    many = 2 if one else 4
    grad_outs, (act_out, pre_out) = refs[4 : 4 + many], refs[4 + many : 6 + many]
    seen, grads, up, down, act, grad_pre, held = refs[6 + many : 13 + many]
    kept, sems = refs[13 + many : -1], refs[-1]
    mover = Mover(sems)
    waits = bring_cut_all(
        mover, chunk, tiled, up_hbm, down_hbm, up, down, (seen_hbm, seen), (grads_hbm, grads), rows
    )
    if one:
        put_up, put_down = slab_putters(mover, kept, grad_outs, held.shape[1])
    else:
        put_up = up_putter(mover, *kept[:2], *grad_outs[:2], held.shape[1])

        def put_down(number, at, value):
            target, out = kept[2 + number], grad_outs[2 + number]
            target[...] = value.reshape(target.shape)
            mover.start(target, out)

    outs = (act_out, pre_out, put_up, put_down)
    feed_rows(mover, bit, rows, seen, grads, up, down, act, grad_pre, held, outs, waits, True)
    mover.finish()


def result_body(bit, members, rows, block, experts, tiled, *refs):
    parts = 1 + CHUNKS
    acts_hbm, pres_hbm = refs[:CHUNKS], refs[CHUNKS : 2 * CHUNKS]
    given = 4 if tiled else 2 * parts
    weights_hbm = refs[2 * CHUNKS : 2 * CHUNKS + given]
    rest = refs[2 * CHUNKS + given :]
    seen_hbm, grads_hbm, gate_hbm = rest[:3]
    up_keep_out, up_send_out, down_keep_out, down_send_out = rest[3:7]
    back_keep_out, back_send_out, mixed_keep_out, mixed_send_out = rest[7:11]
    scratch, sems = rest[11:-1], rest[-1]
    acts, pres, ups, downs = [scratch[i * parts : (i + 1) * parts] for i in range(4)]
    seen, grads, gate, back, up_keep, up_send, down_keep, down_send, held = scratch[4 * parts :]
    mover = Mover(sems)
    width = grads.shape[1]
    me = lax.axis_index("dp")
    column = lax.broadcasted_iota(jnp.int32, (1, LANES), 1)
    last = CHUNKS - 1
    if tiled:
        up_hbm, down_hbm = weights_hbm[2:]
    else:
        up_hbm, down_hbm = weights_hbm[parts - 1], weights_hbm[2 * parts - 1]
    waits = bring_cut_all(
        mover,
        last,
        tiled,
        up_hbm,
        down_hbm,
        ups[-1],
        downs[-1],
        (seen_hbm, seen),
        (grads_hbm, grads),
        block,
    )

    def bring_weights(kind, targets):
        if not tiled:
            sources = weights_hbm[kind * parts : (kind + 1) * parts]
            return [[mover.start(a, b, False)] for a, b in zip(sources[:-1], targets)]
        part, expert = weights_hbm[kind], weights_hbm[2 + kind]
        if kind:
            found = [bring_part_down(mover, members, part, targets[0])]
        else:
            found = [[mover.start(part, targets[0], False)]]
        for c in range(last):
            found.append(
                bring_cut(mover, c, 0, expert, targets[1 + c], kind == 0)
                + bring_cut(mover, c, 1, expert, targets[1 + c], kind == 0)
            )
        return found

    more = [mover.start(a, b, False) for a, b in zip(acts_hbm, acts)]
    for found in bring_weights(1, downs):
        more += found
    more.append(mover.start(gate_hbm, gate, False))
    later = [mover.start(a, b, False) for a, b in zip(pres_hbm, pres)]
    for found in bring_weights(0, ups):
        later += found

    def put_down(number, at, value):
        target, out = ((down_send, down_send_out), (down_keep, down_keep_out))[number]
        target[...] = value.reshape(target.shape)
        mover.start(target, out)

    put_up = up_putter(mover, up_send, up_keep, up_send_out, up_keep_out, held.shape[1])
    outs = (None, None, put_up, put_down)
    feed_rows(
        mover,
        bit,
        block,
        seen,
        grads,
        ups[-1],
        downs[-1],
        acts[-1],
        pres[-1],
        held,
        outs,
        waits,
        True,
    )
    wait(more)
    mixed = seen
    for i in [*range(1, members, 2), *range(0, members, 2)]:
        at = pl.ds(i * rows, rows)
        to = pl.ds((i // 2) * rows, rows)
        routed = sum(product(a[at, :], d[...]) for a, d in zip(acts[1:], downs[1:]))
        routed = wide(to_low(routed))
        mixed[at, :] = to_low(product(acts[0][at, :], downs[0][...]) + gate[at, :1] * routed)
        mover.start(mixed.at[at], (mixed_send_out if i % 2 else mixed_keep_out).at[to])
        weighed = jnp.sum(wide(grads[at, :]) * routed, axis=1, keepdims=True)
        high = wide(to_low(weighed))
        back[at, width:] = to_low(
            jnp.where(column == me, high, 0.0)
            + jnp.where(column == experts + me, weighed - high, 0.0)
        )
        wait(later)
        back[at, :width] = to_low(sum(product_nt(p[at, :], u[...]) for p, u in zip(pres, ups)))
        mover.start(back.at[at], (back_send_out if i % 2 else back_keep_out).at[to])
    mover.finish()


def middle_back_body(
    kept,
    got,
    packed,
    middle,
    modulation,
    gates,
    cotangent,
    live,
    attn_out,
    attended,
    proj,
    router,
    proj_keep,
    proj_send,
    grad_attended,
    grad_middle_out,
    grad_pieces,
    held,
):
    rows, width = cotangent.shape
    experts = router.shape[0]
    piece = lambda i: modulation[:, pl.ds(i * width, width)]
    back = wide(kept[:, width:]) + wide(got[:, width:])
    weighed = back[:, :experts] + back[:, experts : 2 * experts]
    mine = gates[:, :experts]
    grad_logits = to_low(weighed - mine * jnp.sum(weighed, axis=1, keepdims=True))
    mix_in = packed[:rows, :]
    grad_mix_in = wide(kept[:, :width]) + wide(got[:, :width])
    grad_mix_in = grad_mix_in + product(grad_logits, router[...])
    normed, inverse = normalize(middle[...])
    grad_result = wide(cotangent[...]) * wide(live[0])
    grad_middle = grad_result + normalize_back(grad_mix_in * (1.0 + piece(4)), normed, inverse)
    grad_middle_out[...] = grad_middle
    grad_attn_out = to_low(piece(2) * grad_middle)
    held[:, width:] = jnp.zeros((width, LANES), full)
    held[:, width : width + experts] = product_tn(mix_in, grad_logits)
    held[:, :width] = product_tn(attended[...], grad_attn_out)
    part_rows(held, proj_keep, proj_send, slice(None))
    grad_attended[...] = to_low(product_nt(grad_attn_out, proj[...]))
    grad_pieces[0:1] = column_sum(grad_middle * attn_out[...])
    grad_pieces[1:2] = column_sum(grad_mix_in)
    grad_pieces[2:3] = column_sum(grad_mix_in * normed)


def part_rows(held, keep, send, at):
    groups, members = lax.axis_size("grp"), lax.axis_size("dp")
    share = held.shape[0] // (groups * members)
    if len(keep.shape) == 2:
        keep[:, at] = to_low(held[...])
        return
    mine = lax.axis_index("dp") & 1
    for target, value in ((send, 1 - mine), (keep, mine)):
        for i in range(members // 2):
            for g in range(groups):
                first = pl.multiple_of((g * members + 2 * i + value) * share, 8)
                target[i * groups + g, :, at] = to_low(held[pl.ds(first, share)])


def attend_back_body(
    grad_attended,
    projected,
    logs,
    attn_in,
    tokens,
    grad_middle,
    modulation,
    qkv_hbm,
    grad_tokens,
    qkv_keep_out,
    qkv_send_out,
    grad_pieces,
    grad_projected,
    held,
    qkv,
    qkv_keep,
    qkv_send,
    sems,
):
    rows, width = tokens.shape
    head = width // HEADS
    scaling = float(head) ** (-0.5)
    mover = Mover(sems)
    qkv_copy = mover.start(qkv_hbm, qkv, False)
    masks = halves(head)
    column = lax.broadcasted_iota(jnp.int32, (1, LANES), 1)
    for block in range(width // LANES):
        parts = [pl.ds(i * width + block * LANES, LANES) for i in range(3)]
        query, key, value = [projected[:, at] for at in parts]
        grads = grad_attended[:, parts[0]]
        grad_query, grad_key, grad_value = [jnp.zeros((rows, LANES), full)] * 3
        for i, mask in enumerate(masks):
            zero = jnp.zeros_like(query)
            scores = product_nt(jnp.where(mask, query, zero), key) * scaling
            log = jnp.sum(
                jnp.where(column == block * len(masks) + i, logs[...], 0.0), axis=1, keepdims=True
            )
            probs = jnp.exp(scores - log)
            grad_probs = product_nt(jnp.where(mask, grads, zero), value)
            grad_value = jnp.where(mask, product_tn(to_low(probs), grads), grad_value)
            drift = jnp.sum(probs * grad_probs, axis=-1, keepdims=True)
            grad_scores = to_low(probs * (grad_probs - drift))
            grad_query = jnp.where(mask, product(grad_scores, key), grad_query)
            grad_key = jnp.where(mask, product_tn(grad_scores, query), grad_key)
        for at, grad in zip(parts, (grad_query * scaling, grad_key * scaling, grad_value)):
            grad_projected[:, at] = to_low(grad)
    for i in range(3):
        at = pl.ds(i * width, width)
        held[...] = product_tn(attn_in[...], grad_projected[:, at])
        part_rows(held, qkv_keep, qkv_send, at)
    mover.start(qkv_keep, qkv_keep_out)
    if len(qkv_keep.shape) > 2:
        mover.start(qkv_send, qkv_send_out)
    qkv_copy.wait()
    grad_attn_in = product_nt(grad_projected[...], qkv[...])
    normed, inverse = normalize(wide(tokens[...]))
    scale_attn = modulation[:, pl.ds(width, width)]
    grad_pieces[0:1] = column_sum(grad_attn_in)
    grad_pieces[1:2] = column_sum(grad_attn_in * normed)
    grad_tokens[...] = grad_middle[...] + normalize_back(
        grad_attn_in * (1.0 + scale_attn), normed, inverse
    )
    mover.finish()


def condition_body(
    kept,
    got,
    middle,
    modulation,
    cotangent,
    live,
    attn_pieces,
    mix_pieces,
    conditioned,
    activated,
    bucket,
    ada_hbm,
    mixed_out,
    factors,
    grad_condition,
    table_part,
    ada,
    sem,
):
    rows, width = cotangent.shape
    copy = pltpu.make_async_copy(ada_hbm, ada, sem)
    copy.start()
    alive = wide(live[0])
    gate_mix = modulation[:, pl.ds(5 * width, width)]
    mixture = wide(kept[...]) + wide(got[...])
    mixed_out[...] = to_low((middle[...] + gate_mix * mixture) * alive)
    grad_gate_mix = column_sum(wide(cotangent[...]) * alive * mixture)
    grads = [
        attn_pieces[0:1],
        attn_pieces[1:2],
        mix_pieces[0:1],
        mix_pieces[1:2],
        mix_pieces[2:3],
        grad_gate_mix,
    ]
    factors[...] = to_low(
        jnp.concatenate(grads + [wide(activated[...]), jnp.zeros((1, width), full)], axis=0)
    )
    copy.wait()
    pulled = jnp.zeros((1, width), full)
    for i, grad in enumerate(grads):
        spread = jnp.broadcast_to(to_low(grad), (16, width))
        pulled = pulled + product_nt(spread, ada[:, pl.ds(i * width, width)])[:1]
    drive = conditioned[...]
    gate = 1.0 / (1.0 + jnp.exp(-drive))
    grad = pulled * gate * (1.0 + drive * (1.0 - gate))
    grad_condition[...] = grad
    share = table_part.shape[0]
    row = lax.broadcasted_iota(jnp.int32, (share, 1), 0) + lax.axis_index("grp") * share
    table_part[...] = jnp.where(row == bucket[0], grad, 0.0)


def split_body(mine, keep_a, got_a, keep_b, got_b, keep_out, send_out):
    keep_out[...] = to_low(wide(keep_a[...]) + wide(got_a[...]))
    send_out[...] = to_low(wide(keep_b[...]) + wide(got_b[...]))


def split_sum(axis, bit, place, keep, got):
    mine = ((lax.axis_index(axis) >> bit) & 1).reshape(1)
    count, *block = keep.shape
    spec = lambda other: pl.BlockSpec(
        (1, *block), lambda i, mine: (parted(count, place, mine[0] ^ other, i), 0, 0)
    )
    out = pl.BlockSpec((1, *block), lambda i, mine: (i, 0, 0))
    return pl.pallas_call(
        split_body,
        grid_spec=pltpu.PrefetchScalarGridSpec(
            num_scalar_prefetch=1,
            grid=(count // 2,),
            in_specs=[spec(0), spec(0), spec(1), spec(1)],
            out_specs=[out, out],
        ),
        out_shape=[like((count // 2, *block), low)] * 2,
        compiler_params=pltpu.CompilerParams(vmem_limit_bytes=16 << 20),
        cost_estimate=pl.CostEstimate(flops=int(1.5 * PEAK * WEIGH), bytes_accessed=0, transcendentals=0),
    )(mine, keep, got, keep, got)


def even_odd_body(keep_a, got_a, keep_b, got_b, keep_out, send_out):
    keep_out[...] = to_low(wide(keep_a[...]) + wide(got_a[...]))
    send_out[...] = to_low(wide(keep_b[...]) + wide(got_b[...]))


def even_odd_sum(keep, got):
    count, *block = keep.shape
    spec = lambda other: pl.BlockSpec((1, *block), lambda i: (2 * i + other, 0, 0))
    out = pl.BlockSpec((1, *block), lambda i: (i, 0, 0))
    return pl.pallas_call(
        even_odd_body,
        grid=(count // 2,),
        in_specs=[spec(0), spec(0), spec(1), spec(1)],
        out_specs=[out, out],
        out_shape=[like((count // 2, *block), low)] * 2,
        compiler_params=pltpu.CompilerParams(vmem_limit_bytes=16 << 20),
        cost_estimate=pl.CostEstimate(flops=int(1.5 * PEAK * WEIGH), bytes_accessed=0, transcendentals=0),
    )(keep, got, keep, got)


def join_body(mine, *refs):
    keep_out, send_out = refs[-2:]
    width = refs[0].shape[-1]
    for out, terms in ((keep_out, refs[0:4]), (send_out, refs[4:8])):
        out[:, :, :width] = to_low(wide(terms[0][...]) + wide(terms[1][...]))
        out[:, :, width:] = to_low(wide(terms[2][...]) + wide(terms[3][...]))


def join_sum(axis, bit, place, first, second):
    mine = ((lax.axis_index(axis) >> bit) & 1).reshape(1)
    count, rows, width = first[0].shape
    columns = width + second[0].shape[2]

    def spec(columns, other):
        return pl.BlockSpec(
            (1, rows, columns), lambda i, mine: (parted(count, place, mine[0] ^ other, i), 0, 0)
        )

    out = pl.BlockSpec((1, rows, columns), lambda i, mine: (i, 0, 0))
    return pl.pallas_call(
        join_body,
        grid_spec=pltpu.PrefetchScalarGridSpec(
            num_scalar_prefetch=1,
            grid=(count // 2,),
            in_specs=[
                spec(c, other) for other in (0, 1) for c in (width, width, columns - width, columns - width)
            ],
            out_specs=[out, out],
        ),
        out_shape=[like((count // 2, rows, columns), low)] * 2,
        compiler_params=pltpu.CompilerParams(vmem_limit_bytes=16 << 20),
        cost_estimate=pl.CostEstimate(flops=int(1.5 * PEAK * WEIGH), bytes_accessed=0, transcendentals=0),
    )(mine, *first, *second, *first, *second)


def stack_body(*refs):
    *pairs, total = refs
    start = 0
    for i in range(0, len(pairs), 2):
        rows = pl.ds(start, pairs[i].shape[0])
        total[rows, :] = to_low(wide(pairs[i][...]) + wide(pairs[i + 1][...]))
        start += pairs[i].shape[0]


def sum_body(keep, got, total):
    total[...] = to_low(wide(keep[...]) + wide(got[...]))


def own_up_body(*refs):
    *pairs, out = refs
    share = out.shape[0]
    groups = lax.axis_size("grp")
    for c in range(CHUNKS):
        total = wide(pairs[2 * c][...]) + wide(pairs[2 * c + 1][...])
        for i in range(groups):
            place = (i & 1) * (groups // 2) + (i >> 1)
            if c == 0:
                value = total[place * share : (place + 1) * share]
            else:
                value = total[:, place * LANES : (place + 1) * LANES]
            out[:, pl.ds((i * CHUNKS + c) * LANES, LANES)] = value


def own_down_body(*refs):
    *pairs, out = refs
    width = out.shape[1]
    cut = pairs[-1].shape[0]
    for c in range(CHUNKS):
        rows = pl.ds(c * cut, cut)
        if c > 0:
            out[rows] = wide(pairs[2 * c][...]) + wide(pairs[2 * c + 1][...])
            continue
        first = pairs[0].shape[0] - width // LANES * cut
        for j in range(width // LANES):
            at = pl.ds(first + j * cut, cut)
            out[rows, pl.ds(j * LANES, LANES)] = wide(pairs[0][at, :]) + wide(pairs[1][at, :])


def shared_end_body(members, *refs):
    blocks, up_out, down_out = refs[:members], refs[-2], refs[-1]
    share = up_out.shape[0]
    me = lax.axis_index("dp")
    groups = lax.axis_size("grp")
    span = up_out.shape[1] // groups
    part = span // members
    for i in range(0, groups, 4):
        total = 0.0
        for far in range(members):
            pick = spread_units(span, part, me ^ far, 1)
            total = total + product(blocks[far][:share, pl.ds(i * part, 4 * part)], pick)
        up_out[:, pl.ds(i * span, 4 * span)] = total
    for far in range(members):
        start = pl.multiple_of((me ^ far) * part, 8)
        down_out[pl.ds(start, part)] = wide(blocks[far][share:, :])


def rows_end_body(members, *refs):
    blocks, outs = refs[:members], refs[members:]
    me = lax.axis_index("dp")
    share = blocks[0].shape[0]
    for far in range(members):
        start = pl.multiple_of((me ^ far) * share, 8)
        column = 0
        for out in outs:
            out[pl.ds(start, share), :] = wide(blocks[far][:, column : column + out.shape[1]])
            column += out.shape[1]


def bits_of(axis):
    return lax.axis_size(axis).bit_length() - 1


def tie(tensor, *before):
    return lax.optimization_barrier((tensor, *before))[0]


DEPTH_X, DEPTH_Y, DEPTH_Z = 1, 2, 3


class Links:
    depth = {"y": DEPTH_Y, "z": DEPTH_Z, "x": DEPTH_X}

    def __init__(self):
        self.past = {}

    def swap(self, tensor, axis, bit):
        pairs = [(i, i ^ (1 << bit)) for i in range(lax.axis_size(axis))]
        if axis == "dp":
            name = "x" if bit else None
        else:
            name = "y" if bit < bits_of("grp") // 2 else "z"
        past = self.past.setdefault(name, [])
        depth = self.depth.get(name, 0)
        if 0 < depth <= len(past):
            tensor = tie(tensor, past[-depth])
        past.append(lax.ppermute(tensor, axis, pairs))
        return past[-1]


def over_call(body, outs, args):
    return kernel_call(body, outs, [VMEM] * len(args), args, (), 16, 1.5)


class Order:
    def __init__(self):
        self.tokens = ()

    def after(self, tensor):
        return tie(tensor, *self.tokens) if self.tokens else tensor

    def done(self, *tokens):
        self.tokens = tokens

    def also(self, token):
        self.tokens += (token,)


class Sum:
    def __init__(self, run, links, tiled, keep, send, order, left):
        self.run, self.links, self.tiled, self.keep, self.send = run, links, tiled, keep, send
        self.order = list(order)
        self.left = [bit for bit in left if bit != order[0]]
        self.folded = True

    def move(self):
        self.got = self.links.swap(self.send, *self.order.pop(0))
        self.folded = False

    def fold(self):
        if self.folded:
            return
        self.folded = True
        bit = self.order[0]
        place = len(self.left) - 1 - self.left.index(bit)
        self.left.remove(bit)
        if self.tiled:
            self.keep, self.send = split_sum(*bit, place, self.run.after(self.keep), self.got)
        else:
            total = to_low(wide(self.keep) + wide(self.got))
            self.keep, self.send = split(total, *bit, place)
        self.run.done(self.send)

    def step(self):
        self.fold()
        self.move()

    def last(self):
        while self.order:
            self.step()

    def terms(self):
        return self.keep[0], self.got[0]


def split(tensor, axis, bit, place):
    mine = (lax.axis_index(axis) >> bit) & 1
    parts = tensor.reshape((-1, 2, 1 << place) + tensor.shape[1:])
    halves_of = [
        lax.dynamic_index_in_dim(parts, i, 1, keepdims=False).reshape((-1,) + tensor.shape[1:])
        for i in (mine, 1 - mine)
    ]
    return halves_of


def gather_near(links, tensor, axis, before=()):
    blocks = {0: tensor}
    for bit in range(bits_of(axis) - 1, -1, -1):
        for far in list(blocks):
            block = tie(blocks[far], *before) if far and not bit and before else blocks[far]
            blocks[far ^ (1 << bit)] = links.swap(block, axis, bit)
    return [blocks[i] for i in range(len(blocks))]


def in_order(blocks, axis):
    me = lax.axis_index(axis)
    blocks = jnp.stack(blocks)
    return jnp.stack(
        [lax.dynamic_index_in_dim(blocks, i ^ me, 0, keepdims=False) for i in range(blocks.shape[0])]
    )


def per_device(
    tokens,
    condition,
    bucket,
    live_mask,
    routes,
    bucket_table,
    ada_weight,
    ada_bias,
    qkv_weight,
    proj_weight,
    shared_up,
    shared_down,
    router_weight,
    expert_up,
    expert_down,
    cotangent,
):
    tokens, routes, cotangent = tokens[0], routes[0], cotangent[0]
    rows, width = tokens.shape
    members, groups = lax.axis_size("dp"), lax.axis_size("grp")
    me, group = lax.axis_index("dp"), lax.axis_index("grp")
    experts = expert_up.shape[0] * members
    hidden = shared_up.shape[1]
    table_rows = bucket_table.shape[0]
    seen_rows = members * rows
    y_first = tuple(range(bits_of("grp")))
    z_first = y_first[1:] + y_first[:1]
    y_first, z_first = [tuple(("grp", bit) for bit in bits) for bits in (y_first, z_first)]
    all_left = tuple(("dp", bit) for bit in range(bits_of("dp") - 1, 0, -1)) + y_first[::-1]
    all_order = tuple(("dp", bit) for bit in range(bits_of("dp"))) + y_first

    links, run = Links(), Order()
    cotangents = gather_near(links, cotangent, "dp")

    extra = -(-(2 * experts + 2) // 16) * 16
    saved = [
        like((rows, width), low),
        like((rows, 3 * width), low),
        like((rows, LANES), full),
        like((rows, width), low),
        like((rows, width), full),
        like((rows, width), full),
    ]
    (
        packed,
        gates,
        modulation,
        conditioned,
        activated,
        attn_in,
        projected,
        logs,
        attended,
        attn_out,
        middle,
    ) = kernel_call(
        attend_body,
        [
            like((rows + extra, width), low),
            like((rows, LANES), full),
            like((1, 6 * width), full),
            like((1, width), full),
            like((1, width), low),
        ]
        + saved,
        [VMEM, VMEM, SMEM, SMEM] + [VMEM] * 4 + [HBM] * 3,
        (
            tokens,
            condition,
            bucket,
            live_mask,
            routes.T,
            bucket_table,
            ada_bias.reshape(-1, LANES),
            router_weight.T,
            ada_weight,
            qkv_weight,
            proj_weight,
        ),
        [pltpu.VMEM(out.shape, out.dtype) for out in saved]
        + [
            pltpu.VMEM(ada_weight.shape, low),
            pltpu.VMEM(qkv_weight.shape, low),
            pltpu.VMEM(proj_weight.shape, low),
            pltpu.SemaphoreType.DMA((4 + len(saved),)),
        ],
        MOST,
        10,
        [VMEM] * 5 + [HBM] * len(saved),
    )


    part = hidden // (groups * members)
    cut = hidden // (groups * CHUNKS)
    tiled = cut % LANES == 0
    if tiled:
        run.done(gates)
        [part_up] = kernel_call(
            functools.partial(pick_body, members),
            [like((width, groups * part), low)],
            [VMEM],
            (run.after(shared_up),),
            (),
            20,
            4,
        )
        part_down = shared_down
    else:
        part_up = lax.dynamic_index_in_dim(
            shared_up.reshape(width, groups, members, part), me, 2, keepdims=False
        ).reshape(width, groups * part)
        part_down = lax.dynamic_index_in_dim(
            shared_down.reshape(groups, members, part, width), me, 1, keepdims=False
        ).reshape(groups * part, width)
        sides = lambda tensor, place: jnp.concatenate(
            [
                lax.dynamic_index_in_dim(tensor, side, place + 1, keepdims=False)
                for side in (1 - group % 2, group % 2)
            ],
            axis=place,
        )
        own_ups = sides(expert_up[0].reshape(width, groups // 2, 2, CHUNKS, cut), 1)
        own_downs = sides(expert_down[0].reshape(groups // 2, 2, CHUNKS, cut, width), 0)
        ups = [own_ups[:, :, i].reshape(width, groups * cut) for i in range(CHUNKS)]
        downs = [own_downs[:, i].reshape(groups * cut, width) for i in range(CHUNKS)]
    share = width // groups
    packs = gather_near(links, packed, "dp", (part_up,))
    def sum_of(keep, send, order):
        return Sum(run, links, tiled, keep, send, order, y_first[::-1])

    def room(columns, step):
        return [
            pltpu.VMEM((seen_rows, columns), low),
            pltpu.VMEM((seen_rows, columns), low),
            pltpu.VMEM((groups // 2, share, columns), low),
            pltpu.VMEM((groups // 2, share, columns), low),
        ]

    ups_first = [z_first, y_first, z_first, y_first]
    columns = groups * part
    halved = [like((groups // 2, share, columns), low)] * 2
    patches = pltpu.VMEM((seen_rows, width), low)
    seen, routed_grads, gate, up_keep, up_send, grad_part_down, *kept = kernel_call(
        functools.partial(shared_body, ups_first[0][0][1], members, rows, experts, tiled),
        [
            like((seen_rows, width), low),
            like((seen_rows, width), low),
            like((seen_rows, LANES), full),
        ]
        + halved
        + [like((columns, width), low)]
        + [like((seen_rows, columns), low)] * 2,
        [HBM] * (2 * members + 2),
        (*packs, *cotangents, part_up, part_down),
        [
            pltpu.VMEM((members, rows + extra, width), low),
            pltpu.VMEM((members, rows, width), low),
            pltpu.VMEM((width, columns), low),
            pltpu.VMEM((columns, width), low),
            patches,
            patches,
            patches,
            pltpu.VMEM((seen_rows, LANES), full),
        ]
        + room(columns, 384)
        + [
            pltpu.VMEM((columns, width), low),
            pltpu.VMEM((width, 384), full),
            pltpu.SemaphoreType.DMA((64,)),
        ],
        MOST,
        9,
        [HBM] * 8,
    )
    acts, pres = [kept[0]], [kept[1]]
    run.done(gate)
    sums = {"su": sum_of(up_keep, up_send, ups_first[0])}
    sums["su"].move()
    grad_part_down = grad_part_down.reshape(groups, part, width)
    sums["sd"] = sum_of(*split(grad_part_down, "grp", 0, 0), y_first)
    sums["sd"].move()
    columns = groups * cut
    halved = [like((groups // 2, share, columns), low)] * 2
    halved += [like((groups // 2, cut, width), low)] * 2
    block = seen_rows if members == 4 else rows
    slab = (groups // 2, share * columns // LANES + cut * width // LANES, LANES)
    for i in range(CHUNKS - 1):
        one = tiled and i == 0
        if i == 1:
            sums["su"].step()
            sums["sd"].step()
            if tiled:
                sums["e0"].move()
            else:
                sums["u0"].move()
                sums["d0"].move()
        *outs, act, grad_pre = kernel_call(
            functools.partial(routed_body, ups_first[1 + i][0][1], i, block, tiled, one),
            ([like(slab, low)] * 2 if one else halved) + [like((seen_rows, columns), low)] * 2,
            [HBM] * 4,
            (
                run.after(seen),
                routed_grads,
                *((expert_up, expert_down) if tiled else (ups[i], downs[i])),
            ),
            [
                patches,
                patches,
                pltpu.VMEM((width, columns), low),
                pltpu.VMEM((columns, width), low),
                pltpu.VMEM((seen_rows, columns), low),
                pltpu.VMEM((seen_rows, columns), low),
                pltpu.VMEM((width, columns // 2), full),
            ]
            + [pltpu.VMEM(out.shape, low) for out in ([like(slab, low)] * 2 if one else halved)]
            + [pltpu.SemaphoreType.DMA((64,))],
            MOST,
            10,
            [HBM] * (4 if one else 6),
        )
        if one:
            sums["e0"] = sum_of(outs[1], outs[0], y_first)
        else:
            sums["u%d" % i] = sum_of(outs[1], outs[0], ups_first[1 + i])
            sums["d%d" % i] = sum_of(outs[3], outs[2], y_first)
        acts.append(act)
        pres.append(grad_pre)
        run.done(grad_pre)
    sums["sd"].step()
    sums["su"].fold()
    sums["u1"].move()
    sums["d1"].move()
    (
        up_keep,
        up_send,
        down_keep,
        down_send,
        back_keep,
        back_send,
        mixed_keep,
        mixed_send,
    ) = kernel_call(
        functools.partial(
            result_body, ups_first[-1][0][1], members, rows, block, experts, tiled
        ),
        halved
        + [like((seen_rows // 2, width + LANES), low)] * 2
        + [like((seen_rows // 2, width), low)] * 2,
        [HBM] * (2 * CHUNKS + (4 if tiled else 2 * (1 + CHUNKS)) + 3),
        (
            *acts,
            *pres,
            *(
                (part_up, part_down, expert_up, expert_down)
                if tiled
                else (part_up, *ups, part_down, *downs)
            ),
            run.after(seen),
            routed_grads,
            gate,
        ),
        [pltpu.VMEM(a.shape, low) for a in acts]
        + [pltpu.VMEM((seen_rows, columns), low)]
        + [pltpu.VMEM(a.shape, low) for a in pres]
        + [pltpu.VMEM((seen_rows, columns), low)]
        + [pltpu.VMEM((width, groups * part), low)]
        + [pltpu.VMEM((width, columns), low)] * CHUNKS
        + [pltpu.VMEM((groups * part, width), low)]
        + [pltpu.VMEM((columns, width), low)] * CHUNKS
        + [
            patches,
            patches,
            pltpu.VMEM((seen_rows, LANES), full),
            pltpu.VMEM((seen_rows, width + LANES), low),
        ]
        + room(columns, 0)[2:]
        + [
            pltpu.VMEM((groups // 2, cut, width), low),
            pltpu.VMEM((groups // 2, cut, width), low),
            pltpu.VMEM((width, columns // 2), full),
            pltpu.SemaphoreType.DMA((160,)),
        ],
        MOST if members == 4 else 61,
        24,
        [HBM] * 8,
    )
    sums["u2"] = sum_of(up_keep, up_send, ups_first[-1])
    sums["d2"] = sum_of(down_keep, down_send, y_first)
    run.done(back_send)

    def fold_near(keep, got):
        keep, got = [t.reshape(-1, rows, t.shape[-1]) for t in (keep, got)]
        keep, send = even_odd_sum(run.after(keep), got)
        run.done(send)
        return keep, send

    for name in ("sd", "u1", "d1"):
        run.also(sums[name].got)
    if tiled:
        sums["e0"].fold()
    back_keep, back_send, mixed_keep, mixed_send = [
        run.after(t) for t in (back_keep, back_send, mixed_keep, mixed_send)
    ]
    for name in ("u2", "d2"):
        sums[name].keep, sums[name].send = [
            run.after(t) for t in (sums[name].keep, sums[name].send)
        ]
    back_got = links.swap(back_send, "dp", 0)
    if tiled:
        sums["e0"].move()
    for bit in range(1, bits_of("dp")):
        back_keep, back_send = fold_near(back_keep, back_got)
        back_got = links.swap(back_send, "dp", bit)
    sums["u1"].step()
    sums["u2"].move()
    mixed_got = links.swap(mixed_send, "dp", 0)
    for bit in range(1, bits_of("dp")):
        mixed_keep, mixed_send = fold_near(mixed_keep, mixed_got)
        mixed_got = links.swap(mixed_send, "dp", bit)
    sums["d1"].fold()

    def row_parts(columns):
        if tiled:
            return [like((members // 2 * groups, share // members, columns), low)] * 2
        return [like((width, columns), low)] * 2

    proj_keep, proj_send, grad_attended, grad_middle, mix_pieces = kernel_call(
        middle_back_body,
        row_parts(width + LANES)
        + [
            like((rows, width), low),
            like((rows, width), full),
            like((8, width), full),
        ],
        [VMEM] * 7 + [SMEM] + [VMEM] * 4,
        (
            run.after(back_keep[0]),
            back_got[0],
            packed,
            middle,
            modulation,
            gates,
            cotangent,
            live_mask,
            attn_out,
            attended,
            proj_weight,
            router_weight.T,
        ),
        [pltpu.VMEM((width, width + LANES), full)],
        K3A,
        4,
    )
    run.done(mix_pieces)

    def all_sum(keep, send):
        if not tiled:
            columns = keep.shape[1]
            tensor = keep.reshape(groups, members, -1, columns)
            tensor = tensor.swapaxes(0, 1).reshape(members * groups, -1, columns)
            keep, send = split(tensor, "dp", 0, bits_of("grp"))
        found = Sum(run, links, tiled, keep, send, all_order, all_left)
        found.move()
        return found

    sums["p"] = all_sum(proj_keep, proj_send)
    grad_tokens, qkv_keep, qkv_send, attn_pieces = kernel_call(
        attend_back_body,
        [like((rows, width), full)] + row_parts(3 * width) + [like((8, width), full)],
        [VMEM] * 7 + [HBM],
        (run.after(grad_attended), projected, logs, attn_in, tokens, grad_middle, modulation, qkv_weight),
        [
            pltpu.VMEM((rows, 3 * width), low),
            pltpu.VMEM((width, width), full),
            pltpu.VMEM(qkv_weight.shape, low),
        ]
        + [pltpu.VMEM(out.shape, low) for out in row_parts(3 * width)]
        + [pltpu.SemaphoreType.DMA((4,))],
        MOST,
        8,
        [VMEM, HBM, HBM, VMEM],
    )
    run.done(attn_pieces)
    run.also(mixed_got)
    run.also(sums["u2"].got)
    run.also(sums["u1"].got)
    if tiled:
        run.also(sums["e0"].got)
    sums["p"].fold()
    sums["q"] = all_sum(run.after(qkv_keep), run.after(qkv_send))
    attn_pieces = run.after(attn_pieces)
    sums["p"].move()
    sums["d2"].move()
    if tiled:
        sums["e0"].step()
    sums["u2"].fold()
    sums["q"].step()
    sums["u2"].move()
    mixed_out, factors, grad_condition, table_part = kernel_call(
        condition_body,
        [
            like((rows, width), low),
            like((8, width), low),
            like((1, width), full),
            like((table_rows // groups, width), full),
        ],
        [VMEM] * 5 + [SMEM] + [VMEM] * 4 + [SMEM, HBM],
        (
            run.after(mixed_keep[0]),
            mixed_got[0],
            middle,
            modulation,
            cotangent,
            live_mask,
            attn_pieces,
            mix_pieces,
            conditioned,
            activated,
            bucket,
            ada_weight,
        ),
        [pltpu.VMEM(ada_weight.shape, low), pltpu.SemaphoreType.DMA],
        24,
        4,
    )

    run.done(factors)

    factors = factors[None]

    def widen(factors, axis, bit):
        return jnp.concatenate([factors, links.swap(factors, axis, bit)], axis=0)

    if tiled:
        run.also(sums["p"].got)
        run.also(sums["e0"].got)
        sums["u1"].step()
        sums["d1"].move()
        sums["u2"].step()
        factors = widen(factors, "dp", 0)
        table_part = table_part + links.swap(table_part, "dp", 0)
        run.also(sums["u1"].got)
        sums["d2"].step()
        sums["su"].move()
        sums["d1"].step()
        run.also(sums["u2"].got)
        sums["sd"].last()
        p, q = sums["p"], sums["q"]
        bit = q.order[0]
        place = len(q.left) - 1 - q.left.index(bit)
        keep, send = join_sum(*bit, place, (run.after(p.keep), p.got), (q.keep, q.got))
        run.done(send)
        both = sum_of(keep, send, y_first)
        both.move()
        [shared_total] = over_call(
            stack_body,
            [like((share + hidden // (groups * members), width), low)],
            (run.after(sums["su"].terms()[0]), sums["su"].terms()[1], *sums["sd"].terms()),
        )
        run.done(shared_total)
        shared_blocks = gather_near(links, shared_total, "dp")
        factors = widen(factors, "dp", 1)
        table_part = table_part + links.swap(table_part, "dp", 1)
        sums["d2"].step()
        both.step()
        factors = widen(factors, "grp", 0)
        both.step()
        factors = widen(factors, "grp", 1)
        up_part, down_part = over_call(
            functools.partial(shared_end_body, members),
            [like((share, hidden), full), like((hidden // groups, width), full)],
            (run.after(shared_blocks[0]), *shared_blocks[1:]),
        )
        run.done(down_part)
        factors = widen(factors, "grp", 2)
        ends = [t for name in ("e0", "u1", "u2") for t in sums[name].terms()]
        [expert_up_part] = over_call(
            own_up_body, [like((share, hidden), full)], (run.after(ends[0]), *ends[1:])
        )
        run.done(expert_up_part)
        [total] = over_call(
            sum_body, [like(both.terms()[0].shape, low)], (run.after(both.terms()[0]), both.terms()[1])
        )
        run.done(total)
        all_blocks = gather_near(links, total, "dp")
        ends = [t for name in ("e0", "d1", "d2") for t in sums[name].terms()]
        [expert_down_part] = over_call(
            own_down_body,
            [like((hidden // groups, width), full)],
            (run.after(ends[0]), *ends[1:]),
        )
        proj_part, router_part, qkv_part = over_call(
            functools.partial(rows_end_body, members),
            [
                like((share, width), full),
                like((share, LANES), full),
                like((share, 3 * width), full),
            ],
            all_blocks,
        )
    else:
        for bit in range(1, bits_of("dp")):
            factors = widen(factors, "dp", bit)
            table_part = table_part + links.swap(table_part, "dp", bit)
        factors = widen(factors, "dp", 0)
        table_part = table_part + links.swap(table_part, "dp", 0)
        sums["su"].move()
        for each in sums.values():
            each.last()
        for bit in range(bits_of("grp")):
            factors = widen(factors, "grp", bit)
        total = lambda name: wide(sums[name].terms()[0]) + wide(sums[name].terms()[1])
        ends = {
            name: gather_near(links, to_low(total(name)), "dp") for name in ("su", "sd", "p", "q")
        }
        up_part = wide(in_order(ends["su"], "dp")).reshape(members, share, groups, part)
        up_part = up_part.transpose(1, 2, 0, 3).reshape(share, hidden)
        down_part = wide(in_order(ends["sd"], "dp")).reshape(hidden // groups, width)
        own_ups = [total("u%d" % i).reshape(share, 2, groups // 2, cut) for i in range(CHUNKS)]
        expert_up_part = jnp.stack(own_ups, axis=3).transpose(0, 2, 1, 3, 4).reshape(share, hidden)
        expert_down_part = jnp.concatenate([total("d%d" % i) for i in range(CHUNKS)], axis=0)
        qkv_part = wide(in_order(ends["q"], "dp")).reshape(share, 3 * width)
        proj_part = wide(in_order(ends["p"], "dp")).reshape(share, width + LANES)
        proj_part, router_part = jnp.split(proj_part, [width], axis=1)
    left = lax.dynamic_slice_in_dim(factors[:, 6], group * share, share, axis=1)
    right = factors[:, :6].reshape(-1, 6 * width)
    ada_w_part = product_tn(left, right)
    ada_share = 6 * width // groups
    ada_b_part = lax.dynamic_slice_in_dim(jnp.sum(wide(right), axis=0), group * ada_share, ada_share)
    return (
        mixed_out[None],
        grad_tokens[None],
        grad_condition,
        table_part,
        ada_w_part,
        ada_b_part,
        qkv_part,
        proj_part,
        up_part,
        down_part,
        router_part[:, :experts],
        expert_up_part[None],
        expert_down_part[None],
    )


def solution(mesh):
    in_specs = (
        P(("grp", "dp"), None, None),
        P(("grp", "dp"), None),
        P(("grp", "dp")),
        P(("grp", "dp")),
        P(("grp", "dp"), None, None),
        P(),
        P(),
        P(),
        P(),
        P(),
        P(),
        P(),
        P(),
        P("dp", None, None),
        P("dp", None, None),
        P(("grp", "dp"), None, None),
    )
    out_specs = (
        P(("grp", "dp"), None, None),
        P(("grp", "dp"), None, None),
        P(("grp", "dp"), None),
        P("grp", None),
        P("grp", None),
        P("grp"),
        P("grp", None),
        P("grp", None),
        P("grp", None),
        P("grp", None),
        P("grp", None),
        P("dp", "grp", None),
        P("dp", "grp", None),
    )
    return jax.shard_map(
        per_device, mesh=mesh, in_specs=in_specs, out_specs=out_specs, check_vma=False
    )
```

```python
import functools
import math

import jax
import jax.numpy as jnp
from jax import lax
from jax.experimental import pallas as pl
from jax.experimental.pallas import tpu as pltpu
from jax.sharding import PartitionSpec as P

HEADS = 12
LANES = 128
CHUNKS = 3
PEAK = 1.15e9
WEIGH = 0.3
MOST = 58
K3A = 20
K4 = 58
FOLD = 20
SLAB = 58


EPSILON = 1e-06
CURVE = math.sqrt(2.0 / math.pi)
CUBIC = 0.044715

low, full = jnp.bfloat16, jnp.float32
VMEM = pl.BlockSpec(memory_space=pltpu.VMEM)
SMEM = pl.BlockSpec(memory_space=pltpu.SMEM)
HBM = pl.BlockSpec(memory_space=pltpu.MemorySpace.HBM)


def product(left_mat, right_mat, left_dim=1, right_dim=0):
    return lax.dot_general(
        left_mat,
        right_mat,
        (((left_dim,), (right_dim,)), ((), ())),
        preferred_element_type=jnp.float32,
    )


def product_nt(left_mat, right_mat):
    return product(left_mat, right_mat, 1, 1)


def product_tn(left_mat, right_mat):
    return product(left_mat, right_mat, 0, 0)


def to_low(tensor):
    return tensor.astype(low)


def wide(tensor):
    return tensor.astype(full)


def like(shape, kind):
    return jax.ShapeDtypeStruct(shape, kind)


def kernel_call(
    body, outs, in_specs, args, scratch=(), megabytes=24, microseconds=1, out_specs=None
):
    return pl.pallas_call(
        body,
        out_shape=outs,
        in_specs=in_specs,
        out_specs=out_specs or [VMEM] * len(outs),
        scratch_shapes=list(scratch),
        compiler_params=pltpu.CompilerParams(vmem_limit_bytes=megabytes << 20),
        cost_estimate=pl.CostEstimate(
            flops=int(microseconds * PEAK * WEIGH), bytes_accessed=0, transcendentals=0
        ),
    )(*args)


def normalize(tensor):
    average = jnp.mean(tensor, axis=-1, keepdims=True)
    centered = tensor - average
    inverse = lax.rsqrt(jnp.mean(centered * centered, axis=-1, keepdims=True) + EPSILON)
    return (centered * inverse, inverse)


def normalize_back(gradient, normed, inverse):
    first_term = jnp.mean(gradient, axis=-1, keepdims=True)
    second_term = jnp.mean(gradient * normed, axis=-1, keepdims=True)
    return inverse * (gradient - first_term - normed * second_term)


def column_sum(tensor):
    return jnp.sum(tensor, axis=0, keepdims=True)


def gelu_pair(pre):
    square = pre * pre
    bend = jnp.tanh(CURVE * (pre + CUBIC * pre * square))
    half = 0.5 + 0.5 * bend
    slope = half + (0.5 * CURVE) * pre * (1.0 - bend * bend) * (1.0 + 3.0 * CUBIC * square)
    return pre * half, slope


def halves(width):
    lane = lax.broadcasted_iota(jnp.int32, (1, LANES), 1)
    return [lane // width == i for i in range(LANES // width)]


def attend_body(
    tokens,
    condition,
    bucket,
    live,
    routes,
    table,
    ada_bias,
    router,
    ada_hbm,
    qkv_hbm,
    proj_hbm,
    packed,
    gates_out,
    modulation_out,
    conditioned_out,
    activated_out,
    attn_in_hbm,
    projected_hbm,
    log_hbm,
    attended_hbm,
    attn_out_hbm,
    middle_hbm,
    attn_in_out,
    projected_out,
    log_out,
    attended_out,
    attn_out_out,
    middle_out,
    ada,
    qkv,
    proj,
    sems,
):
    rows, width = tokens.shape
    experts = router.shape[0]
    leaving = []

    def leave(source, target):
        copy = pltpu.make_async_copy(source, target, sems.at[4 + len(leaving)])
        copy.start()
        leaving.append(copy)

    head = width // HEADS
    scaling = float(head) ** (-0.5)
    early = 2 * width
    copies = [
        pltpu.make_async_copy(ada_hbm.at[:, :early], ada.at[:, :early], sems.at[0]),
        pltpu.make_async_copy(qkv_hbm, qkv, sems.at[1]),
        pltpu.make_async_copy(ada_hbm.at[:, early:], ada.at[:, early:], sems.at[2]),
        pltpu.make_async_copy(proj_hbm, proj, sems.at[3]),
    ]
    for copy in copies:
        copy.start()

    named = lax.broadcasted_iota(jnp.int32, (table.shape[0], 1), 0) == bucket[0]
    conditioned = wide(condition[...]) + column_sum(jnp.where(named, wide(table[...]), 0.0))
    activated = to_low(conditioned * (1.0 / (1.0 + jnp.exp(-conditioned))))
    conditioned_out[...] = conditioned
    activated_out[...] = activated
    activated = jnp.broadcast_to(activated, (16, width))

    bias = wide(ada_bias[...])
    bias = jnp.concatenate([bias[i : i + 1] for i in range(bias.shape[0])], axis=1)
    inputs = wide(tokens[...])
    normed, _ = normalize(inputs)
    copies[0].wait()
    modulation_out[:, :early] = product(activated, ada[:, :early])[:1] + bias[:, :early]
    shift_attn = modulation_out[:, :width]
    scale_attn = modulation_out[:, width:early]
    attn_in = to_low(normed * (1.0 + scale_attn) + shift_attn)
    attn_in_out[...] = attn_in
    leave(attn_in_out, attn_in_hbm)
    copies[1].wait()
    projected_out[...] = to_low(product(attn_in, qkv[...]))
    leave(projected_out, projected_hbm)
    copies[2].wait()
    modulation_out[:, early:] = product(activated, ada[:, early:])[:1] + bias[:, early:]

    masks = halves(head)
    column = lax.broadcasted_iota(jnp.int32, (1, LANES), 1)
    logs = jnp.zeros((rows, LANES), full)
    for block in range(width // LANES):
        at = pl.ds(block * LANES, LANES)
        query = projected_out[:, at]
        key = projected_out[:, pl.ds(width + block * LANES, LANES)]
        value = projected_out[:, pl.ds(2 * width + block * LANES, LANES)]
        total = jnp.zeros((rows, LANES), full)
        for i, mask in enumerate(masks):
            scores = product_nt(jnp.where(mask, query, jnp.zeros_like(query)), key) * scaling
            top = jnp.max(scores, axis=-1, keepdims=True)
            raised = jnp.exp(scores - top)
            whole = jnp.sum(raised, axis=-1, keepdims=True)
            probs = to_low(raised / whole)
            logs = jnp.where(column == block * len(masks) + i, top + jnp.log(whole), logs)
            total = jnp.where(mask, product(probs, value), total)
        attended_out[:, at] = to_low(total)
    log_out[...] = logs
    leave(log_out, log_hbm)
    leave(attended_out, attended_hbm)

    copies[3].wait()
    attn_out = product(attended_out[...], proj[...])
    attn_out_out[...] = attn_out
    leave(attn_out_out, attn_out_hbm)
    piece = lambda i: modulation_out[:, pl.ds(i * width, width)]
    middle = inputs + piece(2) * attn_out
    middle_out[...] = middle
    leave(middle_out, middle_hbm)
    normed, _ = normalize(middle)
    mix_in = to_low(normed * (1.0 + piece(4)) + piece(3))
    packed[:rows, :] = mix_in

    logits = product_nt(router[...], mix_in)
    ids = lax.broadcasted_iota(jnp.int32, (experts, rows), 0)
    hot = (routes[:1] == ids) | (routes[1:2] == ids)
    top = jnp.max(jnp.where(hot, logits, -jnp.inf), axis=0, keepdims=True)
    turned = jnp.where(hot, jnp.exp(jnp.where(hot, logits, top) - top), 0.0)
    turned = turned / jnp.sum(turned, axis=0, keepdims=True)
    gates_out[...] = jnp.transpose(
        jnp.concatenate([turned, jnp.zeros((LANES - experts, rows), full)], axis=0)
    )
    gate_mix = piece(5) * wide(live[0])
    extra = packed.shape[0] - rows
    high, turned_high = to_low(gate_mix), to_low(turned)
    wall = jnp.zeros((experts, width - rows), full)
    packed[rows:, :] = to_low(
        jnp.concatenate(
            [
                jnp.concatenate([wide(turned_high), wall], axis=1),
                jnp.concatenate([turned - wide(turned_high), wall], axis=1),
                wide(high),
                gate_mix - wide(high),
                jnp.zeros((extra - 2 * experts - 2, width), full),
            ],
            axis=0,
        )
    )
    for copy in leaving:
        copy.wait()


class Mover:
    def __init__(self, sems):
        self.sems, self.count, self.open = sems, 0, []

    def start(self, source, target, keep=True):
        copy = pltpu.make_async_copy(source, target, self.sems.at[self.count])
        copy.start()
        self.count += 1
        if keep:
            self.open.append(copy)
        return copy

    def finish(self):
        for copy in self.open:
            copy.wait()


def wait(copies):
    while copies:
        copies.pop().wait()


def pick_body(members, shared_up, part_up):
    groups = lax.axis_size("grp")
    span = shared_up.shape[1] // groups
    part = span // members
    pick = spread_units(span, part, lax.axis_index("dp"), 0)
    for i in range(0, groups, 4):
        part_up[:, pl.ds(i * part, 4 * part)] = to_low(
            product(shared_up[:, pl.ds(i * span, 4 * span)], pick)
        )


def spread_units(span, part, member, dim):
    shape = (4 * span, 4 * part) if dim == 0 else (4 * part, 4 * span)
    whole = lax.broadcasted_iota(jnp.int32, shape, dim)
    own = lax.broadcasted_iota(jnp.int32, shape, 1 - dim)
    place = own + (own // part) * (span - part) + member * part
    return to_low(jnp.where(whole == place, 1.0, 0.0))


def parted(groups, bit, mine, i):
    return ((i >> bit) << (bit + 1)) + (mine << bit) + (i & ((1 << bit) - 1))


def bring_part_down(mover, members, shared_down, part_down):
    groups = lax.axis_size("grp")
    span = shared_down.shape[0] // groups
    part = span // members
    copies = []
    for i in range(groups):
        start = pl.multiple_of(i * span + lax.axis_index("dp") * part, 16)
        copies.append(
            mover.start(
                shared_down.at[pl.ds(start, part)], part_down.at[pl.ds(i * part, part)], False
            )
        )
    return copies


def bring_cut(mover, chunk, half, expert, own, lanes):
    groups = lax.axis_size("grp")
    span = expert.shape[2 if lanes else 1] // groups
    cut = span // CHUNKS
    side = lax.axis_index("grp") & 1
    copies = []
    for place in range(groups // 2):
        group = 2 * place + (side if half else 1 - side)
        start = pl.multiple_of(group * span + chunk * cut, LANES)
        to = pl.ds((half * groups // 2 + place) * cut, cut)
        if lanes:
            copies.append(mover.start(expert.at[0, :, pl.ds(start, cut)], own.at[:, to], False))
        else:
            copies.append(mover.start(expert.at[0, pl.ds(start, cut)], own.at[to], False))
    return copies


def feed_rows(mover, bit, rows, seen, grads, up, down, act, grad_pre, held, outs, waits, ordered):
    act_out, pre_out, put_up, put_down = outs
    wait_up, wait_down, wait_seen, wait_grads = waits
    groups = lax.axis_size("grp")
    mine = (lax.axis_index("grp") >> bit) & 1
    side = lax.axis_index("grp") & 1
    share = seen.shape[1] // groups
    step = held.shape[1]
    for number, start in enumerate(range(0, up.shape[1], step)):
        at = pl.ds(start, step)
        wait(wait_up[number])
        slopes = []
        for i in range(0, seen.shape[0], rows):
            wait(wait_seen[i // rows])
            raised, slope = gelu_pair(product(seen[pl.ds(i, rows), :], up[:, at]))
            act[pl.ds(i, rows), at] = to_low(raised)
            slopes.append(slope)
            if i == 0:
                wait(wait_down[number])
            wait(wait_grads[i // rows])
            slope = slopes.pop()
            grad_pre[pl.ds(i, rows), at] = to_low(
                slope * product_nt(grads[pl.ds(i, rows), :], down[at, :])
            )
        if act_out is not None:
            mover.start(act.at[:, at], act_out.at[:, at])
            mover.start(grad_pre.at[:, at], pre_out.at[:, at])
        held[...] = product_tn(seen[...], grad_pre[:, at])
        place = (1 - side if number == 0 else side) if ordered else number
        for kind, value in enumerate((1 - mine, mine)):
            rows_of = []
            for i in range(groups // 2):
                first = pl.multiple_of(parted(groups, bit, value, i) * share, 8)
                rows_of.append(to_low(held[pl.ds(first, share)]))
            put_up(kind, place, rows_of)
        put_down(number, at, to_low(product_tn(act[:, at], grads[...])))


def up_putter(mover, send, keep, send_out, keep_out, step):
    def put_up(kind, place, rows_of):
        target, out = ((send, send_out), (keep, keep_out))[kind]
        at = pl.ds(place * step, step)
        if not isinstance(place, int):
            at = pl.ds(pl.multiple_of(place * step, LANES), step)
        for i, value in enumerate(rows_of):
            target[i, :, at] = value
        mover.start(target.at[:, :, at], out.at[:, :, at])

    return put_up


def slab_putters(mover, slabs, slab_outs, step):
    groups, whole, _ = slabs[0].shape
    count = step // LANES

    def put_up(kind, place, rows_of):
        slab, out = slabs[kind], slab_outs[kind]
        share = rows_of[0].shape[0]
        first = pl.multiple_of(place * count * share, 16)
        for i, value in enumerate(rows_of):
            for j in range(count):
                at = pl.ds(pl.multiple_of(first + j * share, 16), share)
                slab[i, at, :] = value[:, j * LANES : (j + 1) * LANES]
        at = pl.ds(first, count * share)
        mover.start(slab.at[:, at], out.at[:, at])

    def put_down(number, at, value):
        slab, out = slabs[number], slab_outs[number]
        cut = value.shape[0] // groups
        first = whole - value.shape[1] // LANES * cut
        for i in range(groups):
            for j in range(value.shape[1] // LANES):
                slab[i, pl.ds(first + j * cut, cut), :] = value[
                    i * cut : (i + 1) * cut, j * LANES : (j + 1) * LANES
                ]
        at = pl.ds(first, whole - first)
        mover.start(slab.at[:, at], out.at[:, at])

    return put_up, put_down


def shared_body(bit, members, rows, experts, tiled, *refs):
    packs_hbm, cotangents_hbm = refs[:members], refs[members : 2 * members]
    (
        up_hbm,
        down_hbm,
        seen_out,
        routed_out,
        gate_out,
        up_keep_out,
        up_send_out,
        down_keep_out,
        down_send_out,
        act_out,
        pre_out,
        packs,
        cotangents,
        up,
        down,
        seen,
        routed_grads,
        grads,
        gate_held,
        act,
        grad_pre,
        up_keep,
        up_send,
        down_keep,
        down_send,
        held,
        sems,
    ) = refs[2 * members :]
    mover = Mover(sems)
    width = seen.shape[1]
    me = lax.axis_index("dp")
    named = lax.broadcasted_iota(jnp.int32, (experts, 1), 0) == me
    pack_copies = [mover.start(p, packs.at[i], False) for i, p in enumerate(packs_hbm)]
    up_copy = mover.start(up_hbm, up, False)
    cotangent_copies = [mover.start(c, cotangents.at[i], False) for i, c in enumerate(cotangents_hbm)]
    if tiled:
        down_copies = bring_part_down(mover, members, down_hbm, down)
    else:
        down_copies = [mover.start(down_hbm, down, False)]
    for i in range(members):
        at = pl.ds(i * rows, rows)
        pack_copies[i].wait()
        seen[at, :] = packs[i, :rows, :]
        extra = wide(packs[i, rows:, :])
        gates = extra[:experts, :rows] + extra[experts : 2 * experts, :rows]
        gate = column_sum(jnp.where(named, gates, 0.0))
        gate = jnp.transpose(jnp.broadcast_to(gate, (LANES, rows)))
        gate_held[at, :] = gate
        gate_mix = extra[2 * experts : 2 * experts + 1] + extra[2 * experts + 1 : 2 * experts + 2]
        cotangent_copies[i].wait()
        mixture_grads = to_low(gate_mix * wide(cotangents[i]))
        grads[at, :] = mixture_grads
        routed_grads[at, :] = to_low(gate[:, :1] * wide(mixture_grads))
    mover.start(seen, seen_out)
    mover.start(routed_grads, routed_out)
    mover.start(gate_held, gate_out)

    side = lax.axis_index("grp") & 1
    groups = lax.axis_size("grp")
    part = up.shape[1] // groups

    def put_down(number, at, value):
        if not tiled:
            down_keep[...] = value
            mover.start(down_keep, down_keep_out)
            return
        count = value.shape[0] // part
        for mine in range(2):

            @pl.when(side == mine)
            def _():
                for i in range(count):
                    g = number * count + i
                    target = down_keep if g & 1 == mine else down_send
                    target[g >> 1] = value[i * part : (i + 1) * part]

        rows_at = pl.ds(number * count // 2, count // 2)
        mover.start(down_keep.at[rows_at], down_keep_out.at[rows_at])
        mover.start(down_send.at[rows_at], down_send_out.at[rows_at])

    blocks = range(seen.shape[0] // rows)
    waits = ([[up_copy], []], [down_copies, []], [[] for _ in blocks], [[] for _ in blocks])
    put_up = up_putter(mover, up_send, up_keep, up_send_out, up_keep_out, held.shape[1])
    outs = (act_out, pre_out, put_up, put_down)
    feed_rows(mover, bit, rows, seen, grads, up, down, act, grad_pre, held, outs, waits, False)
    mover.finish()


def bring_rows(mover, rows, source, target):
    return [
        [mover.start(source.at[pl.ds(i, rows)], target.at[pl.ds(i, rows)], False)]
        for i in range(0, source.shape[0], rows)
    ]


def bring_cut_all(mover, chunk, tiled, up_hbm, down_hbm, up, down, seen, grads, rows):
    if tiled:
        wait_up = [bring_cut(mover, chunk, 0, up_hbm, up, True)]
        wait_seen = bring_rows(mover, rows, *seen)
        wait_down = [bring_cut(mover, chunk, 0, down_hbm, down, False)]
        wait_grads = bring_rows(mover, rows, *grads)
        wait_up.append(bring_cut(mover, chunk, 1, up_hbm, up, True))
        wait_down.append(bring_cut(mover, chunk, 1, down_hbm, down, False))
    else:
        wait_up = [[mover.start(up_hbm, up, False)], []]
        wait_seen = bring_rows(mover, rows, *seen)
        wait_down = [[mover.start(down_hbm, down, False)], []]
        wait_grads = bring_rows(mover, rows, *grads)
    return wait_up, wait_down, wait_seen, wait_grads


def routed_body(bit, chunk, rows, tiled, one, *refs):
    seen_hbm, grads_hbm, up_hbm, down_hbm = refs[:4]
    many = 2 if one else 4
    grad_outs, (act_out, pre_out) = refs[4 : 4 + many], refs[4 + many : 6 + many]
    seen, grads, up, down, act, grad_pre, held = refs[6 + many : 13 + many]
    kept, sems = refs[13 + many : -1], refs[-1]
    mover = Mover(sems)
    waits = bring_cut_all(
        mover, chunk, tiled, up_hbm, down_hbm, up, down, (seen_hbm, seen), (grads_hbm, grads), rows
    )
    if one:
        put_up, put_down = slab_putters(mover, kept, grad_outs, held.shape[1])
    else:
        put_up = up_putter(mover, *kept[:2], *grad_outs[:2], held.shape[1])

        def put_down(number, at, value):
            target, out = kept[2 + number], grad_outs[2 + number]
            target[...] = value.reshape(target.shape)
            mover.start(target, out)

    outs = (act_out, pre_out, put_up, put_down)
    feed_rows(mover, bit, rows, seen, grads, up, down, act, grad_pre, held, outs, waits, True)
    mover.finish()


def result_body(bit, members, rows, block, experts, tiled, *refs):
    parts = 1 + CHUNKS
    acts_hbm, pres_hbm = refs[:CHUNKS], refs[CHUNKS : 2 * CHUNKS]
    given = 4 if tiled else 2 * parts
    weights_hbm = refs[2 * CHUNKS : 2 * CHUNKS + given]
    rest = refs[2 * CHUNKS + given :]
    seen_hbm, grads_hbm, gate_hbm = rest[:3]
    up_keep_out, up_send_out, down_keep_out, down_send_out = rest[3:7]
    back_keep_out, back_send_out, mixed_keep_out, mixed_send_out = rest[7:11]
    scratch, sems = rest[11:-1], rest[-1]
    acts, pres, ups, downs = [scratch[i * parts : (i + 1) * parts] for i in range(4)]
    seen, grads, gate, back, up_keep, up_send, down_keep, down_send, held = scratch[4 * parts :]
    mover = Mover(sems)
    width = grads.shape[1]
    me = lax.axis_index("dp")
    column = lax.broadcasted_iota(jnp.int32, (1, LANES), 1)
    last = CHUNKS - 1
    if tiled:
        up_hbm, down_hbm = weights_hbm[2:]
    else:
        up_hbm, down_hbm = weights_hbm[parts - 1], weights_hbm[2 * parts - 1]
    waits = bring_cut_all(
        mover,
        last,
        tiled,
        up_hbm,
        down_hbm,
        ups[-1],
        downs[-1],
        (seen_hbm, seen),
        (grads_hbm, grads),
        block,
    )

    def bring_weights(kind, targets):
        if not tiled:
            sources = weights_hbm[kind * parts : (kind + 1) * parts]
            return [[mover.start(a, b, False)] for a, b in zip(sources[:-1], targets)]
        part, expert = weights_hbm[kind], weights_hbm[2 + kind]
        if kind:
            found = [bring_part_down(mover, members, part, targets[0])]
        else:
            found = [[mover.start(part, targets[0], False)]]
        for c in range(last):
            found.append(
                bring_cut(mover, c, 0, expert, targets[1 + c], kind == 0)
                + bring_cut(mover, c, 1, expert, targets[1 + c], kind == 0)
            )
        return found

    more = [mover.start(a, b, False) for a, b in zip(acts_hbm, acts)]
    for found in bring_weights(1, downs):
        more += found
    more.append(mover.start(gate_hbm, gate, False))
    later = [mover.start(a, b, False) for a, b in zip(pres_hbm, pres)]
    for found in bring_weights(0, ups):
        later += found

    def put_down(number, at, value):
        target, out = ((down_send, down_send_out), (down_keep, down_keep_out))[number]
        target[...] = value.reshape(target.shape)
        mover.start(target, out)

    put_up = up_putter(mover, up_send, up_keep, up_send_out, up_keep_out, held.shape[1])
    outs = (None, None, put_up, put_down)
    feed_rows(
        mover,
        bit,
        block,
        seen,
        grads,
        ups[-1],
        downs[-1],
        acts[-1],
        pres[-1],
        held,
        outs,
        waits,
        True,
    )
    wait(more)
    mixed = seen
    for i in [*range(1, members, 2), *range(0, members, 2)]:
        at = pl.ds(i * rows, rows)
        to = pl.ds((i // 2) * rows, rows)
        routed = sum(product(a[at, :], d[...]) for a, d in zip(acts[1:], downs[1:]))
        routed = wide(to_low(routed))
        mixed[at, :] = to_low(product(acts[0][at, :], downs[0][...]) + gate[at, :1] * routed)
        mover.start(mixed.at[at], (mixed_send_out if i % 2 else mixed_keep_out).at[to])
        weighed = jnp.sum(wide(grads[at, :]) * routed, axis=1, keepdims=True)
        high = wide(to_low(weighed))
        back[at, width:] = to_low(
            jnp.where(column == me, high, 0.0)
            + jnp.where(column == experts + me, weighed - high, 0.0)
        )
        wait(later)
        back[at, :width] = to_low(sum(product_nt(p[at, :], u[...]) for p, u in zip(pres, ups)))
        mover.start(back.at[at], (back_send_out if i % 2 else back_keep_out).at[to])
    mover.finish()


def middle_back_body(
    kept,
    got,
    packed,
    middle,
    modulation,
    gates,
    cotangent,
    live,
    attn_out,
    attended,
    proj,
    router,
    proj_keep,
    proj_send,
    grad_attended,
    grad_middle_out,
    grad_pieces,
    held,
):
    rows, width = cotangent.shape
    experts = router.shape[0]
    piece = lambda i: modulation[:, pl.ds(i * width, width)]
    back = wide(kept[:, width:]) + wide(got[:, width:])
    weighed = back[:, :experts] + back[:, experts : 2 * experts]
    mine = gates[:, :experts]
    grad_logits = to_low(weighed - mine * jnp.sum(weighed, axis=1, keepdims=True))
    mix_in = packed[:rows, :]
    grad_mix_in = wide(kept[:, :width]) + wide(got[:, :width])
    grad_mix_in = grad_mix_in + product(grad_logits, router[...])
    normed, inverse = normalize(middle[...])
    grad_result = wide(cotangent[...]) * wide(live[0])
    grad_middle = grad_result + normalize_back(grad_mix_in * (1.0 + piece(4)), normed, inverse)
    grad_middle_out[...] = grad_middle
    grad_attn_out = to_low(piece(2) * grad_middle)
    held[:, width:] = jnp.zeros((width, LANES), full)
    held[:, width : width + experts] = product_tn(mix_in, grad_logits)
    held[:, :width] = product_tn(attended[...], grad_attn_out)
    part_rows(held, proj_keep, proj_send, slice(None))
    grad_attended[...] = to_low(product_nt(grad_attn_out, proj[...]))
    grad_pieces[0:1] = column_sum(grad_middle * attn_out[...])
    grad_pieces[1:2] = column_sum(grad_mix_in)
    grad_pieces[2:3] = column_sum(grad_mix_in * normed)


def part_rows(held, keep, send, at):
    groups, members = lax.axis_size("grp"), lax.axis_size("dp")
    share = held.shape[0] // (groups * members)
    if len(keep.shape) == 2:
        keep[:, at] = to_low(held[...])
        return
    mine = lax.axis_index("dp") & 1
    for target, value in ((send, 1 - mine), (keep, mine)):
        for i in range(members // 2):
            for g in range(groups):
                first = pl.multiple_of((g * members + 2 * i + value) * share, 8)
                target[i * groups + g, :, at] = to_low(held[pl.ds(first, share)])


def attend_back_body(
    grad_attended,
    projected,
    logs,
    modulation,
    attn_in_hbm,
    tokens_hbm,
    grad_middle_hbm,
    qkv_hbm,
    grad_tokens,
    keep_outs,
    send_outs,
    value_keep_out,
    value_send_out,
    grad_pieces,
    grad_projected,
    held,
    qkv,
    keeps,
    sends,
    value_keep,
    value_send,
    attn_in,
    tokens,
    grad_middle,
    sems,
):
    rows, width = tokens.shape
    head = width // HEADS
    scaling = float(head) ** (-0.5)
    mover = Mover(sems)
    attn_copy = mover.start(attn_in_hbm, attn_in, False)
    late = [
        mover.start(a, b, False)
        for a, b in ((qkv_hbm, qkv), (tokens_hbm, tokens), (grad_middle_hbm, grad_middle))
    ]
    masks = halves(head)
    column = lax.broadcasted_iota(jnp.int32, (1, LANES), 1)
    for block in range(width // LANES):
        parts = [pl.ds(i * width + block * LANES, LANES) for i in range(3)]
        query, key, value = [projected[:, at] for at in parts]
        grads = grad_attended[:, parts[0]]
        grad_query, grad_key, grad_value = [jnp.zeros((rows, LANES), full)] * 3
        for i, mask in enumerate(masks):
            zero = jnp.zeros_like(query)
            scores = product_nt(jnp.where(mask, query, zero), key) * scaling
            log = jnp.sum(
                jnp.where(column == block * len(masks) + i, logs[...], 0.0), axis=1, keepdims=True
            )
            probs = jnp.exp(scores - log)
            grad_probs = product_nt(jnp.where(mask, grads, zero), value)
            grad_value = jnp.where(mask, product_tn(to_low(probs), grads), grad_value)
            drift = jnp.sum(probs * grad_probs, axis=-1, keepdims=True)
            grad_scores = to_low(probs * (grad_probs - drift))
            grad_query = jnp.where(mask, product(grad_scores, key), grad_query)
            grad_key = jnp.where(mask, product_tn(grad_scores, query), grad_key)
        for at, grad in zip(parts, (grad_query * scaling, grad_key * scaling, grad_value)):
            grad_projected[:, at] = to_low(grad)
    attn_copy.wait()
    for i in range(3):
        at = pl.ds(i * width, width)
        held[...] = product_tn(attn_in[...], grad_projected[:, at])
        pairs = [(keeps, keep_outs), (sends, send_outs)]
        if i == 2:
            at, pairs = slice(None), [(value_keep, value_keep_out), (value_send, value_send_out)]
        part_rows(held, pairs[0][0], pairs[1][0], at)
        for source, target in pairs[: len(keeps.shape) - 1]:
            place = (slice(None),) * (len(source.shape) - 1) + (at,)
            mover.start(source.at[place], target.at[place])
    wait(late)
    grad_attn_in = product_nt(grad_projected[...], qkv[...])
    normed, inverse = normalize(wide(tokens[...]))
    scale_attn = modulation[:, pl.ds(width, width)]
    grad_pieces[0:1] = column_sum(grad_attn_in)
    grad_pieces[1:2] = column_sum(grad_attn_in * normed)
    grad_tokens[...] = grad_middle[...] + normalize_back(
        grad_attn_in * (1.0 + scale_attn), normed, inverse
    )
    mover.finish()


def condition_body(
    kept,
    got,
    middle,
    modulation,
    cotangent,
    live,
    attn_pieces,
    mix_pieces,
    conditioned,
    activated,
    bucket,
    ada_hbm,
    mixed_out,
    factors,
    grad_condition,
    table_part,
    ada,
    sem,
):
    rows, width = cotangent.shape
    copy = pltpu.make_async_copy(ada_hbm, ada, sem)
    copy.start()
    alive = wide(live[0])
    gate_mix = modulation[:, pl.ds(5 * width, width)]
    mixture = wide(kept[...]) + wide(got[...])
    mixed_out[...] = to_low((middle[...] + gate_mix * mixture) * alive)
    grad_gate_mix = column_sum(wide(cotangent[...]) * alive * mixture)
    grads = [
        attn_pieces[0:1],
        attn_pieces[1:2],
        mix_pieces[0:1],
        mix_pieces[1:2],
        mix_pieces[2:3],
        grad_gate_mix,
    ]
    factors[...] = to_low(
        jnp.concatenate(grads + [wide(activated[...]), jnp.zeros((1, width), full)], axis=0)
    )
    copy.wait()
    pulled = jnp.zeros((1, width), full)
    for i, grad in enumerate(grads):
        spread = jnp.broadcast_to(to_low(grad), (16, width))
        pulled = pulled + product_nt(spread, ada[:, pl.ds(i * width, width)])[:1]
    drive = conditioned[...]
    gate = 1.0 / (1.0 + jnp.exp(-drive))
    grad = pulled * gate * (1.0 + drive * (1.0 - gate))
    grad_condition[...] = grad
    share = table_part.shape[0]
    row = lax.broadcasted_iota(jnp.int32, (share, 1), 0) + lax.axis_index("grp") * share
    table_part[...] = jnp.where(row == bucket[0], grad, 0.0)


def split_body(mine, keep_a, got_a, keep_b, got_b, keep_out, send_out):
    keep_out[...] = to_low(wide(keep_a[...]) + wide(got_a[...]))
    send_out[...] = to_low(wide(keep_b[...]) + wide(got_b[...]))


def split_sum(axis, bit, place, keep, got):
    mine = ((lax.axis_index(axis) >> bit) & 1).reshape(1)
    count, *block = keep.shape
    run = 1 << place
    spec = lambda other: pl.BlockSpec(
        (run, *block), lambda i, mine: (2 * i + (mine[0] ^ other), 0, 0)
    )
    out = pl.BlockSpec((run, *block), lambda i, mine: (i, 0, 0))
    return pl.pallas_call(
        split_body,
        grid_spec=pltpu.PrefetchScalarGridSpec(
            num_scalar_prefetch=1,
            grid=(count // 2 // run,),
            in_specs=[spec(0), spec(0), spec(1), spec(1)],
            out_specs=[out, out],
        ),
        out_shape=[like((count // 2, *block), low)] * 2,
        compiler_params=pltpu.CompilerParams(vmem_limit_bytes=FOLD << 20),
        cost_estimate=pl.CostEstimate(flops=int(1.5 * PEAK * WEIGH), bytes_accessed=0, transcendentals=0),
    )(mine, keep, got, keep, got)


def even_odd_body(keep_a, got_a, keep_b, got_b, keep_out, send_out):
    keep_out[...] = to_low(wide(keep_a[...]) + wide(got_a[...]))
    send_out[...] = to_low(wide(keep_b[...]) + wide(got_b[...]))


def even_odd_sum(keep, got):
    count, *block = keep.shape
    spec = lambda other: pl.BlockSpec((1, *block), lambda i: (2 * i + other, 0, 0))
    out = pl.BlockSpec((1, *block), lambda i: (i, 0, 0))
    return pl.pallas_call(
        even_odd_body,
        grid=(count // 2,),
        in_specs=[spec(0), spec(0), spec(1), spec(1)],
        out_specs=[out, out],
        out_shape=[like((count // 2, *block), low)] * 2,
        compiler_params=pltpu.CompilerParams(vmem_limit_bytes=FOLD << 20),
        cost_estimate=pl.CostEstimate(flops=int(1.5 * PEAK * WEIGH), bytes_accessed=0, transcendentals=0),
    )(keep, got, keep, got)


def join_body(mine, *refs):
    keep_out, send_out = refs[-2:]
    width = refs[0].shape[-1]
    for out, terms in ((keep_out, refs[0:4]), (send_out, refs[4:8])):
        out[:, :, :width] = to_low(wide(terms[0][...]) + wide(terms[1][...]))
        out[:, :, width:] = to_low(wide(terms[2][...]) + wide(terms[3][...]))


def join_sum(axis, bit, place, first, second):
    mine = ((lax.axis_index(axis) >> bit) & 1).reshape(1)
    count, rows, width = first[0].shape
    columns = width + second[0].shape[2]

    def spec(columns, other):
        return pl.BlockSpec(
            (run, rows, columns), lambda i, mine: (2 * i + (mine[0] ^ other), 0, 0)
        )

    run = 1 << place
    out = pl.BlockSpec((run, rows, columns), lambda i, mine: (i, 0, 0))
    return pl.pallas_call(
        join_body,
        grid_spec=pltpu.PrefetchScalarGridSpec(
            num_scalar_prefetch=1,
            grid=(count // 2 // run,),
            in_specs=[
                spec(c, other) for other in (0, 1) for c in (width, width, columns - width, columns - width)
            ],
            out_specs=[out, out],
        ),
        out_shape=[like((count // 2, rows, columns), low)] * 2,
        compiler_params=pltpu.CompilerParams(vmem_limit_bytes=FOLD << 20),
        cost_estimate=pl.CostEstimate(flops=int(1.5 * PEAK * WEIGH), bytes_accessed=0, transcendentals=0),
    )(mine, *first, *second, *first, *second)


def slab_join_body(mine, *refs):
    keep_out, send_out = refs[-2:]
    half = (len(refs) - 2) // 2
    for out, terms in ((keep_out, refs[:half]), (send_out, refs[half:-2])):
        start = 0
        for keep, got in zip(terms[::2], terms[1::2]):
            _, rows, columns = keep.shape
            for j in range(columns // LANES):
                at = slice(j * LANES, (j + 1) * LANES)
                out[0, start : start + rows, :] = to_low(
                    wide(keep[0, :, at]) + wide(got[0, :, at])
                )
                start += rows


def slab_join(axis, bit, place, *pairs):
    mine = ((lax.axis_index(axis) >> bit) & 1).reshape(1)
    count = pairs[0][0].shape[0]
    whole = sum(keep.size for keep, _ in pairs) // (count * LANES)

    def spec(block, other):
        return pl.BlockSpec(
            (1, *block), lambda i, mine: (parted(count, place, mine[0] ^ other, i), 0, 0)
        )

    out = pl.BlockSpec((1, whole, LANES), lambda i, mine: (i, 0, 0))
    terms = [term for pair in pairs for term in pair]
    return pl.pallas_call(
        slab_join_body,
        grid_spec=pltpu.PrefetchScalarGridSpec(
            num_scalar_prefetch=1,
            grid=(count // 2,),
            in_specs=[spec(t.shape[1:], other) for other in (0, 1) for t in terms],
            out_specs=[out, out],
        ),
        out_shape=[like((count // 2, whole, LANES), low)] * 2,
        compiler_params=pltpu.CompilerParams(vmem_limit_bytes=SLAB << 20),
        cost_estimate=pl.CostEstimate(flops=int(1.5 * PEAK * WEIGH), bytes_accessed=0, transcendentals=0),
    )(mine, *terms, *terms)


def stack_body(*refs):
    *pairs, total = refs
    start = 0
    for i in range(0, len(pairs), 2):
        rows = pl.ds(start, pairs[i].shape[0])
        total[rows, :] = to_low(wide(pairs[i][...]) + wide(pairs[i + 1][...]))
        start += pairs[i].shape[0]


def sum_body(keep, got, total):
    total[...] = to_low(wide(keep[...]) + wide(got[...]))


def own_up_body(*refs):
    *pairs, out = refs
    share, hidden = out.shape
    groups = lax.axis_size("grp")
    for c in range(CHUNKS):
        keep, got = pairs[2 * c : 2 * c + 2]
        rows = hidden // CHUNKS // LANES * share if c != 1 else share
        total = wide(keep[:rows, :]) + wide(got[:rows, :])
        for i in range(groups):
            place = (i & 1) * (groups // 2) + (i >> 1)
            if c == 1:
                value = total[:, place * LANES : (place + 1) * LANES]
            else:
                value = total[place * share : (place + 1) * share]
            out[:, pl.ds((i * CHUNKS + c) * LANES, LANES)] = value


def own_down_body(first, *refs):
    *pairs, out = refs
    width = out.shape[1]
    cut = out.shape[0] // CHUNKS
    size = width // LANES * cut
    for c in range(CHUNKS):
        keep, got = pairs[:2] if c < 2 else pairs[2:]
        start = first + (size if c == 1 else 0)
        for j in range(width // LANES):
            at = pl.ds(start + j * cut, cut)
            out[pl.ds(c * cut, cut), pl.ds(j * LANES, LANES)] = wide(keep[at, :]) + wide(got[at, :])


def shared_end_body(members, *refs):
    blocks, up_out, down_out = refs[:members], refs[-2], refs[-1]
    share = up_out.shape[0]
    me = lax.axis_index("dp")
    groups = lax.axis_size("grp")
    span = up_out.shape[1] // groups
    part = span // members
    for i in range(0, groups, 4):
        total = 0.0
        for far in range(members):
            pick = spread_units(span, part, me ^ far, 1)
            total = total + product(blocks[far][:share, pl.ds(i * part, 4 * part)], pick)
        up_out[:, pl.ds(i * span, 4 * span)] = total
    for far in range(members):
        start = pl.multiple_of((me ^ far) * part, 8)
        down_out[pl.ds(start, part)] = wide(blocks[far][share:, :])


def rows_end_body(members, *refs):
    blocks, outs = refs[:members], refs[members:]
    me = lax.axis_index("dp")
    share = blocks[0].shape[0]
    for far in range(members):
        start = pl.multiple_of((me ^ far) * share, 8)
        column = 0
        for out in outs:
            out[pl.ds(start, share), :] = wide(blocks[far][:, column : column + out.shape[1]])
            column += out.shape[1]


def bits_of(axis):
    return lax.axis_size(axis).bit_length() - 1


def tie(tensor, *before):
    return lax.optimization_barrier((tensor, *before))[0]


DEPTH_X, DEPTH_Y, DEPTH_Z = 2, 2, 3


class Links:
    depth = {"y": DEPTH_Y, "z": DEPTH_Z, "x": DEPTH_X}

    def __init__(self):
        self.past = {}

    def swap(self, tensor, axis, bit):
        pairs = [(i, i ^ (1 << bit)) for i in range(lax.axis_size(axis))]
        if axis == "dp":
            name = "x" if bit else None
        else:
            name = "y" if bit < bits_of("grp") // 2 else "z"
        past = self.past.setdefault(name, [])
        depth = 1 if name == "x" and len(past) < bits_of("dp") else self.depth.get(name, 0)
        if 0 < depth <= len(past):
            tensor = tie(tensor, past[-depth])
        past.append(lax.ppermute(tensor, axis, pairs))
        return past[-1]


def over_call(body, outs, args):
    return kernel_call(body, outs, [VMEM] * len(args), args, (), 16, 1.5)


class Order:
    def __init__(self):
        self.tokens = ()

    def after(self, tensor):
        return tie(tensor, *self.tokens) if self.tokens else tensor

    def done(self, *tokens):
        self.tokens = tokens

    def also(self, token):
        self.tokens += (token,)


class Sum:
    def __init__(self, run, links, tiled, keep, send, order, left):
        self.run, self.links, self.tiled, self.keep, self.send = run, links, tiled, keep, send
        self.order = list(order)
        self.left = [bit for bit in left if bit != order[0]]
        self.folded = True

    def move(self):
        self.got = self.links.swap(self.send, *self.order.pop(0))
        self.folded = False

    def fold(self):
        if self.folded:
            return
        self.folded = True
        bit = self.order[0]
        place = len(self.left) - 1 - self.left.index(bit)
        self.left.remove(bit)
        if self.tiled:
            self.keep, self.send = split_sum(*bit, place, self.run.after(self.keep), self.got)
        else:
            total = to_low(wide(self.keep) + wide(self.got))
            self.keep, self.send = split(total, *bit, place)
        self.run.done(self.send)

    def step(self):
        self.fold()
        self.move()

    def last(self):
        while self.order:
            self.step()

    def terms(self):
        return self.keep[0], self.got[0]


def split(tensor, axis, bit, place):
    mine = (lax.axis_index(axis) >> bit) & 1
    parts = tensor.reshape((-1, 2, 1 << place) + tensor.shape[1:])
    halves_of = [
        lax.dynamic_index_in_dim(parts, i, 1, keepdims=False).reshape((-1,) + tensor.shape[1:])
        for i in (mine, 1 - mine)
    ]
    return halves_of


def gather_near(links, tensor, axis, before=()):
    blocks = {0: tensor}
    for bit in range(bits_of(axis) - 1, -1, -1):
        for far in list(blocks):
            block = tie(blocks[far], *before) if far and not bit and before else blocks[far]
            blocks[far ^ (1 << bit)] = links.swap(block, axis, bit)
    return [blocks[i] for i in range(len(blocks))]


def in_order(blocks, axis):
    me = lax.axis_index(axis)
    blocks = jnp.stack(blocks)
    return jnp.stack(
        [lax.dynamic_index_in_dim(blocks, i ^ me, 0, keepdims=False) for i in range(blocks.shape[0])]
    )


def per_device(
    tokens,
    condition,
    bucket,
    live_mask,
    routes,
    bucket_table,
    ada_weight,
    ada_bias,
    qkv_weight,
    proj_weight,
    shared_up,
    shared_down,
    router_weight,
    expert_up,
    expert_down,
    cotangent,
):
    tokens, routes, cotangent = tokens[0], routes[0], cotangent[0]
    rows, width = tokens.shape
    members, groups = lax.axis_size("dp"), lax.axis_size("grp")
    me, group = lax.axis_index("dp"), lax.axis_index("grp")
    experts = expert_up.shape[0] * members
    hidden = shared_up.shape[1]
    table_rows = bucket_table.shape[0]
    seen_rows = members * rows
    y_first = tuple(range(bits_of("grp")))
    z_first = y_first[1:] + y_first[:1]
    y_first, z_first = [tuple(("grp", bit) for bit in bits) for bits in (y_first, z_first)]
    all_left = tuple(("dp", bit) for bit in range(bits_of("dp") - 1, 0, -1)) + y_first[::-1]
    all_order = tuple(("dp", bit) for bit in range(bits_of("dp"))) + y_first

    links, run = Links(), Order()
    cotangents = gather_near(links, cotangent, "dp")

    extra = -(-(2 * experts + 2) // 16) * 16
    saved = [
        like((rows, width), low),
        like((rows, 3 * width), low),
        like((rows, LANES), full),
        like((rows, width), low),
        like((rows, width), full),
        like((rows, width), full),
    ]
    (
        packed,
        gates,
        modulation,
        conditioned,
        activated,
        attn_in,
        projected,
        logs,
        attended,
        attn_out,
        middle,
    ) = kernel_call(
        attend_body,
        [
            like((rows + extra, width), low),
            like((rows, LANES), full),
            like((1, 6 * width), full),
            like((1, width), full),
            like((1, width), low),
        ]
        + saved,
        [VMEM, VMEM, SMEM, SMEM] + [VMEM] * 4 + [HBM] * 3,
        (
            tokens,
            condition,
            bucket,
            live_mask,
            routes.T,
            bucket_table,
            ada_bias.reshape(-1, LANES),
            router_weight.T,
            ada_weight,
            qkv_weight,
            proj_weight,
        ),
        [pltpu.VMEM(out.shape, out.dtype) for out in saved]
        + [
            pltpu.VMEM(ada_weight.shape, low),
            pltpu.VMEM(qkv_weight.shape, low),
            pltpu.VMEM(proj_weight.shape, low),
            pltpu.SemaphoreType.DMA((4 + len(saved),)),
        ],
        MOST,
        10,
        [VMEM] * 5 + [HBM] * len(saved),
    )


    part = hidden // (groups * members)
    cut = hidden // (groups * CHUNKS)
    tiled = cut % LANES == 0
    if tiled:
        run.done(gates)
        [part_up] = kernel_call(
            functools.partial(pick_body, members),
            [like((width, groups * part), low)],
            [VMEM],
            (run.after(shared_up),),
            (),
            20,
            4,
        )
        part_down = shared_down
    else:
        part_up = lax.dynamic_index_in_dim(
            shared_up.reshape(width, groups, members, part), me, 2, keepdims=False
        ).reshape(width, groups * part)
        part_down = lax.dynamic_index_in_dim(
            shared_down.reshape(groups, members, part, width), me, 1, keepdims=False
        ).reshape(groups * part, width)
        sides = lambda tensor, place: jnp.concatenate(
            [
                lax.dynamic_index_in_dim(tensor, side, place + 1, keepdims=False)
                for side in (1 - group % 2, group % 2)
            ],
            axis=place,
        )
        own_ups = sides(expert_up[0].reshape(width, groups // 2, 2, CHUNKS, cut), 1)
        own_downs = sides(expert_down[0].reshape(groups // 2, 2, CHUNKS, cut, width), 0)
        ups = [own_ups[:, :, i].reshape(width, groups * cut) for i in range(CHUNKS)]
        downs = [own_downs[:, i].reshape(groups * cut, width) for i in range(CHUNKS)]
    share = width // groups
    packs = gather_near(links, packed, "dp", (part_up,))
    def sum_of(keep, send, order):
        return Sum(run, links, tiled, keep, send, order, y_first[::-1])

    def room(columns, step):
        return [
            pltpu.VMEM((seen_rows, columns), low),
            pltpu.VMEM((seen_rows, columns), low),
            pltpu.VMEM((groups // 2, share, columns), low),
            pltpu.VMEM((groups // 2, share, columns), low),
        ]

    ups_first = [z_first, y_first, z_first, y_first]
    columns = groups * part
    halved = [like((groups // 2, share, columns), low)] * 2
    patches = pltpu.VMEM((seen_rows, width), low)
    down_halved = [like((groups // 2, part, width), low)] * 2
    if not tiled:
        down_halved = [like((columns, width), low)] * 2
    seen, routed_grads, gate, up_keep, up_send, down_keep, down_send, *kept = kernel_call(
        functools.partial(shared_body, ups_first[0][0][1], members, rows, experts, tiled),
        [
            like((seen_rows, width), low),
            like((seen_rows, width), low),
            like((seen_rows, LANES), full),
        ]
        + halved
        + down_halved
        + [like((seen_rows, columns), low)] * 2,
        [HBM] * (2 * members + 2),
        (*packs, *cotangents, part_up, part_down),
        [
            pltpu.VMEM((members, rows + extra, width), low),
            pltpu.VMEM((members, rows, width), low),
            pltpu.VMEM((width, columns), low),
            pltpu.VMEM((columns, width), low),
            patches,
            patches,
            patches,
            pltpu.VMEM((seen_rows, LANES), full),
        ]
        + room(columns, 384)
        + [pltpu.VMEM(out.shape, low) for out in down_halved]
        + [
            pltpu.VMEM((width, 384), full),
            pltpu.SemaphoreType.DMA((64,)),
        ],
        MOST,
        9,
        [HBM] * 9,
    )
    acts, pres = [kept[0]], [kept[1]]
    run.done(gate)
    sums = {"su": sum_of(up_keep, up_send, ups_first[0])}
    sums["su"].move()
    if not tiled:
        down_keep, down_send = split(down_keep.reshape(groups, part, width), "grp", 0, 0)
    sums["sd"] = sum_of(down_keep, down_send, y_first)
    sums["sd"].move()
    columns = groups * cut
    halved = [like((groups // 2, share, columns), low)] * 2
    halved += [like((groups // 2, cut, width), low)] * 2
    block = seen_rows if members == 4 else rows
    slab = (groups // 2, share * columns // LANES + cut * width // LANES, LANES)
    for i in range(CHUNKS - 1):
        one = tiled and i == 0
        if i == 1:
            sums["su"].step()
            sums["sd"].step()
            if tiled:
                sums["e0"].move()
            else:
                sums["u0"].move()
                sums["d0"].move()
        *outs, act, grad_pre = kernel_call(
            functools.partial(routed_body, ups_first[1 + i][0][1], i, block, tiled, one),
            ([like(slab, low)] * 2 if one else halved) + [like((seen_rows, columns), low)] * 2,
            [HBM] * 4,
            (
                run.after(seen),
                routed_grads,
                *((expert_up, expert_down) if tiled else (ups[i], downs[i])),
            ),
            [
                patches,
                patches,
                pltpu.VMEM((width, columns), low),
                pltpu.VMEM((columns, width), low),
                pltpu.VMEM((seen_rows, columns), low),
                pltpu.VMEM((seen_rows, columns), low),
                pltpu.VMEM((width, columns // 2), full),
            ]
            + [pltpu.VMEM(out.shape, low) for out in ([like(slab, low)] * 2 if one else halved)]
            + [pltpu.SemaphoreType.DMA((64,))],
            MOST,
            10,
            [HBM] * (4 if one else 6),
        )
        if one:
            sums["e0"] = sum_of(outs[1], outs[0], y_first)
        else:
            sums["u%d" % i] = sum_of(outs[1], outs[0], ups_first[1 + i])
            sums["d%d" % i] = sum_of(outs[3], outs[2], y_first)
        acts.append(act)
        pres.append(grad_pre)
        run.done(grad_pre)
    sums["sd"].step()
    sums["su"].fold()
    sums["u1"].move()
    sums["d1"].move()
    (
        up_keep,
        up_send,
        down_keep,
        down_send,
        back_keep,
        back_send,
        mixed_keep,
        mixed_send,
    ) = kernel_call(
        functools.partial(
            result_body, ups_first[-1][0][1], members, rows, block, experts, tiled
        ),
        halved
        + [like((seen_rows // 2, width + LANES), low)] * 2
        + [like((seen_rows // 2, width), low)] * 2,
        [HBM] * (2 * CHUNKS + (4 if tiled else 2 * (1 + CHUNKS)) + 3),
        (
            *acts,
            *pres,
            *(
                (part_up, part_down, expert_up, expert_down)
                if tiled
                else (part_up, *ups, part_down, *downs)
            ),
            run.after(seen),
            routed_grads,
            gate,
        ),
        [pltpu.VMEM(a.shape, low) for a in acts]
        + [pltpu.VMEM((seen_rows, columns), low)]
        + [pltpu.VMEM(a.shape, low) for a in pres]
        + [pltpu.VMEM((seen_rows, columns), low)]
        + [pltpu.VMEM((width, groups * part), low)]
        + [pltpu.VMEM((width, columns), low)] * CHUNKS
        + [pltpu.VMEM((groups * part, width), low)]
        + [pltpu.VMEM((columns, width), low)] * CHUNKS
        + [
            patches,
            patches,
            pltpu.VMEM((seen_rows, LANES), full),
            pltpu.VMEM((seen_rows, width + LANES), low),
        ]
        + room(columns, 0)[2:]
        + [
            pltpu.VMEM((groups // 2, cut, width), low),
            pltpu.VMEM((groups // 2, cut, width), low),
            pltpu.VMEM((width, columns // 2), full),
            pltpu.SemaphoreType.DMA((160,)),
        ],
        MOST if members == 4 else 61,
        24,
        [HBM] * 8,
    )
    sums["u2"] = sum_of(up_keep, up_send, ups_first[-1])
    sums["d2"] = sum_of(down_keep, down_send, y_first)
    run.done(back_send)

    def fold_near(keep, got):
        keep, got = [t.reshape(-1, rows, t.shape[-1]) for t in (keep, got)]
        keep, send = even_odd_sum(run.after(keep), got)
        run.done(send)
        return keep, send

    def joined(*names):
        first, *others = [sums.pop(name) for name in names]
        bit = first.order[0]
        place = len(first.left) - 1 - first.left.index(bit)
        pairs = [(run.after(first.keep), first.got), *((o.keep, o.got) for o in others)]
        keep, send = slab_join(*bit, place, *pairs)
        run.done(send)
        found = Sum(run, links, tiled, keep, send, first.order, first.left)
        found.left = [b for b in first.left if b != bit]
        return found

    for name in ("sd", "u1", "d1"):
        run.also(sums[name].got)
    if tiled:
        sums["ed"] = joined("e0", "d1")
    back_keep, back_send, mixed_keep, mixed_send = [
        run.after(t) for t in (back_keep, back_send, mixed_keep, mixed_send)
    ]
    for name in ("u2", "d2"):
        sums[name].keep, sums[name].send = [
            run.after(t) for t in (sums[name].keep, sums[name].send)
        ]
    back_got = links.swap(back_send, "dp", 0)
    if tiled:
        sums["ed"].move()
    for bit in range(1, bits_of("dp")):
        back_keep, back_send = fold_near(back_keep, back_got)
        back_got = links.swap(back_send, "dp", bit)
    sums["u1"].step()
    sums["u2"].move()
    mixed_got = links.swap(mixed_send, "dp", 0)
    for bit in range(1, bits_of("dp")):
        mixed_keep, mixed_send = fold_near(mixed_keep, mixed_got)
        mixed_got = links.swap(mixed_send, "dp", bit)

    def row_parts(columns):
        if tiled:
            return [like((members // 2 * groups, share // members, columns), low)] * 2
        return [like((width, columns), low)] * 2

    proj_keep, proj_send, grad_attended, grad_middle, mix_pieces = kernel_call(
        middle_back_body,
        row_parts(width + LANES)
        + [
            like((rows, width), low),
            like((rows, width), full),
            like((8, width), full),
        ],
        [VMEM] * 7 + [SMEM] + [VMEM] * 4,
        (
            run.after(back_keep[0]),
            back_got[0],
            packed,
            middle,
            modulation,
            gates,
            cotangent,
            live_mask,
            attn_out,
            attended,
            proj_weight,
            router_weight.T,
        ),
        [pltpu.VMEM((width, width + LANES), full)],
        K3A,
        4,
    )
    run.done(mix_pieces)

    def all_sum(keep, send, order):
        if not tiled:
            columns = keep.shape[1]
            tensor = keep.reshape(groups, members, -1, columns)
            tensor = tensor.swapaxes(0, 1).reshape(members * groups, -1, columns)
            keep, send = split(tensor, "dp", 0, bits_of("grp"))
        found = Sum(run, links, tiled, keep, send, order, all_left)
        found.move()
        return found

    sums["d2"].move()
    grad_tokens, keeps, sends, value_keep, value_send, attn_pieces = kernel_call(
        attend_back_body,
        [like((rows, width), full)]
        + row_parts(2 * width)
        + row_parts(width)
        + [like((8, width), full)],
        [VMEM] * 4 + [HBM] * 4,
        (run.after(grad_attended), projected, logs, modulation, attn_in, tokens, grad_middle, qkv_weight),
        [
            pltpu.VMEM((rows, 3 * width), low),
            pltpu.VMEM((width, width), full),
            pltpu.VMEM(qkv_weight.shape, low),
        ]
        + [pltpu.VMEM(out.shape, low) for out in row_parts(2 * width) + row_parts(width)]
        + [
            pltpu.VMEM((rows, width), low),
            pltpu.VMEM((rows, width), low),
            pltpu.VMEM((rows, width), full),
            pltpu.SemaphoreType.DMA((16,)),
        ],
        MOST,
        8,
        [VMEM] + [HBM] * 4 + [VMEM],
    )
    run.done(attn_pieces)
    run.also(mixed_got)
    for name in ("u1", "u2", "d2"):
        run.also(sums[name].got)
    if tiled:
        sums["ed"].fold()
    proj_keep, proj_send, keeps, sends, value_keep, value_send, attn_pieces = [
        run.after(t)
        for t in (proj_keep, proj_send, keeps, sends, value_keep, value_send, attn_pieces)
    ]
    turned = (all_order[0], y_first[0], *all_order[1:-len(y_first)], *y_first[1:])
    sums["p"] = all_sum(proj_keep, proj_send, all_order)
    sums["v"] = all_sum(value_keep, value_send, all_order)
    sums["qk"] = all_sum(keeps, sends, turned)
    if tiled:
        sums["ed"].move()
        sums["ud"] = joined("u2", "d2")
        sums["ud"].move()
        p, v = sums.pop("p"), sums.pop("v")
        bit = v.order[0]
        place = len(v.left) - 1 - v.left.index(bit)
        keep, send = join_sum(*bit, place, (run.after(p.keep), p.got), (v.keep, v.got))
        run.done(send)
        sums["pv"] = Sum(run, links, tiled, keep, send, v.order, v.left)
        sums["pv"].move()
    sums["qk"].step()
    mixed_out, factors, grad_condition, table_part = kernel_call(
        condition_body,
        [
            like((rows, width), low),
            like((8, width), low),
            like((1, width), full),
            like((table_rows // groups, width), full),
        ],
        [VMEM] * 5 + [SMEM] + [VMEM] * 4 + [SMEM, HBM],
        (
            run.after(mixed_keep[0]),
            mixed_got[0],
            middle,
            modulation,
            cotangent,
            live_mask,
            attn_pieces,
            mix_pieces,
            conditioned,
            activated,
            bucket,
            ada_weight,
        ),
        [pltpu.VMEM(ada_weight.shape, low), pltpu.SemaphoreType.DMA],
        K4,
        4,
    )

    run.done(factors)

    factors = factors[None]

    def widen(factors, axis, bit):
        return jnp.concatenate([factors, links.swap(factors, axis, bit)], axis=0)

    if tiled:
        sums["pv"].step()
        sums["qk"].step()
        factors = widen(factors, "dp", 0)
        table_part = table_part + links.swap(table_part, "dp", 0)
        pv, qk = sums["pv"], sums["qk"]
        bit = qk.order[0]
        place = len(qk.left) - 1 - qk.left.index(bit)
        keep, send = join_sum(*bit, place, (run.after(pv.keep), pv.got), (qk.keep, qk.got))
        run.done(send)
        both = sum_of(keep, send, qk.order)
        both.left = [b for b in qk.left if b != bit]
        both.move()
        run.also(sums["ed"].got)
        sums["ud"].step()
        sums["su"].send, factors, table_part = [
            run.after(t) for t in (sums["su"].send, factors, table_part)
        ]
        both.step()
        sums["su"].move()
        factors = widen(factors, "dp", 1)
        factors = widen(factors, "grp", 0)
        sums["u1"].step()
        sums["sd"].last()
        [shared_total] = over_call(
            stack_body,
            [like((share + hidden // (groups * members), width), low)],
            (run.after(sums["su"].terms()[0]), sums["su"].terms()[1], *sums["sd"].terms()),
        )
        run.done(shared_total)
        shared_blocks = gather_near(links, shared_total, "dp")
        table_part = table_part + links.swap(table_part, "dp", 1)
        factors = widen(factors, "grp", 2)
        run.also(sums["u1"].got)
        up_part, down_part = over_call(
            functools.partial(shared_end_body, members),
            [like((share, hidden), full), like((hidden // groups, width), full)],
            (run.after(shared_blocks[0]), *shared_blocks[1:]),
        )
        run.done(down_part)
        [total] = over_call(
            sum_body, [like(both.terms()[0].shape, low)], (run.after(both.terms()[0]), both.terms()[1])
        )
        run.done(total)
        all_blocks = gather_near(links, total, "dp")
        factors = widen(factors, "grp", 1)
        ends = [t for name in ("ed", "u1", "ud") for t in sums[name].terms()]
        [expert_up_part] = over_call(
            own_up_body, [like((share, hidden), full)], (run.after(ends[0]), *ends[1:])
        )
        run.done(expert_up_part)
        ends = [t for name in ("ed", "ud") for t in sums[name].terms()]
        [expert_down_part] = over_call(
            functools.partial(own_down_body, share * columns // LANES),
            [like((hidden // groups, width), full)],
            (run.after(ends[0]), *ends[1:]),
        )
        proj_part, router_part, *ends = over_call(
            functools.partial(rows_end_body, members),
            [like((share, n), full) for n in (width, LANES, width, 2 * width)],
            all_blocks,
        )
        qkv_part = jnp.concatenate([ends[1], ends[0]], axis=1)
    else:
        for bit in range(1, bits_of("dp")):
            factors = widen(factors, "dp", bit)
            table_part = table_part + links.swap(table_part, "dp", bit)
        factors = widen(factors, "dp", 0)
        table_part = table_part + links.swap(table_part, "dp", 0)
        sums["su"].move()
        for each in sums.values():
            each.last()
        for bit in range(bits_of("grp")):
            factors = widen(factors, "grp", bit)
        total = lambda name: wide(sums[name].terms()[0]) + wide(sums[name].terms()[1])
        ends = {
            name: gather_near(links, to_low(total(name)), "dp")
            for name in ("su", "sd", "p", "v", "qk")
        }
        up_part = wide(in_order(ends["su"], "dp")).reshape(members, share, groups, part)
        up_part = up_part.transpose(1, 2, 0, 3).reshape(share, hidden)
        down_part = wide(in_order(ends["sd"], "dp")).reshape(hidden // groups, width)
        own_ups = [total("u%d" % i).reshape(share, 2, groups // 2, cut) for i in range(CHUNKS)]
        expert_up_part = jnp.stack(own_ups, axis=3).transpose(0, 2, 1, 3, 4).reshape(share, hidden)
        expert_down_part = jnp.concatenate([total("d%d" % i) for i in range(CHUNKS)], axis=0)
        qkv_part = jnp.concatenate(
            [wide(in_order(ends[n], "dp")).reshape(share, -1) for n in ("qk", "v")], axis=1
        )
        proj_part = wide(in_order(ends["p"], "dp")).reshape(share, width + LANES)
        proj_part, router_part = jnp.split(proj_part, [width], axis=1)
    left = lax.dynamic_slice_in_dim(factors[:, 6], group * share, share, axis=1)
    right = factors[:, :6].reshape(-1, 6 * width)
    ada_w_part = product_tn(left, right)
    ada_share = 6 * width // groups
    ada_b_part = lax.dynamic_slice_in_dim(jnp.sum(wide(right), axis=0), group * ada_share, ada_share)
    return (
        mixed_out[None],
        grad_tokens[None],
        grad_condition,
        table_part,
        ada_w_part,
        ada_b_part,
        qkv_part,
        proj_part,
        up_part,
        down_part,
        router_part[:, :experts],
        expert_up_part[None],
        expert_down_part[None],
    )


def solution(mesh):
    in_specs = (
        P(("grp", "dp"), None, None),
        P(("grp", "dp"), None),
        P(("grp", "dp")),
        P(("grp", "dp")),
        P(("grp", "dp"), None, None),
        P(),
        P(),
        P(),
        P(),
        P(),
        P(),
        P(),
        P(),
        P("dp", None, None),
        P("dp", None, None),
        P(("grp", "dp"), None, None),
    )
    out_specs = (
        P(("grp", "dp"), None, None),
        P(("grp", "dp"), None, None),
        P(("grp", "dp"), None),
        P("grp", None),
        P("grp", None),
        P("grp"),
        P("grp", None),
        P("grp", None),
        P("grp", None),
        P("grp", None),
        P("grp", None),
        P("dp", "grp", None),
        P("dp", "grp", None),
    )
    return jax.shard_map(
        per_device, mesh=mesh, in_specs=in_specs, out_specs=out_specs, check_vma=False
    )
```

```python
import functools
import math

import jax
import jax.numpy as jnp
from jax import lax
from jax.experimental import pallas as pl
from jax.experimental.pallas import tpu as pltpu
from jax.sharding import PartitionSpec as P

HEADS = 12
LANES = 128
CHUNKS = 3
PEAK = 1.15e9
WEIGH = 0.3
MOST = 58
K3A = 20
K4 = 58
FOLD = 20
SLAB = 58


EPSILON = 1e-06
CURVE = math.sqrt(2.0 / math.pi)
CUBIC = 0.044715

low, full = jnp.bfloat16, jnp.float32
VMEM = pl.BlockSpec(memory_space=pltpu.VMEM)
SMEM = pl.BlockSpec(memory_space=pltpu.SMEM)
HBM = pl.BlockSpec(memory_space=pltpu.MemorySpace.HBM)


def product(left_mat, right_mat, left_dim=1, right_dim=0):
    return lax.dot_general(
        left_mat,
        right_mat,
        (((left_dim,), (right_dim,)), ((), ())),
        preferred_element_type=jnp.float32,
    )


def product_nt(left_mat, right_mat):
    return product(left_mat, right_mat, 1, 1)


def product_tn(left_mat, right_mat):
    return product(left_mat, right_mat, 0, 0)


def to_low(tensor):
    return tensor.astype(low)


def wide(tensor):
    return tensor.astype(full)


def like(shape, kind):
    return jax.ShapeDtypeStruct(shape, kind)


def kernel_call(
    body, outs, in_specs, args, scratch=(), megabytes=24, microseconds=1, out_specs=None
):
    return pl.pallas_call(
        body,
        out_shape=outs,
        in_specs=in_specs,
        out_specs=out_specs or [VMEM] * len(outs),
        scratch_shapes=list(scratch),
        compiler_params=pltpu.CompilerParams(vmem_limit_bytes=megabytes << 20),
        cost_estimate=pl.CostEstimate(
            flops=int(microseconds * PEAK * WEIGH), bytes_accessed=0, transcendentals=0
        ),
    )(*args)


def normalize(tensor):
    average = jnp.mean(tensor, axis=-1, keepdims=True)
    centered = tensor - average
    inverse = lax.rsqrt(jnp.mean(centered * centered, axis=-1, keepdims=True) + EPSILON)
    return (centered * inverse, inverse)


def normalize_back(gradient, normed, inverse):
    first_term = jnp.mean(gradient, axis=-1, keepdims=True)
    second_term = jnp.mean(gradient * normed, axis=-1, keepdims=True)
    return inverse * (gradient - first_term - normed * second_term)


def column_sum(tensor):
    return jnp.sum(tensor, axis=0, keepdims=True)


def gelu_pair(pre):
    square = pre * pre
    bend = jnp.tanh(CURVE * (pre + CUBIC * pre * square))
    half = 0.5 + 0.5 * bend
    slope = half + (0.5 * CURVE) * pre * (1.0 - bend * bend) * (1.0 + 3.0 * CUBIC * square)
    return pre * half, slope


def halves(width):
    lane = lax.broadcasted_iota(jnp.int32, (1, LANES), 1)
    return [lane // width == i for i in range(LANES // width)]


def attend_body(
    tokens,
    condition,
    bucket,
    live,
    routes,
    table,
    ada_bias,
    router,
    ada_hbm,
    qkv_hbm,
    proj_hbm,
    packed,
    gates_out,
    modulation_out,
    conditioned_out,
    activated_out,
    attn_in_hbm,
    projected_hbm,
    log_hbm,
    attended_hbm,
    attn_out_hbm,
    middle_hbm,
    attn_in_out,
    projected_out,
    log_out,
    attended_out,
    attn_out_out,
    middle_out,
    ada,
    qkv,
    proj,
    sems,
):
    rows, width = tokens.shape
    experts = router.shape[0]
    leaving = []

    def leave(source, target):
        copy = pltpu.make_async_copy(source, target, sems.at[4 + len(leaving)])
        copy.start()
        leaving.append(copy)

    head = width // HEADS
    scaling = float(head) ** (-0.5)
    early = 2 * width
    copies = [
        pltpu.make_async_copy(ada_hbm.at[:, :early], ada.at[:, :early], sems.at[0]),
        pltpu.make_async_copy(qkv_hbm, qkv, sems.at[1]),
        pltpu.make_async_copy(ada_hbm.at[:, early:], ada.at[:, early:], sems.at[2]),
        pltpu.make_async_copy(proj_hbm, proj, sems.at[3]),
    ]
    for copy in copies:
        copy.start()

    named = lax.broadcasted_iota(jnp.int32, (table.shape[0], 1), 0) == bucket[0]
    conditioned = wide(condition[...]) + column_sum(jnp.where(named, wide(table[...]), 0.0))
    activated = to_low(conditioned * (1.0 / (1.0 + jnp.exp(-conditioned))))
    conditioned_out[...] = conditioned
    activated_out[...] = activated
    activated = jnp.broadcast_to(activated, (16, width))

    bias = wide(ada_bias[...])
    bias = jnp.concatenate([bias[i : i + 1] for i in range(bias.shape[0])], axis=1)
    inputs = wide(tokens[...])
    normed, _ = normalize(inputs)
    copies[0].wait()
    modulation_out[:, :early] = product(activated, ada[:, :early])[:1] + bias[:, :early]
    shift_attn = modulation_out[:, :width]
    scale_attn = modulation_out[:, width:early]
    attn_in = to_low(normed * (1.0 + scale_attn) + shift_attn)
    attn_in_out[...] = attn_in
    leave(attn_in_out, attn_in_hbm)
    copies[1].wait()
    projected_out[...] = to_low(product(attn_in, qkv[...]))
    leave(projected_out, projected_hbm)
    copies[2].wait()
    modulation_out[:, early:] = product(activated, ada[:, early:])[:1] + bias[:, early:]

    masks = halves(head)
    column = lax.broadcasted_iota(jnp.int32, (1, LANES), 1)
    logs = jnp.zeros((rows, LANES), full)
    for block in range(width // LANES):
        at = pl.ds(block * LANES, LANES)
        query = projected_out[:, at]
        key = projected_out[:, pl.ds(width + block * LANES, LANES)]
        value = projected_out[:, pl.ds(2 * width + block * LANES, LANES)]
        total = jnp.zeros((rows, LANES), full)
        for i, mask in enumerate(masks):
            scores = product_nt(jnp.where(mask, query, jnp.zeros_like(query)), key) * scaling
            top = jnp.max(scores, axis=-1, keepdims=True)
            raised = jnp.exp(scores - top)
            whole = jnp.sum(raised, axis=-1, keepdims=True)
            probs = to_low(raised / whole)
            logs = jnp.where(column == block * len(masks) + i, top + jnp.log(whole), logs)
            total = jnp.where(mask, product(probs, value), total)
        attended_out[:, at] = to_low(total)
    log_out[...] = logs
    leave(log_out, log_hbm)
    leave(attended_out, attended_hbm)

    copies[3].wait()
    attn_out = product(attended_out[...], proj[...])
    attn_out_out[...] = attn_out
    leave(attn_out_out, attn_out_hbm)
    piece = lambda i: modulation_out[:, pl.ds(i * width, width)]
    middle = inputs + piece(2) * attn_out
    middle_out[...] = middle
    leave(middle_out, middle_hbm)
    normed, _ = normalize(middle)
    mix_in = to_low(normed * (1.0 + piece(4)) + piece(3))
    packed[:rows, :] = mix_in

    logits = product_nt(router[...], mix_in)
    ids = lax.broadcasted_iota(jnp.int32, (experts, rows), 0)
    hot = (routes[:1] == ids) | (routes[1:2] == ids)
    top = jnp.max(jnp.where(hot, logits, -jnp.inf), axis=0, keepdims=True)
    turned = jnp.where(hot, jnp.exp(jnp.where(hot, logits, top) - top), 0.0)
    turned = turned / jnp.sum(turned, axis=0, keepdims=True)
    gates_out[...] = jnp.transpose(
        jnp.concatenate([turned, jnp.zeros((LANES - experts, rows), full)], axis=0)
    )
    gate_mix = piece(5) * wide(live[0])
    extra = packed.shape[0] - rows
    high, turned_high = to_low(gate_mix), to_low(turned)
    wall = jnp.zeros((experts, width - rows), full)
    packed[rows:, :] = to_low(
        jnp.concatenate(
            [
                jnp.concatenate([wide(turned_high), wall], axis=1),
                jnp.concatenate([turned - wide(turned_high), wall], axis=1),
                wide(high),
                gate_mix - wide(high),
                jnp.zeros((extra - 2 * experts - 2, width), full),
            ],
            axis=0,
        )
    )
    for copy in leaving:
        copy.wait()


class Mover:
    def __init__(self, sems):
        self.sems, self.count, self.open = sems, 0, []

    def start(self, source, target, keep=True):
        copy = pltpu.make_async_copy(source, target, self.sems.at[self.count])
        copy.start()
        self.count += 1
        if keep:
            self.open.append(copy)
        return copy

    def finish(self):
        for copy in self.open:
            copy.wait()


def wait(copies):
    while copies:
        copies.pop().wait()


def pick_body(members, shared_up, part_up):
    groups = lax.axis_size("grp")
    span = shared_up.shape[1] // groups
    part = span // members
    pick = spread_units(span, part, lax.axis_index("dp"), 0)
    for i in range(0, groups, 4):
        part_up[:, pl.ds(i * part, 4 * part)] = to_low(
            product(shared_up[:, pl.ds(i * span, 4 * span)], pick)
        )


def spread_units(span, part, member, dim):
    shape = (4 * span, 4 * part) if dim == 0 else (4 * part, 4 * span)
    whole = lax.broadcasted_iota(jnp.int32, shape, dim)
    own = lax.broadcasted_iota(jnp.int32, shape, 1 - dim)
    place = own + (own // part) * (span - part) + member * part
    return to_low(jnp.where(whole == place, 1.0, 0.0))


def parted(groups, bit, mine, i):
    return ((i >> bit) << (bit + 1)) + (mine << bit) + (i & ((1 << bit) - 1))


def bring_part_down(mover, members, shared_down, part_down):
    groups = lax.axis_size("grp")
    span = shared_down.shape[0] // groups
    part = span // members
    copies = []
    for i in range(groups):
        start = pl.multiple_of(i * span + lax.axis_index("dp") * part, 16)
        copies.append(
            mover.start(
                shared_down.at[pl.ds(start, part)], part_down.at[pl.ds(i * part, part)], False
            )
        )
    return copies


def bring_cut(mover, chunk, half, expert, own, lanes):
    groups = lax.axis_size("grp")
    span = expert.shape[2 if lanes else 1] // groups
    cut = span // CHUNKS
    side = lax.axis_index("grp") & 1
    copies = []
    for place in range(groups // 2):
        group = 2 * place + (side if half else 1 - side)
        start = pl.multiple_of(group * span + chunk * cut, LANES)
        to = pl.ds((half * groups // 2 + place) * cut, cut)
        if lanes:
            copies.append(mover.start(expert.at[0, :, pl.ds(start, cut)], own.at[:, to], False))
        else:
            copies.append(mover.start(expert.at[0, pl.ds(start, cut)], own.at[to], False))
    return copies


def feed_rows(mover, bit, rows, seen, grads, up, down, act, grad_pre, held, outs, waits, ordered):
    act_out, pre_out, put_up, put_down = outs
    wait_up, wait_down, wait_seen, wait_grads = waits
    groups = lax.axis_size("grp")
    mine = (lax.axis_index("grp") >> bit) & 1
    side = lax.axis_index("grp") & 1
    share = seen.shape[1] // groups
    step = held.shape[1]
    for number, start in enumerate(range(0, up.shape[1], step)):
        at = pl.ds(start, step)
        wait(wait_up[number])
        slopes = []
        for i in range(0, seen.shape[0], rows):
            wait(wait_seen[i // rows])
            raised, slope = gelu_pair(product(seen[pl.ds(i, rows), :], up[:, at]))
            act[pl.ds(i, rows), at] = to_low(raised)
            slopes.append(slope)
            if i == 0:
                wait(wait_down[number])
            wait(wait_grads[i // rows])
            slope = slopes.pop()
            grad_pre[pl.ds(i, rows), at] = to_low(
                slope * product_nt(grads[pl.ds(i, rows), :], down[at, :])
            )
        if act_out is not None:
            mover.start(act.at[:, at], act_out.at[:, at])
            mover.start(grad_pre.at[:, at], pre_out.at[:, at])
        held[...] = product_tn(seen[...], grad_pre[:, at])
        place = (1 - side if number == 0 else side) if ordered else number
        for kind, value in enumerate((1 - mine, mine)):
            rows_of = []
            for i in range(groups // 2):
                first = pl.multiple_of(parted(groups, bit, value, i) * share, 8)
                rows_of.append(to_low(held[pl.ds(first, share)]))
            put_up(kind, place, rows_of)
        put_down(number, at, to_low(product_tn(act[:, at], grads[...])))


def up_putter(mover, send, keep, send_out, keep_out, step):
    def put_up(kind, place, rows_of):
        target, out = ((send, send_out), (keep, keep_out))[kind]
        at = pl.ds(place * step, step)
        if not isinstance(place, int):
            at = pl.ds(pl.multiple_of(place * step, LANES), step)
        for i, value in enumerate(rows_of):
            target[i, :, at] = value
        mover.start(target.at[:, :, at], out.at[:, :, at])

    return put_up


def slab_putters(mover, slabs, slab_outs, step):
    groups, whole, _ = slabs[0].shape
    count = step // LANES

    def put_up(kind, place, rows_of):
        slab, out = slabs[kind], slab_outs[kind]
        share = rows_of[0].shape[0]
        first = pl.multiple_of(place * count * share, 16)
        for i, value in enumerate(rows_of):
            for j in range(count):
                at = pl.ds(pl.multiple_of(first + j * share, 16), share)
                slab[i, at, :] = value[:, j * LANES : (j + 1) * LANES]
        at = pl.ds(first, count * share)
        mover.start(slab.at[:, at], out.at[:, at])

    def put_down(number, at, value):
        slab, out = slabs[number], slab_outs[number]
        cut = value.shape[0] // groups
        first = whole - value.shape[1] // LANES * cut
        for i in range(groups):
            for j in range(value.shape[1] // LANES):
                slab[i, pl.ds(first + j * cut, cut), :] = value[
                    i * cut : (i + 1) * cut, j * LANES : (j + 1) * LANES
                ]
        at = pl.ds(first, whole - first)
        mover.start(slab.at[:, at], out.at[:, at])

    return put_up, put_down


def shared_body(bit, members, rows, experts, tiled, *refs):
    packs_hbm, cotangents_hbm = refs[:members], refs[members : 2 * members]
    (
        up_hbm,
        down_hbm,
        seen_out,
        routed_out,
        gate_out,
        up_keep_out,
        up_send_out,
        down_keep_out,
        down_send_out,
        act_out,
        pre_out,
        packs,
        cotangents,
        up,
        down,
        seen,
        routed_grads,
        grads,
        gate_held,
        act,
        grad_pre,
        up_keep,
        up_send,
        down_keep,
        down_send,
        held,
        sems,
    ) = refs[2 * members :]
    mover = Mover(sems)
    width = seen.shape[1]
    me = lax.axis_index("dp")
    named = lax.broadcasted_iota(jnp.int32, (experts, 1), 0) == me
    pack_copies = [mover.start(p, packs.at[i], False) for i, p in enumerate(packs_hbm)]
    up_copy = mover.start(up_hbm, up, False)
    cotangent_copies = [mover.start(c, cotangents.at[i], False) for i, c in enumerate(cotangents_hbm)]
    if tiled:
        down_copies = bring_part_down(mover, members, down_hbm, down)
    else:
        down_copies = [mover.start(down_hbm, down, False)]
    for i in range(members):
        at = pl.ds(i * rows, rows)
        pack_copies[i].wait()
        seen[at, :] = packs[i, :rows, :]
        extra = wide(packs[i, rows:, :])
        gates = extra[:experts, :rows] + extra[experts : 2 * experts, :rows]
        gate = column_sum(jnp.where(named, gates, 0.0))
        gate = jnp.transpose(jnp.broadcast_to(gate, (LANES, rows)))
        gate_held[at, :] = gate
        gate_mix = extra[2 * experts : 2 * experts + 1] + extra[2 * experts + 1 : 2 * experts + 2]
        cotangent_copies[i].wait()
        mixture_grads = to_low(gate_mix * wide(cotangents[i]))
        grads[at, :] = mixture_grads
        routed_grads[at, :] = to_low(gate[:, :1] * wide(mixture_grads))
    mover.start(seen, seen_out)
    mover.start(routed_grads, routed_out)
    mover.start(gate_held, gate_out)

    side = lax.axis_index("grp") & 1
    groups = lax.axis_size("grp")
    part = up.shape[1] // groups

    def put_down(number, at, value):
        if not tiled:
            down_keep[...] = value
            mover.start(down_keep, down_keep_out)
            return
        count = value.shape[0] // part
        for mine in range(2):

            @pl.when(side == mine)
            def _():
                for i in range(count):
                    g = number * count + i
                    target = down_keep if g & 1 == mine else down_send
                    target[g >> 1] = value[i * part : (i + 1) * part]

        rows_at = pl.ds(number * count // 2, count // 2)
        mover.start(down_keep.at[rows_at], down_keep_out.at[rows_at])
        mover.start(down_send.at[rows_at], down_send_out.at[rows_at])

    blocks = range(seen.shape[0] // rows)
    waits = ([[up_copy], []], [down_copies, []], [[] for _ in blocks], [[] for _ in blocks])
    put_up = up_putter(mover, up_send, up_keep, up_send_out, up_keep_out, held.shape[1])
    outs = (act_out, pre_out, put_up, put_down)
    feed_rows(mover, bit, rows, seen, grads, up, down, act, grad_pre, held, outs, waits, False)
    mover.finish()


def bring_rows(mover, rows, source, target):
    return [
        [mover.start(source.at[pl.ds(i, rows)], target.at[pl.ds(i, rows)], False)]
        for i in range(0, source.shape[0], rows)
    ]


def bring_cut_all(mover, chunk, tiled, up_hbm, down_hbm, up, down, seen, grads, rows):
    if tiled:
        wait_up = [bring_cut(mover, chunk, 0, up_hbm, up, True)]
        wait_seen = bring_rows(mover, rows, *seen)
        wait_down = [bring_cut(mover, chunk, 0, down_hbm, down, False)]
        wait_grads = bring_rows(mover, rows, *grads)
        wait_up.append(bring_cut(mover, chunk, 1, up_hbm, up, True))
        wait_down.append(bring_cut(mover, chunk, 1, down_hbm, down, False))
    else:
        wait_up = [[mover.start(up_hbm, up, False)], []]
        wait_seen = bring_rows(mover, rows, *seen)
        wait_down = [[mover.start(down_hbm, down, False)], []]
        wait_grads = bring_rows(mover, rows, *grads)
    return wait_up, wait_down, wait_seen, wait_grads


def routed_body(bit, chunk, rows, tiled, one, *refs):
    seen_hbm, grads_hbm, up_hbm, down_hbm = refs[:4]
    many = 2 if one else 4
    grad_outs, (act_out, pre_out) = refs[4 : 4 + many], refs[4 + many : 6 + many]
    seen, grads, up, down, act, grad_pre, held = refs[6 + many : 13 + many]
    kept, sems = refs[13 + many : -1], refs[-1]
    mover = Mover(sems)
    waits = bring_cut_all(
        mover, chunk, tiled, up_hbm, down_hbm, up, down, (seen_hbm, seen), (grads_hbm, grads), rows
    )
    if one:
        put_up, put_down = slab_putters(mover, kept, grad_outs, held.shape[1])
    else:
        put_up = up_putter(mover, *kept[:2], *grad_outs[:2], held.shape[1])

        def put_down(number, at, value):
            target, out = kept[2 + number], grad_outs[2 + number]
            target[...] = value.reshape(target.shape)
            mover.start(target, out)

    outs = (act_out, pre_out, put_up, put_down)
    feed_rows(mover, bit, rows, seen, grads, up, down, act, grad_pre, held, outs, waits, True)
    mover.finish()


def result_body(bit, members, rows, block, experts, tiled, *refs):
    parts = 1 + CHUNKS
    acts_hbm, pres_hbm = refs[:CHUNKS], refs[CHUNKS : 2 * CHUNKS]
    given = 4 if tiled else 2 * parts
    weights_hbm = refs[2 * CHUNKS : 2 * CHUNKS + given]
    rest = refs[2 * CHUNKS + given :]
    seen_hbm, grads_hbm, gate_hbm = rest[:3]
    up_keep_out, up_send_out, down_keep_out, down_send_out = rest[3:7]
    back_keep_out, back_send_out, mixed_keep_out, mixed_send_out = rest[7:11]
    scratch, sems = rest[11:-1], rest[-1]
    acts, pres, ups, downs = [scratch[i * parts : (i + 1) * parts] for i in range(4)]
    seen, grads, gate, back, up_keep, up_send, down_keep, down_send, held = scratch[4 * parts :]
    mover = Mover(sems)
    width = grads.shape[1]
    me = lax.axis_index("dp")
    column = lax.broadcasted_iota(jnp.int32, (1, LANES), 1)
    last = CHUNKS - 1
    if tiled:
        up_hbm, down_hbm = weights_hbm[2:]
    else:
        up_hbm, down_hbm = weights_hbm[parts - 1], weights_hbm[2 * parts - 1]
    waits = bring_cut_all(
        mover,
        last,
        tiled,
        up_hbm,
        down_hbm,
        ups[-1],
        downs[-1],
        (seen_hbm, seen),
        (grads_hbm, grads),
        block,
    )

    def bring_weights(kind, targets):
        if not tiled:
            sources = weights_hbm[kind * parts : (kind + 1) * parts]
            return [[mover.start(a, b, False)] for a, b in zip(sources[:-1], targets)]
        part, expert = weights_hbm[kind], weights_hbm[2 + kind]
        if kind:
            found = [bring_part_down(mover, members, part, targets[0])]
        else:
            found = [[mover.start(part, targets[0], False)]]
        for c in range(last):
            found.append(
                bring_cut(mover, c, 0, expert, targets[1 + c], kind == 0)
                + bring_cut(mover, c, 1, expert, targets[1 + c], kind == 0)
            )
        return found

    more = [mover.start(a, b, False) for a, b in zip(acts_hbm, acts)]
    for found in bring_weights(1, downs):
        more += found
    more.append(mover.start(gate_hbm, gate, False))
    later = [mover.start(a, b, False) for a, b in zip(pres_hbm, pres)]
    for found in bring_weights(0, ups):
        later += found

    def put_down(number, at, value):
        target, out = ((down_send, down_send_out), (down_keep, down_keep_out))[number]
        target[...] = value.reshape(target.shape)
        mover.start(target, out)

    put_up = up_putter(mover, up_send, up_keep, up_send_out, up_keep_out, held.shape[1])
    outs = (None, None, put_up, put_down)
    feed_rows(
        mover,
        bit,
        block,
        seen,
        grads,
        ups[-1],
        downs[-1],
        acts[-1],
        pres[-1],
        held,
        outs,
        waits,
        True,
    )
    wait(more)
    mixed = seen
    for i in [*range(1, members, 2), *range(0, members, 2)]:
        at = pl.ds(i * rows, rows)
        to = pl.ds((i // 2) * rows, rows)
        routed = sum(product(a[at, :], d[...]) for a, d in zip(acts[1:], downs[1:]))
        routed = wide(to_low(routed))
        mixed[at, :] = to_low(product(acts[0][at, :], downs[0][...]) + gate[at, :1] * routed)
        mover.start(mixed.at[at], (mixed_send_out if i % 2 else mixed_keep_out).at[to])
        weighed = jnp.sum(wide(grads[at, :]) * routed, axis=1, keepdims=True)
        high = wide(to_low(weighed))
        back[at, width:] = to_low(
            jnp.where(column == me, high, 0.0)
            + jnp.where(column == experts + me, weighed - high, 0.0)
        )
        wait(later)
        back[at, :width] = to_low(sum(product_nt(p[at, :], u[...]) for p, u in zip(pres, ups)))
        mover.start(back.at[at], (back_send_out if i % 2 else back_keep_out).at[to])
    mover.finish()


def middle_back_body(
    kept,
    got,
    packed,
    middle,
    modulation,
    gates,
    cotangent,
    live,
    attn_out,
    attended,
    proj,
    router,
    proj_keep,
    proj_send,
    grad_attended,
    grad_middle_out,
    grad_pieces,
    held,
):
    rows, width = cotangent.shape
    experts = router.shape[0]
    piece = lambda i: modulation[:, pl.ds(i * width, width)]
    back = wide(kept[:, width:]) + wide(got[:, width:])
    weighed = back[:, :experts] + back[:, experts : 2 * experts]
    mine = gates[:, :experts]
    grad_logits = to_low(weighed - mine * jnp.sum(weighed, axis=1, keepdims=True))
    mix_in = packed[:rows, :]
    grad_mix_in = wide(kept[:, :width]) + wide(got[:, :width])
    grad_mix_in = grad_mix_in + product(grad_logits, router[...])
    normed, inverse = normalize(middle[...])
    grad_result = wide(cotangent[...]) * wide(live[0])
    grad_middle = grad_result + normalize_back(grad_mix_in * (1.0 + piece(4)), normed, inverse)
    grad_middle_out[...] = grad_middle
    grad_attn_out = to_low(piece(2) * grad_middle)
    held[:, width:] = jnp.zeros((width, LANES), full)
    held[:, width : width + experts] = product_tn(mix_in, grad_logits)
    held[:, :width] = product_tn(attended[...], grad_attn_out)
    part_rows(held, proj_keep, proj_send, slice(None))
    grad_attended[...] = to_low(product_nt(grad_attn_out, proj[...]))
    grad_pieces[0:1] = column_sum(grad_middle * attn_out[...])
    grad_pieces[1:2] = column_sum(grad_mix_in)
    grad_pieces[2:3] = column_sum(grad_mix_in * normed)


def part_rows(held, keep, send, at):
    groups, members = lax.axis_size("grp"), lax.axis_size("dp")
    share = held.shape[0] // (groups * members)
    if len(keep.shape) == 2:
        keep[:, at] = to_low(held[...])
        return
    mine = lax.axis_index("dp") & 1
    for target, value in ((send, 1 - mine), (keep, mine)):
        for i in range(members // 2):
            for g in range(groups):
                first = pl.multiple_of((g * members + 2 * i + value) * share, 8)
                target[i * groups + g, :, at] = to_low(held[pl.ds(first, share)])


def attend_back_body(
    grad_attended,
    projected,
    logs,
    modulation,
    attn_in_hbm,
    tokens_hbm,
    grad_middle_hbm,
    qkv_hbm,
    grad_tokens,
    keep_outs,
    send_outs,
    value_keep_out,
    value_send_out,
    grad_pieces,
    grad_projected,
    held,
    qkv,
    keeps,
    sends,
    value_keep,
    value_send,
    attn_in,
    tokens,
    grad_middle,
    sems,
):
    rows, width = tokens.shape
    head = width // HEADS
    scaling = float(head) ** (-0.5)
    mover = Mover(sems)
    attn_copy = mover.start(attn_in_hbm, attn_in, False)
    late = [
        mover.start(a, b, False)
        for a, b in ((qkv_hbm, qkv), (tokens_hbm, tokens), (grad_middle_hbm, grad_middle))
    ]
    masks = halves(head)
    column = lax.broadcasted_iota(jnp.int32, (1, LANES), 1)
    for block in range(width // LANES):
        parts = [pl.ds(i * width + block * LANES, LANES) for i in range(3)]
        query, key, value = [projected[:, at] for at in parts]
        grads = grad_attended[:, parts[0]]
        grad_query, grad_key, grad_value = [jnp.zeros((rows, LANES), full)] * 3
        for i, mask in enumerate(masks):
            zero = jnp.zeros_like(query)
            scores = product_nt(jnp.where(mask, query, zero), key) * scaling
            log = jnp.sum(
                jnp.where(column == block * len(masks) + i, logs[...], 0.0), axis=1, keepdims=True
            )
            probs = jnp.exp(scores - log)
            grad_probs = product_nt(jnp.where(mask, grads, zero), value)
            grad_value = jnp.where(mask, product_tn(to_low(probs), grads), grad_value)
            drift = jnp.sum(probs * grad_probs, axis=-1, keepdims=True)
            grad_scores = to_low(probs * (grad_probs - drift))
            grad_query = jnp.where(mask, product(grad_scores, key), grad_query)
            grad_key = jnp.where(mask, product_tn(grad_scores, query), grad_key)
        for at, grad in zip(parts, (grad_query * scaling, grad_key * scaling, grad_value)):
            grad_projected[:, at] = to_low(grad)
    attn_copy.wait()
    for i in range(3):
        at = pl.ds(i * width, width)
        held[...] = product_tn(attn_in[...], grad_projected[:, at])
        pairs = [(keeps, keep_outs), (sends, send_outs)]
        if i == 2:
            at, pairs = slice(None), [(value_keep, value_keep_out), (value_send, value_send_out)]
        part_rows(held, pairs[0][0], pairs[1][0], at)
        for source, target in pairs[: len(keeps.shape) - 1]:
            place = (slice(None),) * (len(source.shape) - 1) + (at,)
            mover.start(source.at[place], target.at[place])
    wait(late)
    grad_attn_in = product_nt(grad_projected[...], qkv[...])
    normed, inverse = normalize(wide(tokens[...]))
    scale_attn = modulation[:, pl.ds(width, width)]
    grad_pieces[0:1] = column_sum(grad_attn_in)
    grad_pieces[1:2] = column_sum(grad_attn_in * normed)
    grad_tokens[...] = grad_middle[...] + normalize_back(
        grad_attn_in * (1.0 + scale_attn), normed, inverse
    )
    mover.finish()


def condition_body(
    kept,
    got,
    middle,
    modulation,
    cotangent,
    live,
    attn_pieces,
    mix_pieces,
    conditioned,
    activated,
    bucket,
    ada_hbm,
    mixed_out,
    factors,
    grad_condition,
    table_part,
    ada,
    sem,
):
    rows, width = cotangent.shape
    copy = pltpu.make_async_copy(ada_hbm, ada, sem)
    copy.start()
    alive = wide(live[0])
    gate_mix = modulation[:, pl.ds(5 * width, width)]
    mixture = wide(kept[...]) + wide(got[...])
    mixed_out[...] = to_low((middle[...] + gate_mix * mixture) * alive)
    grad_gate_mix = column_sum(wide(cotangent[...]) * alive * mixture)
    grads = [
        attn_pieces[0:1],
        attn_pieces[1:2],
        mix_pieces[0:1],
        mix_pieces[1:2],
        mix_pieces[2:3],
        grad_gate_mix,
    ]
    factors[...] = to_low(
        jnp.concatenate(grads + [wide(activated[...]), jnp.zeros((1, width), full)], axis=0)
    )
    copy.wait()
    pulled = jnp.zeros((1, width), full)
    for i, grad in enumerate(grads):
        spread = jnp.broadcast_to(to_low(grad), (16, width))
        pulled = pulled + product_nt(spread, ada[:, pl.ds(i * width, width)])[:1]
    drive = conditioned[...]
    gate = 1.0 / (1.0 + jnp.exp(-drive))
    grad = pulled * gate * (1.0 + drive * (1.0 - gate))
    grad_condition[...] = grad
    share = table_part.shape[0]
    row = lax.broadcasted_iota(jnp.int32, (share, 1), 0) + lax.axis_index("grp") * share
    table_part[...] = jnp.where(row == bucket[0], grad, 0.0)


def split_body(mine, keep_a, got_a, keep_b, got_b, keep_out, send_out):
    keep_out[...] = to_low(wide(keep_a[...]) + wide(got_a[...]))
    send_out[...] = to_low(wide(keep_b[...]) + wide(got_b[...]))


def split_sum(axis, bit, place, keep, got):
    mine = ((lax.axis_index(axis) >> bit) & 1).reshape(1)
    count, *block = keep.shape
    run = 1 << place
    spec = lambda other: pl.BlockSpec(
        (run, *block), lambda i, mine: (2 * i + (mine[0] ^ other), 0, 0)
    )
    out = pl.BlockSpec((run, *block), lambda i, mine: (i, 0, 0))
    return pl.pallas_call(
        split_body,
        grid_spec=pltpu.PrefetchScalarGridSpec(
            num_scalar_prefetch=1,
            grid=(count // 2 // run,),
            in_specs=[spec(0), spec(0), spec(1), spec(1)],
            out_specs=[out, out],
        ),
        out_shape=[like((count // 2, *block), low)] * 2,
        compiler_params=pltpu.CompilerParams(vmem_limit_bytes=FOLD << 20),
        cost_estimate=pl.CostEstimate(flops=int(1.5 * PEAK * WEIGH), bytes_accessed=0, transcendentals=0),
    )(mine, keep, got, keep, got)


def even_odd_body(keep_a, got_a, keep_b, got_b, keep_out, send_out):
    keep_out[...] = to_low(wide(keep_a[...]) + wide(got_a[...]))
    send_out[...] = to_low(wide(keep_b[...]) + wide(got_b[...]))


def even_odd_sum(keep, got):
    count, *block = keep.shape
    spec = lambda other: pl.BlockSpec((1, *block), lambda i: (2 * i + other, 0, 0))
    out = pl.BlockSpec((1, *block), lambda i: (i, 0, 0))
    return pl.pallas_call(
        even_odd_body,
        grid=(count // 2,),
        in_specs=[spec(0), spec(0), spec(1), spec(1)],
        out_specs=[out, out],
        out_shape=[like((count // 2, *block), low)] * 2,
        compiler_params=pltpu.CompilerParams(vmem_limit_bytes=FOLD << 20),
        cost_estimate=pl.CostEstimate(flops=int(1.5 * PEAK * WEIGH), bytes_accessed=0, transcendentals=0),
    )(keep, got, keep, got)


def join_body(mine, *refs):
    keep_out, send_out = refs[-2:]
    width = refs[0].shape[-1]
    for out, terms in ((keep_out, refs[0:4]), (send_out, refs[4:8])):
        out[:, :, :width] = to_low(wide(terms[0][...]) + wide(terms[1][...]))
        out[:, :, width:] = to_low(wide(terms[2][...]) + wide(terms[3][...]))


def join_sum(axis, bit, place, first, second):
    mine = ((lax.axis_index(axis) >> bit) & 1).reshape(1)
    count, rows, width = first[0].shape
    columns = width + second[0].shape[2]

    def spec(columns, other):
        return pl.BlockSpec(
            (run, rows, columns), lambda i, mine: (2 * i + (mine[0] ^ other), 0, 0)
        )

    run = 1 << place
    out = pl.BlockSpec((run, rows, columns), lambda i, mine: (i, 0, 0))
    return pl.pallas_call(
        join_body,
        grid_spec=pltpu.PrefetchScalarGridSpec(
            num_scalar_prefetch=1,
            grid=(count // 2 // run,),
            in_specs=[
                spec(c, other) for other in (0, 1) for c in (width, width, columns - width, columns - width)
            ],
            out_specs=[out, out],
        ),
        out_shape=[like((count // 2, rows, columns), low)] * 2,
        compiler_params=pltpu.CompilerParams(vmem_limit_bytes=FOLD << 20),
        cost_estimate=pl.CostEstimate(flops=int(1.5 * PEAK * WEIGH), bytes_accessed=0, transcendentals=0),
    )(mine, *first, *second, *first, *second)


def slab_join_body(mine, *refs):
    keep_out, send_out = refs[-2:]
    half = (len(refs) - 2) // 2
    for out, terms in ((keep_out, refs[:half]), (send_out, refs[half:-2])):
        start = 0
        for keep, got in zip(terms[::2], terms[1::2]):
            _, rows, columns = keep.shape
            for j in range(columns // LANES):
                at = slice(j * LANES, (j + 1) * LANES)
                out[0, start : start + rows, :] = to_low(
                    wide(keep[0, :, at]) + wide(got[0, :, at])
                )
                start += rows


def slab_join(axis, bit, place, *pairs):
    mine = ((lax.axis_index(axis) >> bit) & 1).reshape(1)
    count = pairs[0][0].shape[0]
    whole = sum(keep.size for keep, _ in pairs) // (count * LANES)

    def spec(block, other):
        return pl.BlockSpec(
            (1, *block), lambda i, mine: (parted(count, place, mine[0] ^ other, i), 0, 0)
        )

    out = pl.BlockSpec((1, whole, LANES), lambda i, mine: (i, 0, 0))
    terms = [term for pair in pairs for term in pair]
    return pl.pallas_call(
        slab_join_body,
        grid_spec=pltpu.PrefetchScalarGridSpec(
            num_scalar_prefetch=1,
            grid=(count // 2,),
            in_specs=[spec(t.shape[1:], other) for other in (0, 1) for t in terms],
            out_specs=[out, out],
        ),
        out_shape=[like((count // 2, whole, LANES), low)] * 2,
        compiler_params=pltpu.CompilerParams(vmem_limit_bytes=SLAB << 20),
        cost_estimate=pl.CostEstimate(flops=int(1.5 * PEAK * WEIGH), bytes_accessed=0, transcendentals=0),
    )(mine, *terms, *terms)


def stack_body(*refs):
    *pairs, total = refs
    start = 0
    for i in range(0, len(pairs), 2):
        rows = pl.ds(start, pairs[i].shape[0])
        total[rows, :] = to_low(wide(pairs[i][...]) + wide(pairs[i + 1][...]))
        start += pairs[i].shape[0]


def sum_body(keep, got, total):
    total[...] = to_low(wide(keep[...]) + wide(got[...]))


def own_up_body(*refs):
    *pairs, out = refs
    share, hidden = out.shape
    groups = lax.axis_size("grp")
    for c in range(CHUNKS):
        keep, got = pairs[2 * c : 2 * c + 2]
        rows = hidden // CHUNKS // LANES * share if c != 1 else share
        total = wide(keep[:rows, :]) + wide(got[:rows, :])
        for i in range(groups):
            place = (i & 1) * (groups // 2) + (i >> 1)
            if c == 1:
                value = total[:, place * LANES : (place + 1) * LANES]
            else:
                value = total[place * share : (place + 1) * share]
            out[:, pl.ds((i * CHUNKS + c) * LANES, LANES)] = value


def own_down_body(first, *refs):
    *pairs, out = refs
    width = out.shape[1]
    cut = out.shape[0] // CHUNKS
    size = width // LANES * cut
    for c in range(CHUNKS):
        keep, got = pairs[:2] if c < 2 else pairs[2:]
        start = first + (size if c == 1 else 0)
        for j in range(width // LANES):
            at = pl.ds(start + j * cut, cut)
            out[pl.ds(c * cut, cut), pl.ds(j * LANES, LANES)] = wide(keep[at, :]) + wide(got[at, :])


def shared_end_body(members, *refs):
    blocks, up_out, down_out = refs[:members], refs[-2], refs[-1]
    share = up_out.shape[0]
    me = lax.axis_index("dp")
    groups = lax.axis_size("grp")
    span = up_out.shape[1] // groups
    part = span // members
    for i in range(0, groups, 4):
        total = 0.0
        for far in range(members):
            pick = spread_units(span, part, me ^ far, 1)
            total = total + product(blocks[far][:share, pl.ds(i * part, 4 * part)], pick)
        up_out[:, pl.ds(i * span, 4 * span)] = total
    for far in range(members):
        start = pl.multiple_of((me ^ far) * part, 8)
        down_out[pl.ds(start, part)] = wide(blocks[far][share:, :])


def rows_end_body(members, *refs):
    blocks, (proj, router, qkv) = refs[:members], refs[members:]
    me = lax.axis_index("dp")
    share, width = blocks[0].shape[0], proj.shape[1]
    value = width + LANES
    for far in range(members):
        at = pl.ds(pl.multiple_of((me ^ far) * share, 8), share)
        block = blocks[far]
        proj[at, :] = wide(block[:, :width])
        router[at, :] = wide(block[:, width:value])
        qkv[at, : 2 * width] = wide(block[:, value + width :])
        qkv[at, 2 * width :] = wide(block[:, value : value + width])


def bits_of(axis):
    return lax.axis_size(axis).bit_length() - 1


def tie(tensor, *before):
    return lax.optimization_barrier((tensor, *before))[0]


DEPTH_X, DEPTH_Y, DEPTH_Z = 2, 2, 3


class Links:
    depth = {"y": DEPTH_Y, "z": DEPTH_Z, "x": DEPTH_X}

    def __init__(self):
        self.past = {}

    def swap(self, tensor, axis, bit):
        pairs = [(i, i ^ (1 << bit)) for i in range(lax.axis_size(axis))]
        if axis == "dp":
            name = "x" if bit else None
        else:
            name = "y" if bit < bits_of("grp") // 2 else "z"
        past = self.past.setdefault(name, [])
        depth = 1 if name == "x" and len(past) < bits_of("dp") else self.depth.get(name, 0)
        if 0 < depth <= len(past):
            tensor = tie(tensor, past[-depth])
        past.append(lax.ppermute(tensor, axis, pairs))
        return past[-1]


def over_call(body, outs, args):
    return kernel_call(body, outs, [VMEM] * len(args), args, (), 16, 1.5)


class Order:
    def __init__(self):
        self.tokens = ()

    def after(self, tensor):
        return tie(tensor, *self.tokens) if self.tokens else tensor

    def done(self, *tokens):
        self.tokens = tokens

    def also(self, token):
        self.tokens += (token,)


class Sum:
    def __init__(self, run, links, tiled, keep, send, order, left):
        self.run, self.links, self.tiled, self.keep, self.send = run, links, tiled, keep, send
        self.order = list(order)
        self.left = [bit for bit in left if bit != order[0]]
        self.folded = True

    def move(self):
        self.got = self.links.swap(self.send, *self.order.pop(0))
        self.folded = False

    def fold(self):
        if self.folded:
            return
        self.folded = True
        bit = self.order[0]
        place = len(self.left) - 1 - self.left.index(bit)
        self.left.remove(bit)
        if self.tiled:
            self.keep, self.send = split_sum(*bit, place, self.run.after(self.keep), self.got)
        else:
            total = to_low(wide(self.keep) + wide(self.got))
            self.keep, self.send = split(total, *bit, place)
        self.run.done(self.send)

    def step(self):
        self.fold()
        self.move()

    def last(self):
        while self.order:
            self.step()

    def terms(self):
        return self.keep[0], self.got[0]


def split(tensor, axis, bit, place):
    mine = (lax.axis_index(axis) >> bit) & 1
    parts = tensor.reshape((-1, 2, 1 << place) + tensor.shape[1:])
    halves_of = [
        lax.dynamic_index_in_dim(parts, i, 1, keepdims=False).reshape((-1,) + tensor.shape[1:])
        for i in (mine, 1 - mine)
    ]
    return halves_of


def gather_near(links, tensor, axis, before=()):
    blocks = {0: tensor}
    for bit in range(bits_of(axis) - 1, -1, -1):
        for far in list(blocks):
            block = tie(blocks[far], *before) if far and not bit and before else blocks[far]
            blocks[far ^ (1 << bit)] = links.swap(block, axis, bit)
    return [blocks[i] for i in range(len(blocks))]


def in_order(blocks, axis):
    me = lax.axis_index(axis)
    blocks = jnp.stack(blocks)
    return jnp.stack(
        [lax.dynamic_index_in_dim(blocks, i ^ me, 0, keepdims=False) for i in range(blocks.shape[0])]
    )


def per_device(
    tokens,
    condition,
    bucket,
    live_mask,
    routes,
    bucket_table,
    ada_weight,
    ada_bias,
    qkv_weight,
    proj_weight,
    shared_up,
    shared_down,
    router_weight,
    expert_up,
    expert_down,
    cotangent,
):
    tokens, routes, cotangent = tokens[0], routes[0], cotangent[0]
    rows, width = tokens.shape
    members, groups = lax.axis_size("dp"), lax.axis_size("grp")
    me, group = lax.axis_index("dp"), lax.axis_index("grp")
    experts = expert_up.shape[0] * members
    hidden = shared_up.shape[1]
    table_rows = bucket_table.shape[0]
    seen_rows = members * rows
    y_first = tuple(range(bits_of("grp")))
    z_first = y_first[1:] + y_first[:1]
    y_first, z_first = [tuple(("grp", bit) for bit in bits) for bits in (y_first, z_first)]
    all_left = tuple(("dp", bit) for bit in range(bits_of("dp") - 1, 0, -1)) + y_first[::-1]
    all_order = tuple(("dp", bit) for bit in range(bits_of("dp"))) + y_first

    links, run = Links(), Order()
    cotangents = gather_near(links, cotangent, "dp")

    extra = -(-(2 * experts + 2) // 16) * 16
    saved = [
        like((rows, width), low),
        like((rows, 3 * width), low),
        like((rows, LANES), full),
        like((rows, width), low),
        like((rows, width), full),
        like((rows, width), full),
    ]
    (
        packed,
        gates,
        modulation,
        conditioned,
        activated,
        attn_in,
        projected,
        logs,
        attended,
        attn_out,
        middle,
    ) = kernel_call(
        attend_body,
        [
            like((rows + extra, width), low),
            like((rows, LANES), full),
            like((1, 6 * width), full),
            like((1, width), full),
            like((1, width), low),
        ]
        + saved,
        [VMEM, VMEM, SMEM, SMEM] + [VMEM] * 4 + [HBM] * 3,
        (
            tokens,
            condition,
            bucket,
            live_mask,
            routes.T,
            bucket_table,
            ada_bias.reshape(-1, LANES),
            router_weight.T,
            ada_weight,
            qkv_weight,
            proj_weight,
        ),
        [pltpu.VMEM(out.shape, out.dtype) for out in saved]
        + [
            pltpu.VMEM(ada_weight.shape, low),
            pltpu.VMEM(qkv_weight.shape, low),
            pltpu.VMEM(proj_weight.shape, low),
            pltpu.SemaphoreType.DMA((4 + len(saved),)),
        ],
        MOST,
        10,
        [VMEM] * 5 + [HBM] * len(saved),
    )


    part = hidden // (groups * members)
    cut = hidden // (groups * CHUNKS)
    tiled = cut % LANES == 0
    if tiled:
        run.done(gates)
        [part_up] = kernel_call(
            functools.partial(pick_body, members),
            [like((width, groups * part), low)],
            [VMEM],
            (run.after(shared_up),),
            (),
            20,
            4,
        )
        part_down = shared_down
    else:
        part_up = lax.dynamic_index_in_dim(
            shared_up.reshape(width, groups, members, part), me, 2, keepdims=False
        ).reshape(width, groups * part)
        part_down = lax.dynamic_index_in_dim(
            shared_down.reshape(groups, members, part, width), me, 1, keepdims=False
        ).reshape(groups * part, width)
        sides = lambda tensor, place: jnp.concatenate(
            [
                lax.dynamic_index_in_dim(tensor, side, place + 1, keepdims=False)
                for side in (1 - group % 2, group % 2)
            ],
            axis=place,
        )
        own_ups = sides(expert_up[0].reshape(width, groups // 2, 2, CHUNKS, cut), 1)
        own_downs = sides(expert_down[0].reshape(groups // 2, 2, CHUNKS, cut, width), 0)
        ups = [own_ups[:, :, i].reshape(width, groups * cut) for i in range(CHUNKS)]
        downs = [own_downs[:, i].reshape(groups * cut, width) for i in range(CHUNKS)]
    share = width // groups
    packs = gather_near(links, packed, "dp", (part_up,))
    def sum_of(keep, send, order):
        return Sum(run, links, tiled, keep, send, order, y_first[::-1])

    def room(columns, step):
        return [
            pltpu.VMEM((seen_rows, columns), low),
            pltpu.VMEM((seen_rows, columns), low),
            pltpu.VMEM((groups // 2, share, columns), low),
            pltpu.VMEM((groups // 2, share, columns), low),
        ]

    ups_first = [z_first, y_first, z_first, y_first]
    columns = groups * part
    halved = [like((groups // 2, share, columns), low)] * 2
    patches = pltpu.VMEM((seen_rows, width), low)
    down_halved = [like((groups // 2, part, width), low)] * 2
    if not tiled:
        down_halved = [like((columns, width), low)] * 2
    seen, routed_grads, gate, up_keep, up_send, down_keep, down_send, *kept = kernel_call(
        functools.partial(shared_body, ups_first[0][0][1], members, rows, experts, tiled),
        [
            like((seen_rows, width), low),
            like((seen_rows, width), low),
            like((seen_rows, LANES), full),
        ]
        + halved
        + down_halved
        + [like((seen_rows, columns), low)] * 2,
        [HBM] * (2 * members + 2),
        (*packs, *cotangents, part_up, part_down),
        [
            pltpu.VMEM((members, rows + extra, width), low),
            pltpu.VMEM((members, rows, width), low),
            pltpu.VMEM((width, columns), low),
            pltpu.VMEM((columns, width), low),
            patches,
            patches,
            patches,
            pltpu.VMEM((seen_rows, LANES), full),
        ]
        + room(columns, 384)
        + [pltpu.VMEM(out.shape, low) for out in down_halved]
        + [
            pltpu.VMEM((width, 384), full),
            pltpu.SemaphoreType.DMA((64,)),
        ],
        MOST,
        9,
        [HBM] * 9,
    )
    acts, pres = [kept[0]], [kept[1]]
    run.done(gate)
    sums = {"su": sum_of(up_keep, up_send, ups_first[0])}
    sums["su"].move()
    if not tiled:
        down_keep, down_send = split(down_keep.reshape(groups, part, width), "grp", 0, 0)
    sums["sd"] = sum_of(down_keep, down_send, y_first)
    sums["sd"].move()
    columns = groups * cut
    halved = [like((groups // 2, share, columns), low)] * 2
    halved += [like((groups // 2, cut, width), low)] * 2
    block = seen_rows if members == 4 else rows
    slab = (groups // 2, share * columns // LANES + cut * width // LANES, LANES)
    for i in range(CHUNKS - 1):
        one = tiled and i == 0
        if i == 1:
            sums["su"].step()
            sums["sd"].step()
            if tiled:
                sums["e0"].move()
            else:
                sums["u0"].move()
                sums["d0"].move()
        *outs, act, grad_pre = kernel_call(
            functools.partial(routed_body, ups_first[1 + i][0][1], i, block, tiled, one),
            ([like(slab, low)] * 2 if one else halved) + [like((seen_rows, columns), low)] * 2,
            [HBM] * 4,
            (
                run.after(seen),
                routed_grads,
                *((expert_up, expert_down) if tiled else (ups[i], downs[i])),
            ),
            [
                patches,
                patches,
                pltpu.VMEM((width, columns), low),
                pltpu.VMEM((columns, width), low),
                pltpu.VMEM((seen_rows, columns), low),
                pltpu.VMEM((seen_rows, columns), low),
                pltpu.VMEM((width, columns // 2), full),
            ]
            + [pltpu.VMEM(out.shape, low) for out in ([like(slab, low)] * 2 if one else halved)]
            + [pltpu.SemaphoreType.DMA((64,))],
            MOST,
            10,
            [HBM] * (4 if one else 6),
        )
        if one:
            sums["e0"] = sum_of(outs[1], outs[0], y_first)
        else:
            sums["u%d" % i] = sum_of(outs[1], outs[0], ups_first[1 + i])
            sums["d%d" % i] = sum_of(outs[3], outs[2], y_first)
        acts.append(act)
        pres.append(grad_pre)
        run.done(grad_pre)
    sums["sd"].step()
    sums["su"].fold()
    sums["u1"].move()
    sums["d1"].move()
    (
        up_keep,
        up_send,
        down_keep,
        down_send,
        back_keep,
        back_send,
        mixed_keep,
        mixed_send,
    ) = kernel_call(
        functools.partial(
            result_body, ups_first[-1][0][1], members, rows, block, experts, tiled
        ),
        halved
        + [like((seen_rows // 2, width + LANES), low)] * 2
        + [like((seen_rows // 2, width), low)] * 2,
        [HBM] * (2 * CHUNKS + (4 if tiled else 2 * (1 + CHUNKS)) + 3),
        (
            *acts,
            *pres,
            *(
                (part_up, part_down, expert_up, expert_down)
                if tiled
                else (part_up, *ups, part_down, *downs)
            ),
            run.after(seen),
            routed_grads,
            gate,
        ),
        [pltpu.VMEM(a.shape, low) for a in acts]
        + [pltpu.VMEM((seen_rows, columns), low)]
        + [pltpu.VMEM(a.shape, low) for a in pres]
        + [pltpu.VMEM((seen_rows, columns), low)]
        + [pltpu.VMEM((width, groups * part), low)]
        + [pltpu.VMEM((width, columns), low)] * CHUNKS
        + [pltpu.VMEM((groups * part, width), low)]
        + [pltpu.VMEM((columns, width), low)] * CHUNKS
        + [
            patches,
            patches,
            pltpu.VMEM((seen_rows, LANES), full),
            pltpu.VMEM((seen_rows, width + LANES), low),
        ]
        + room(columns, 0)[2:]
        + [
            pltpu.VMEM((groups // 2, cut, width), low),
            pltpu.VMEM((groups // 2, cut, width), low),
            pltpu.VMEM((width, columns // 2), full),
            pltpu.SemaphoreType.DMA((160,)),
        ],
        MOST if members == 4 else 61,
        24,
        [HBM] * 8,
    )
    sums["u2"] = sum_of(up_keep, up_send, ups_first[-1])
    sums["d2"] = sum_of(down_keep, down_send, y_first)
    run.done(back_send)

    def fold_near(keep, got):
        keep, got = [t.reshape(-1, rows, t.shape[-1]) for t in (keep, got)]
        keep, send = even_odd_sum(run.after(keep), got)
        run.done(send)
        return keep, send

    def joined(*names):
        first, *others = [sums.pop(name) for name in names]
        bit = first.order[0]
        place = len(first.left) - 1 - first.left.index(bit)
        pairs = [(run.after(first.keep), first.got), *((o.keep, o.got) for o in others)]
        keep, send = slab_join(*bit, place, *pairs)
        run.done(send)
        found = Sum(run, links, tiled, keep, send, first.order, first.left)
        found.left = [b for b in first.left if b != bit]
        return found

    for name in ("sd", "u1", "d1"):
        run.also(sums[name].got)
    if tiled:
        sums["ed"] = joined("e0", "d1")
    back_keep, back_send, mixed_keep, mixed_send = [
        run.after(t) for t in (back_keep, back_send, mixed_keep, mixed_send)
    ]
    for name in ("u2", "d2"):
        sums[name].keep, sums[name].send = [
            run.after(t) for t in (sums[name].keep, sums[name].send)
        ]
    back_got = links.swap(back_send, "dp", 0)
    if tiled:
        sums["ed"].move()
    for bit in range(1, bits_of("dp")):
        back_keep, back_send = fold_near(back_keep, back_got)
        back_got = links.swap(back_send, "dp", bit)
    sums["u1"].step()
    sums["u2"].move()
    mixed_got = links.swap(mixed_send, "dp", 0)
    for bit in range(1, bits_of("dp")):
        mixed_keep, mixed_send = fold_near(mixed_keep, mixed_got)
        mixed_got = links.swap(mixed_send, "dp", bit)

    def row_parts(columns):
        if tiled:
            return [like((members // 2 * groups, share // members, columns), low)] * 2
        return [like((width, columns), low)] * 2

    proj_keep, proj_send, grad_attended, grad_middle, mix_pieces = kernel_call(
        middle_back_body,
        row_parts(width + LANES)
        + [
            like((rows, width), low),
            like((rows, width), full),
            like((8, width), full),
        ],
        [VMEM] * 7 + [SMEM] + [VMEM] * 4,
        (
            run.after(back_keep[0]),
            back_got[0],
            packed,
            middle,
            modulation,
            gates,
            cotangent,
            live_mask,
            attn_out,
            attended,
            proj_weight,
            router_weight.T,
        ),
        [pltpu.VMEM((width, width + LANES), full)],
        K3A,
        4,
    )
    run.done(mix_pieces)

    def all_sum(keep, send, order):
        if not tiled:
            columns = keep.shape[1]
            tensor = keep.reshape(groups, members, -1, columns)
            tensor = tensor.swapaxes(0, 1).reshape(members * groups, -1, columns)
            keep, send = split(tensor, "dp", 0, bits_of("grp"))
        found = Sum(run, links, tiled, keep, send, order, all_left)
        found.move()
        return found

    sums["d2"].move()
    grad_tokens, keeps, sends, value_keep, value_send, attn_pieces = kernel_call(
        attend_back_body,
        [like((rows, width), full)]
        + row_parts(2 * width)
        + row_parts(width)
        + [like((8, width), full)],
        [VMEM] * 4 + [HBM] * 4,
        (run.after(grad_attended), projected, logs, modulation, attn_in, tokens, grad_middle, qkv_weight),
        [
            pltpu.VMEM((rows, 3 * width), low),
            pltpu.VMEM((width, width), full),
            pltpu.VMEM(qkv_weight.shape, low),
        ]
        + [pltpu.VMEM(out.shape, low) for out in row_parts(2 * width) + row_parts(width)]
        + [
            pltpu.VMEM((rows, width), low),
            pltpu.VMEM((rows, width), low),
            pltpu.VMEM((rows, width), full),
            pltpu.SemaphoreType.DMA((16,)),
        ],
        MOST,
        8,
        [VMEM] + [HBM] * 4 + [VMEM],
    )
    run.done(attn_pieces)
    run.also(mixed_got)
    for name in ("u1", "u2", "d2"):
        run.also(sums[name].got)
    if tiled:
        sums["ed"].fold()
    proj_keep, proj_send, keeps, sends, value_keep, value_send, attn_pieces = [
        run.after(t)
        for t in (proj_keep, proj_send, keeps, sends, value_keep, value_send, attn_pieces)
    ]
    turned = (all_order[0], y_first[0], *all_order[1:-len(y_first)], *y_first[1:])
    sums["p"] = all_sum(proj_keep, proj_send, all_order)
    sums["v"] = all_sum(value_keep, value_send, all_order)
    sums["qk"] = all_sum(keeps, sends, turned)
    if tiled:
        sums["ed"].move()
        sums["ud"] = joined("u2", "d2")
        sums["ud"].move()
        p, v = sums.pop("p"), sums.pop("v")
        bit = v.order[0]
        place = len(v.left) - 1 - v.left.index(bit)
        keep, send = join_sum(*bit, place, (run.after(p.keep), p.got), (v.keep, v.got))
        run.done(send)
        sums["pv"] = Sum(run, links, tiled, keep, send, v.order, v.left)
        sums["pv"].move()
    sums["qk"].step()
    mixed_out, factors, grad_condition, table_part = kernel_call(
        condition_body,
        [
            like((rows, width), low),
            like((8, width), low),
            like((1, width), full),
            like((table_rows // groups, width), full),
        ],
        [VMEM] * 5 + [SMEM] + [VMEM] * 4 + [SMEM, HBM],
        (
            run.after(mixed_keep[0]),
            mixed_got[0],
            middle,
            modulation,
            cotangent,
            live_mask,
            attn_pieces,
            mix_pieces,
            conditioned,
            activated,
            bucket,
            ada_weight,
        ),
        [pltpu.VMEM(ada_weight.shape, low), pltpu.SemaphoreType.DMA],
        K4,
        4,
    )

    run.done(factors)

    factors = factors[None]

    def widen(factors, axis, bit):
        return jnp.concatenate([factors, links.swap(factors, axis, bit)], axis=0)

    if tiled:
        sums["pv"].step()
        sums["qk"].step()
        factors = widen(factors, "dp", 0)
        table_part = table_part + links.swap(table_part, "dp", 0)
        pv, qk = sums["pv"], sums["qk"]
        bit = qk.order[0]
        place = len(qk.left) - 1 - qk.left.index(bit)
        keep, send = join_sum(*bit, place, (run.after(pv.keep), pv.got), (qk.keep, qk.got))
        run.done(send)
        both = sum_of(keep, send, qk.order)
        both.left = [b for b in qk.left if b != bit]
        both.move()
        run.also(sums["ed"].got)
        sums["ud"].step()
        sums["su"].send, factors, table_part = [
            run.after(t) for t in (sums["su"].send, factors, table_part)
        ]
        both.step()
        sums["su"].move()
        factors = widen(factors, "dp", 1)
        factors = widen(factors, "grp", 0)
        sums["u1"].step()
        sums["sd"].last()
        [shared_total] = over_call(
            stack_body,
            [like((share + hidden // (groups * members), width), low)],
            (run.after(sums["su"].terms()[0]), sums["su"].terms()[1], *sums["sd"].terms()),
        )
        run.done(shared_total)
        shared_blocks = gather_near(links, shared_total, "dp")
        table_part = table_part + links.swap(table_part, "dp", 1)
        factors = widen(factors, "grp", 2)
        run.also(sums["u1"].got)
        up_part, down_part = over_call(
            functools.partial(shared_end_body, members),
            [like((share, hidden), full), like((hidden // groups, width), full)],
            (run.after(shared_blocks[0]), *shared_blocks[1:]),
        )
        run.done(down_part)
        [total] = over_call(
            sum_body, [like(both.terms()[0].shape, low)], (run.after(both.terms()[0]), both.terms()[1])
        )
        run.done(total)
        all_blocks = gather_near(links, total, "dp")
        factors = widen(factors, "grp", 1)
        ends = [t for name in ("ed", "u1", "ud") for t in sums[name].terms()]
        [expert_up_part] = over_call(
            own_up_body, [like((share, hidden), full)], (run.after(ends[0]), *ends[1:])
        )
        run.done(expert_up_part)
        ends = [t for name in ("ed", "ud") for t in sums[name].terms()]
        [expert_down_part] = over_call(
            functools.partial(own_down_body, share * columns // LANES),
            [like((hidden // groups, width), full)],
            (run.after(ends[0]), *ends[1:]),
        )
        run.done(expert_down_part)
        proj_part, router_part, qkv_part = over_call(
            functools.partial(rows_end_body, members),
            [like((share, n), full) for n in (width, LANES, 3 * width)],
            (run.after(all_blocks[0]), *all_blocks[1:]),
        )
    else:
        for bit in range(1, bits_of("dp")):
            factors = widen(factors, "dp", bit)
            table_part = table_part + links.swap(table_part, "dp", bit)
        factors = widen(factors, "dp", 0)
        table_part = table_part + links.swap(table_part, "dp", 0)
        sums["su"].move()
        for each in sums.values():
            each.last()
        for bit in range(bits_of("grp")):
            factors = widen(factors, "grp", bit)
        total = lambda name: wide(sums[name].terms()[0]) + wide(sums[name].terms()[1])
        ends = {
            name: gather_near(links, to_low(total(name)), "dp")
            for name in ("su", "sd", "p", "v", "qk")
        }
        up_part = wide(in_order(ends["su"], "dp")).reshape(members, share, groups, part)
        up_part = up_part.transpose(1, 2, 0, 3).reshape(share, hidden)
        down_part = wide(in_order(ends["sd"], "dp")).reshape(hidden // groups, width)
        own_ups = [total("u%d" % i).reshape(share, 2, groups // 2, cut) for i in range(CHUNKS)]
        expert_up_part = jnp.stack(own_ups, axis=3).transpose(0, 2, 1, 3, 4).reshape(share, hidden)
        expert_down_part = jnp.concatenate([total("d%d" % i) for i in range(CHUNKS)], axis=0)
        qkv_part = jnp.concatenate(
            [wide(in_order(ends[n], "dp")).reshape(share, -1) for n in ("qk", "v")], axis=1
        )
        proj_part = wide(in_order(ends["p"], "dp")).reshape(share, width + LANES)
        proj_part, router_part = jnp.split(proj_part, [width], axis=1)
    left = lax.dynamic_slice_in_dim(factors[:, 6], group * share, share, axis=1)
    right = factors[:, :6].reshape(-1, 6 * width)
    ada_w_part = product_tn(left, right)
    ada_share = 6 * width // groups
    ada_b_part = lax.dynamic_slice_in_dim(jnp.sum(wide(right), axis=0), group * ada_share, ada_share)
    return (
        mixed_out[None],
        grad_tokens[None],
        grad_condition,
        table_part,
        ada_w_part,
        ada_b_part,
        qkv_part,
        proj_part,
        up_part,
        down_part,
        router_part[:, :experts],
        expert_up_part[None],
        expert_down_part[None],
    )


def solution(mesh):
    in_specs = (
        P(("grp", "dp"), None, None),
        P(("grp", "dp"), None),
        P(("grp", "dp")),
        P(("grp", "dp")),
        P(("grp", "dp"), None, None),
        P(),
        P(),
        P(),
        P(),
        P(),
        P(),
        P(),
        P(),
        P("dp", None, None),
        P("dp", None, None),
        P(("grp", "dp"), None, None),
    )
    out_specs = (
        P(("grp", "dp"), None, None),
        P(("grp", "dp"), None, None),
        P(("grp", "dp"), None),
        P("grp", None),
        P("grp", None),
        P("grp"),
        P("grp", None),
        P("grp", None),
        P("grp", None),
        P("grp", None),
        P("grp", None),
        P("dp", "grp", None),
        P("dp", "grp", None),
    )
    return jax.shard_map(
        per_device, mesh=mesh, in_specs=in_specs, out_specs=out_specs, check_vma=False
    )
```
